32 devices in a mesh: grp: 2 (over y), row: 8 (over z, core), ch: 2 (over x), sub: 1.
Axes of the slice: x: 2, y: 2, z: 4, core: 2. Of those that a mesh axis runs over, the one named last changes fastest.
Arguments:
- pair: float32 [256, 128, 128], P(('grp', 'row'), 'sub'), parts along dimension 0, may hold values from -50 to 50
- pair_mask: int32 [256, 128], P(('grp', 'row'), 'sub'), parts along dimension 0, may hold values 0 or 1
- w_proj: float32 [4, 128, 128], P(None, None, 'ch'), may hold values from -0.5 to 0.5
- w_gate: float32 [128, 128], replicated, may hold values from -0.5 to 0.5
- w_out: float32 [128, 128], P('ch'), may hold values from -0.5 to 0.5
- cotangent: float32 [256, 128, 128], P(('grp', 'row'), 'sub'), parts along dimension 0, may hold values from -6 to 6
Outputs:
- update: float32 [256, 128, 128], P(('grp', 'row'), 'sub'), parts along dimension 0
- d_pair: float32 [256, 128, 128], P(('grp', 'row'), 'sub'), parts along dimension 0
The draws below stay inside these ranges and needn't reach their ends.
There are 2 independent parts, one for each index of `grp`. The reference program is written for one: setup_inputs(seed, part) draws one part's arguments, and reference() takes and returns one part's arrays. A program takes and returns all parts, laid end to end along the dimension named above; an argument that names none is the same for every part. Nothing has to cross between parts.
All inputs are finite; a program needn't handle non-finite values. No bound on the sum of `pair_mask` on one device may be relied on, other than what follows from the above.
Results may differ from the reference program's by a relative error of at most 0.0001.
Values sent between devices are 32-bit elements; how exact they have to be, the bound alone decides.
No kernel may reach another device: no remote copies, remote signals or barrier semaphores. Data moves between devices by JAX's collectives and lax.ppermute only.
A program may use at most 64 MiB of HBM per device.

```python
import math
import jax
import jax.numpy as jnp
from jax import lax

CZ = 128
C = 128
N = 128


def draw_pair(key, part):
    key = jax.random.fold_in(key, 7)
    keys = jax.random.split(key, 3)
    cell = jnp.exp(jax.random.uniform(keys[1], (N, N, 1), jnp.float32, 0.0, math.log(10.0)))
    chan = jnp.exp(jax.random.uniform(keys[2], (1, 1, CZ), jnp.float32, 0.0, math.log(10.0)))
    base = jax.random.truncated_normal(keys[0], -5.0, 5.0, (N, N, CZ), jnp.float32)
    return (0.1 * base * cell * chan).astype(jnp.float32)


def set_ends(drawn, rng, least, high):
    longest = drawn.shape.index(max(drawn.shape))
    spots = []
    for shift in (0, 1):
        where = [jax.random.randint(jax.random.fold_in(rng, axis), (), 0, length) for axis, length in enumerate(drawn.shape)]
        where[longest] = (where[longest] + shift) % drawn.shape[longest]
        spots.append(tuple(where))
    return drawn.at[spots[0]].set(least).at[spots[1]].set(high)


def level_of(key, extent, cuts, least, largest):
    def one(dim, blocks):
        draws = jax.random.uniform(jax.random.fold_in(jax.random.fold_in(key, 6), dim), (blocks,), jnp.float32, least / len(cuts), largest / len(cuts))
        return jnp.repeat(jnp.exp(draws), extent[dim] // blocks).reshape((-1,) + (1,) * (len(extent) - dim - 1))

    factor_of = one(*cuts[0])
    for cut in cuts[1:]:
        factor_of = factor_of * one(*cut)
    return factor_of


def gaussian(own_key, extent, width, limit, shards=(), dtype=jnp.bfloat16):
    entries = width * jax.random.normal(own_key, extent, jnp.float32)
    if shards:
        entries = entries * level_of(own_key, extent, shards, -0.22, 0.18)
    return jnp.clip(entries, -limit, limit).astype(dtype)


def setup_inputs(seed: int = 0, part: int = 0) -> dict:
    splits = jax.random.split(jax.random.key(seed), 7)
    own_keys = jax.random.split(jax.random.fold_in(splits[6], part), 7)
    return {
        "pair": draw_pair(jax.random.fold_in(jax.random.fold_in(splits[6], part), 71), part),
        "pair_mask": set_ends((jax.random.randint(own_keys[1], (N, N), 0, 4) < 3).astype(jnp.int32), jax.random.fold_in(own_keys[1], 1), 0, 1),
        "w_proj": gaussian(splits[2], (4, CZ, C), CZ ** -0.5, 0.5, ((2, 2),), jnp.float32),
        "w_gate": gaussian(splits[3], (CZ, CZ), CZ ** -0.5, 0.5, (), jnp.float32),
        "w_out": gaussian(splits[4], (C, CZ), C ** -0.5, 0.5, ((0, 2),), jnp.float32),
        "cotangent": gaussian(own_keys[5], (N, N, CZ), 1.0, 6.0, ((0, 8),), jnp.float32),
    }


def normalize(values):
    mean = lax.optimization_barrier(jnp.mean(values, axis=-1, keepdims=True))
    centered = values - mean
    variance = lax.optimization_barrier(jnp.mean(centered * centered, axis=-1, keepdims=True))
    return centered * lax.rsqrt(variance + 1e-05)

def forward(pair, keep, w_proj, w_gate, w_out):
    highest = lax.Precision.HIGHEST
    normed = normalize(pair)
    proj = jnp.einsum('ijz,pzc->pijc', normed, w_proj, precision=highest)
    left = keep[..., None] * jax.nn.sigmoid(proj[1]) * proj[0]
    right = keep[..., None] * jax.nn.sigmoid(proj[3]) * proj[2]
    mixed = jnp.einsum('ikc,jkc->ijc', left, right, precision=highest)
    mixed_norm = normalize(mixed)
    outgoing = jnp.einsum('ijc,cd->ijd', mixed_norm, w_out, precision=highest)
    gate = jax.nn.sigmoid(jnp.einsum('ijz,zd->ijd', normed, w_gate, precision=highest))
    return gate * outgoing

def reference(pair, pair_mask, w_proj, w_gate, w_out, cotangent):
    keep = pair_mask.astype(jnp.float32)
    update, pullback = jax.vjp(lambda field: forward(field, keep, w_proj, w_gate, w_out), pair)
    d_pair, = pullback(cotangent)
    return (update, d_pair)
```

```python
import functools
import jax
import jax.numpy as jnp
from jax import lax
from jax.experimental import pallas as pl
from jax.experimental.pallas import tpu as pltpu
from jax.sharding import PartitionSpec as P

C = 128
EPS = 1e-05
HIGHEST = lax.Precision.HIGHEST
F32 = jnp.float32
CHUNK = 4
GROUP = 8


def dot(a, b):
    return lax.dot_general(a, b, (((1,), (0,)), ((), ())), precision=HIGHEST, preferred_element_type=F32)


def dot_t(a, b):
    return lax.dot_general(a, b, (((1,), (1,)), ((), ())), precision=HIGHEST, preferred_element_type=F32)


def norm(values):
    mean = jnp.mean(values, axis=-1, keepdims=True)
    centered = values - mean
    variance = jnp.mean(centered * centered, axis=-1, keepdims=True)
    scale = lax.rsqrt(variance + EPS)
    return (centered * scale, scale)


def flat(values):
    return values.reshape(-1, values.shape[-1])


def call(kernel, outs, args, flops=0, scratch=()):
    smem = pl.BlockSpec(memory_space=pltpu.SMEM)
    vmem = pl.BlockSpec(memory_space=pltpu.VMEM)
    return pl.pallas_call(
        kernel,
        out_shape=[jax.ShapeDtypeStruct(shape, F32) for shape in outs],
        in_specs=[smem] + [vmem] * (len(args) - 1),
        out_specs=[vmem] * len(outs),
        scratch_shapes=[pltpu.VMEM(shape, F32) for shape in scratch],
        compiler_params=pltpu.CompilerParams(vmem_limit_bytes=50 * 1024 * 1024),
        cost_estimate=pl.CostEstimate(flops=flops, bytes_accessed=4 * sum(a.size for a in args), transcendentals=0),
    )(*args)


def source_row(place, t, rows):
    half = rows // 2
    if t < half:
        return place[2] * half + t
    return (1 - place[2]) * half + t - half


def gated_kernel(rows, place, pair, mask, w, gated, open_part, slope):
    half = rows // 2
    cols = pair.shape[1]
    chans = w.shape[1] // 2
    for t in range(0, gated.shape[0], CHUNK):
        row = source_row(place, t, rows)
        keep = jnp.concatenate(
            [jnp.transpose(jnp.broadcast_to(mask[pl.ds(row + u, 1), :].astype(F32), (8, cols)))[:, :1] for u in range(CHUNK)], axis=0
        )
        normed, _ = norm(flat(pair[pl.ds(row, CHUNK)]))
        proj = dot(normed, w[...])
        sig = jax.nn.sigmoid(proj[:, chans:]) * keep
        value = sig * proj[:, :chans]
        gated[t : t + CHUNK] = value.reshape(CHUNK, cols, chans)
        if t < half:
            open_part[t : t + CHUNK] = sig.reshape(CHUNK, cols, chans)
            slope[t : t + CHUNK] = (value * (1.0 - sig)).reshape(CHUNK, cols, chans)


def gate_kernel(rows, place, pair, cotangent, w_gate, gate, here, there, d_out):
    half = rows // 2
    cols = pair.shape[1]
    for t in range(0, rows, CHUNK):
        row = source_row(place, t, rows)
        normed, _ = norm(flat(pair[pl.ds(row, CHUNK)]))
        value = jax.nn.sigmoid(dot(normed, w_gate[...])).reshape(CHUNK, cols, -1)
        gate[t : t + CHUNK] = value
        d_out[t : t + CHUNK] = value * cotangent[pl.ds(row, CHUNK)]
    for chip in range(cols // (2 * rows)):
        for core, target in ((place[1], here), (1 - place[1], there)):
            first = pl.multiple_of(chip * 2 * rows + core * rows + place[2] * half, half)
            target[chip] = d_out[:, pl.ds(first, half), :]


def tile_kernel(step, parts, place, *refs):
    rights = refs[:parts]
    left_here, left_there, d_here, d_there, w_out, out_here, out_there, d_x, d_right = refs[parts : parts + 9]
    partial, x = refs[-2:]
    right = rights[0]
    if parts == 2:
        right = refs[parts + 9]
        right[...] = rights[0][...] + rights[1][...]
    rows = left_here.shape[0]
    half, cols, chans = right.shape
    groups = cols // GROUP

    def forward(pair_at, _):
        for which, left in enumerate((left_here, left_there)):
            for u in range(2):
                i = pair_at * 2 + u
                value = left[i]
                for j in range(half):
                    product = (value * right[j]).reshape(groups, GROUP, chans)
                    partial[2 * which + u, j * GROUP : (j + 1) * GROUP] = jnp.sum(product, axis=0)
                total = partial[2 * which + u, pl.ds(0, half, stride=GROUP), :]
                for s in range(1, GROUP):
                    total = total + partial[2 * which + u, pl.ds(s, half, stride=GROUP), :]
                x[pl.ds(pl.multiple_of((which * rows + i) * half, half), half), :] = total
        return 0

    lax.fori_loop(0, rows // 2, forward, 0)
    chip = jnp.bitwise_xor(place[0], step)
    d_out = jnp.concatenate([flat(d_here[chip]), flat(d_there[chip])], axis=0)
    normed, scale = norm(x[...])
    out = dot(normed, w_out[...])
    out_here[...] = out[: rows * half].reshape(rows, half, -1)
    out_there[...] = out[rows * half :].reshape(rows, half, -1)
    d_normed = dot_t(d_out, w_out[...])
    mean_one = jnp.mean(d_normed, axis=-1, keepdims=True)
    mean_two = jnp.mean(d_normed * normed, axis=-1, keepdims=True)
    d_x[...] = (d_normed - mean_one - normed * mean_two) * scale
    for j in range(0, half, 2):

        def backward(i, totals):
            for which, left in enumerate((left_here, left_there)):
                value = left[i]
                at = (which * rows + i) * half + j
                totals = tuple(total + value * d_x[pl.ds(at + u, 1), :] for u, total in enumerate(totals))
            return totals

        zero = jnp.zeros((cols, chans), F32)
        totals = lax.fori_loop(0, rows, backward, (zero, zero))
        d_right[j] = totals[0]
        d_right[j + 1] = totals[1]


def left_kernel(tiles, bases, first, place, *refs):
    rights, d_xs = refs[:tiles], refs[tiles : 2 * tiles]
    base = refs[2 * tiles : 2 * tiles + bases]
    outs = refs[2 * tiles + bases :]
    half, cols, chans = rights[0].shape
    rows = outs[0].shape[0]
    for which, out in enumerate(outs):

        def body(pair_at, _):
            i = pair_at * 2
            if bases:
                totals = [base[which][i], base[which][i + 1]]
            else:
                totals = [jnp.zeros((cols, chans), F32)] * 2
            for right, d_x in zip(rights, d_xs):
                for j in range(half):
                    value = right[j]
                    for u in range(2):
                        at = ((first + which) * rows + i + u) * half + j
                        totals[u] = totals[u] + value * d_x[pl.ds(at, 1), :]
            out[i] = totals[0]
            out[i + 1] = totals[1]
            return 0

        lax.fori_loop(0, rows // 2, body, 0)


def update_kernel(rows, place, *refs):
    early, late = refs[:4], refs[4:8]
    gate, cotangent, w_gate, update, d_normed, out = refs[8:]
    half = rows // 2
    cols = gate.shape[1]
    for quarter in range(4):
        other_core, other_half = quarter % 2, quarter // 2
        core = place[1] + other_core * (1 - 2 * place[1])
        side = place[2] + other_half * (1 - 2 * place[2])
        for step in range(4):
            chip = jnp.bitwise_xor(place[0], step)
            first = pl.multiple_of(chip * 2 * rows + core * rows + side * half, half)
            for t in (0, half):
                source = (t + other_half * half) % rows
                if step < 3:
                    block = early[quarter][step, source : source + half]
                else:
                    block = late[quarter][source : source + half]
                out[t : t + half, pl.ds(first, half), :] = block
    for t in range(0, rows, CHUNK):
        row = source_row(place, t, rows)
        opened = gate[t : t + CHUNK]
        value = opened * out[t : t + CHUNK]
        update[pl.ds(row, CHUNK)] = value
        if t < half:
            d_gate = cotangent[pl.ds(row, CHUNK)] * value * (1.0 - opened)
            d_normed[t : t + CHUNK] = dot_t(flat(d_gate), w_gate[...]).reshape(CHUNK, cols, -1)


def base_kernel(place, d_normed, d_left, d_left_other, open_part, slope, w, base):
    half, cols, chans = d_normed.shape
    for t in range(0, half, CHUNK):
        grad = flat(d_left[t : t + CHUNK] + d_left_other[t : t + CHUNK])
        both = jnp.concatenate([grad * flat(open_part[t : t + CHUNK]), grad * flat(slope[t : t + CHUNK])], axis=1)
        base[t : t + CHUNK] = d_normed[t : t + CHUNK] + dot_t(both, w[...]).reshape(CHUNK, cols, -1)


def pair_kernel(rows, place, pair, base, d_right, d_right_near, d_right_far, open_part, slope, w, d_pair):
    half, cols, chans = base.shape
    for t in range(0, half, CHUNK):
        at = slice(t, t + CHUNK)
        grad = flat(d_right[at] + d_right_near[at] + d_right_far[at])
        both = jnp.concatenate([grad * flat(open_part[at]), grad * flat(slope[at])], axis=1)
        d_normed = flat(base[at]) + dot_t(both, w[...])
        normed, scale = norm(flat(pair[pl.ds(source_row(place, t, rows), CHUNK)]))
        mean_grad = jnp.mean(d_normed, axis=-1, keepdims=True)
        mean_cross = jnp.mean(d_normed * normed, axis=-1, keepdims=True)
        d_pair[at] = ((d_normed - mean_grad - normed * mean_cross) * scale).reshape(CHUNK, cols, -1)


def along(block, pairs):
    return lax.ppermute(block, "row", [(2 * a + core, 2 * b + core) for a, b in pairs for core in (0, 1)])


def other_core(block):
    return lax.ppermute(block, "row", [(i, i ^ 1) for i in range(lax.axis_size("row"))])


def other_half(block):
    return lax.ppermute(block, "ch", [(0, 1), (1, 0)])


def diagonal(block):
    count = lax.axis_size("row") * 2
    return lax.ppermute(block, ("row", "ch"), [(i, i ^ 3) for i in range(count)])


NEXT = [(0, 1), (1, 0), (2, 3), (3, 2)]
MIDDLE = [(1, 2), (2, 1)]
OUTWARD = [(1, 0), (2, 3)]
INWARD = [(0, 1), (3, 2)]
ACROSS = [(0, 3), (3, 0), (1, 2), (2, 1)]


def on_tiles(pair, pair_mask, w_proj, w_gate, w_out, cotangent):
    rows, cols, width = pair.shape
    half = rows // 2
    row, side = lax.axis_index("row"), lax.axis_index("ch")
    place = jnp.stack([row // 2, row % 2, side]).astype(jnp.int32)

    def ordered(mine, other):
        return [jnp.where(side == 0, a, b) for a, b in ((mine, other), (other, mine))]

    def whole(mine, other):
        quarter = mine.shape[1] // 2
        value = ordered(mine[:, :quarter], other[:, :quarter])
        gate = ordered(mine[:, quarter:], other[:, quarter:])
        return jnp.concatenate(value + gate, axis=1)

    my_right = jnp.concatenate([w_proj[2], w_proj[3]], axis=1)
    w_right = whole(my_right, other_half(my_right))
    my_left = jnp.concatenate([w_proj[0], w_proj[1]], axis=1)
    rest = other_half(jnp.concatenate([my_left, w_out], axis=0))
    w_left = whole(my_left, rest[:width])
    w_all_out = jnp.concatenate(ordered(w_out, rest[width:]), axis=0)
    chans = w_all_out.shape[0]

    kept = (half, cols, chans)
    right, open_right, slope_right = call(
        functools.partial(gated_kernel, rows), [kept] * 3, (place, pair, pair_mask, w_right), flops=10**9
    )
    near = along(right, NEXT)
    middle = along(right, MIDDLE)
    left, open_left, slope_left = call(
        functools.partial(gated_kernel, rows),
        [(rows, cols, chans), kept, kept],
        (place, pair, pair_mask, w_left),
        flops=2 * 10**9,
    )
    left_there = other_core(left)
    chips = cols // (2 * rows)
    quarter = (chips, rows, half, width)
    gate, d_here, d_sent = call(
        functools.partial(gate_kernel, rows),
        [(rows, cols, width), quarter, quarter],
        (place, pair, cotangent, w_gate),
        flops=2 * 10**9,
        scratch=[(rows, cols, width)],
    )
    d_there = other_core(d_sent)

    def tile(step, *rights):
        outs = [(rows, half, width)] * 2 + [(2 * rows * half, chans), kept]
        if len(rights) == 2:
            outs.append(kept)
        got = call(
            functools.partial(tile_kernel, step, len(rights)),
            outs,
            (place, *rights, left, left_there, d_here, d_there, w_all_out),
            flops=4 * 10**9,
            scratch=[(4, half * GROUP, chans), (2 * rows * half, chans)],
        )
        return got if len(rights) == 2 else (*got, rights[0])

    out_here, out_there, d_x, d_right, rights = ([None] * 4 for _ in range(5))

    def run(step, *blocks):
        out_here[step], out_there[step], d_x[step], d_right[step], rights[step] = tile(step, *blocks)

    run(0, right)
    run(1, near)
    cross = along(near, MIDDLE)
    outer = along(middle, OUTWARD)
    run(2, cross, outer)
    far = along(cross, OUTWARD)
    inward = along(d_right[2], INWARD)
    swapped = along(d_right[2], MIDDLE)
    early_here, early_there = jnp.stack(out_here[:3]), jnp.stack(out_there[:3])
    early = [early_here, other_core(early_there), other_half(early_here), diagonal(early_there)]
    d_left_here, d_left_there = call(
        functools.partial(left_kernel, 3, 0, 0),
        [(rows, cols, chans)] * 2,
        (place, *rights[:3], *d_x[:3]),
        flops=4 * 10**9,
    )
    from_near = along(d_right[1] + swapped, NEXT)
    run(3, middle, far)
    from_far = along(d_right[3] + inward, ACROSS)
    late = [out_here[3], other_core(out_there[3]), other_half(out_here[3]), diagonal(out_there[3])]
    (d_left_sent,) = call(
        functools.partial(left_kernel, 1, 1, 1),
        [(rows, cols, chans)],
        (place, rights[3], d_x[3], d_left_there),
        flops=10**9,
    )
    (d_left_kept,) = call(
        functools.partial(left_kernel, 1, 1, 0),
        [(rows, cols, chans)],
        (place, rights[3], d_x[3], d_left_here),
        flops=10**9,
    )
    d_left = d_left_kept + other_core(d_left_sent)
    d_left_other = other_half(d_left[half:])
    update, d_normed = call(
        functools.partial(update_kernel, rows),
        [(rows, cols, width), (half, cols, width)],
        (place, *early, *late, gate, cotangent, w_gate),
        flops=10**9,
        scratch=[(rows, cols, width)],
    )
    (base,) = call(
        base_kernel,
        [(half, cols, width)],
        (place, d_normed, d_left[:half], d_left_other, open_left, slope_left, w_left),
        flops=10**9,
    )
    (mine,) = call(
        functools.partial(pair_kernel, rows),
        [(half, cols, width)],
        (place, pair, base, d_right[0], from_near, from_far, open_right, slope_right, w_right),
        flops=10**9,
    )
    d_pair = jnp.concatenate(ordered(mine, other_half(mine)), axis=0)
    return (update, d_pair)


def passed_along(block, axis, distance):
    devices = range(lax.axis_size(axis))
    route = [((i - distance) % len(devices), i) for i in devices]
    return lax.ppermute(block, axis, route)


def normalize(values):
    mean = jnp.mean(values, axis=-1, keepdims=True)
    centered = values - mean
    variance = jnp.mean(centered * centered, axis=-1, keepdims=True)
    scale = lax.rsqrt(variance + 1e-05)
    return (centered * scale, scale)


def on_ring(pair, pair_mask, w_proj, w_gate, w_out, cotangent):
    highest = lax.Precision.HIGHEST
    normed, pair_scale = normalize(pair)
    proj = jnp.einsum("rqz,pzc->pcrq", normed, w_proj, precision=highest)
    keep = pair_mask.astype(jnp.float32)
    sig_left = jax.nn.sigmoid(proj[1])
    sig_right = jax.nn.sigmoid(proj[3])
    left = keep * sig_left * proj[0]
    right = keep * sig_right * proj[2]
    chans, rows, cols = left.shape
    count = lax.axis_size("row")
    here = lax.axis_index("row")

    def visit(step, carry):
        block, store, partial_value = carry
        source = (here - step) % count
        store = lax.dynamic_update_slice_in_dim(store, block, source * rows, 1)
        product = jnp.einsum("cik,cjk->cij", left, block, precision=highest)
        partial_value = lax.dynamic_update_slice_in_dim(partial_value, product, source * rows, 2)
        block = passed_along(block, "row", 1)
        return (block, store, partial_value)

    store = jnp.zeros((chans, rows * count, cols), jnp.float32)
    partial_value = jnp.zeros((chans, rows, rows * count), jnp.float32)
    block, store, partial_value = lax.fori_loop(0, count - 1, visit, (right, store, partial_value))
    source = (here + 1) % count
    right_all = lax.dynamic_update_slice_in_dim(store, block, source * rows, 1)
    product = jnp.einsum("cik,cjk->cij", left, block, precision=highest)
    partial_value = lax.dynamic_update_slice_in_dim(partial_value, product, source * rows, 2)
    mixed = lax.psum_scatter(partial_value, "sub", scatter_dimension=2, tiled=True)
    first = jnp.sum(mixed, axis=0)
    second = jnp.sum(mixed * mixed, axis=0)
    projected = jnp.einsum("crq,cd->rqd", mixed, w_out, precision=highest)
    col_total = jnp.sum(w_out, axis=0)
    projected, first, second, col_total = lax.psum((projected, first, second, col_total), "ch")
    center = first / C
    spread = lax.rsqrt(second / C - center * center + 1e-05)
    outgoing = (projected - center[..., None] * col_total) * spread[..., None]
    gate = jax.nn.sigmoid(jnp.einsum("rqz,zd->rqd", normed, w_gate, precision=highest))
    update = gate * outgoing
    d_outgoing = cotangent * gate
    d_gate_pre = cotangent * outgoing * gate * (1.0 - gate)
    d_mixed_norm = jnp.einsum("rqd,cd->crq", d_outgoing, w_out, precision=highest)
    mean_one = jnp.sum(d_outgoing * col_total, axis=-1) / C
    mean_two = jnp.sum(d_outgoing * outgoing, axis=-1) / C
    mixed_norm = (mixed - center) * spread
    d_mixed = (d_mixed_norm - mean_one - mixed_norm * mean_two) * spread
    d_mixed_full = lax.all_gather(d_mixed, "sub", axis=2, tiled=True)
    d_left = jnp.einsum("cij,cjk->cik", d_mixed_full, right_all, precision=highest)
    d_right = jnp.transpose(
        lax.psum_scatter(
            jnp.einsum("cij,cik->jck", d_mixed_full, left, precision=highest),
            "row",
            scatter_dimension=0,
            tiled=True,
        ),
        (1, 0, 2),
    )
    d_proj = jnp.stack(
        [
            d_left * keep * sig_left,
            d_left * keep * proj[0] * sig_left * (1.0 - sig_left),
            d_right * keep * sig_right,
            d_right * keep * proj[2] * sig_right * (1.0 - sig_right),
        ]
    )
    d_normed_part = jnp.einsum("pcrq,pzc->rqz", d_proj, w_proj, precision=highest)
    d_normed = lax.psum(d_normed_part, "ch")
    d_normed = d_normed + jnp.einsum("rqd,zd->rqz", d_gate_pre, w_gate, precision=highest)
    mean_grad = jnp.mean(d_normed, axis=-1, keepdims=True)
    mean_cross = jnp.mean(d_normed * normed, axis=-1, keepdims=True)
    d_pair = (d_normed - mean_grad - normed * mean_cross) * pair_scale
    return (update, d_pair)


def solution(mesh):
    sizes = mesh.shape
    tiled = sizes["row"] == 8 and sizes["ch"] == 2 and sizes["sub"] == 1
    return jax.shard_map(
        on_tiles if tiled else on_ring,
        mesh=mesh,
        in_specs=(
            P(("grp", "row"), "sub", None),
            P(("grp", "row"), "sub"),
            P(None, None, "ch"),
            P(),
            P("ch", None),
            P(("grp", "row"), "sub", None),
        ),
        out_specs=(P(("grp", "row"), "sub", None), P(("grp", "row"), "sub", None)),
        check_vma=False,
    )
```

```python
import functools
import jax
import jax.numpy as jnp
from jax import lax
from jax.experimental import pallas as pl
from jax.experimental.pallas import tpu as pltpu
from jax.sharding import PartitionSpec as P

C = 128
EPS = 1e-05
HIGHEST = lax.Precision.HIGHEST
F32 = jnp.float32
CHUNK = 4
GROUP = 8


def dot(a, b):
    return lax.dot_general(a, b, (((1,), (0,)), ((), ())), precision=HIGHEST, preferred_element_type=F32)


def dot_t(a, b):
    return lax.dot_general(a, b, (((1,), (1,)), ((), ())), precision=HIGHEST, preferred_element_type=F32)


def norm(values):
    mean = jnp.mean(values, axis=-1, keepdims=True)
    centered = values - mean
    variance = jnp.mean(centered * centered, axis=-1, keepdims=True)
    scale = lax.rsqrt(variance + EPS)
    return (centered * scale, scale)


def flat(values):
    return values.reshape(-1, values.shape[-1])


def call(kernel, outs, args, scratch=(), flops=1000):
    smem = pl.BlockSpec(memory_space=pltpu.SMEM)
    vmem = pl.BlockSpec(memory_space=pltpu.VMEM)
    return pl.pallas_call(
        kernel,
        out_shape=[jax.ShapeDtypeStruct(shape, F32) for shape in outs],
        in_specs=[smem] + [vmem] * (len(args) - 1),
        out_specs=[vmem] * len(outs),
        scratch_shapes=[pltpu.VMEM(shape, F32) for shape in scratch],
        compiler_params=pltpu.CompilerParams(vmem_limit_bytes=50 * 1024 * 1024),
        cost_estimate=pl.CostEstimate(flops=flops, bytes_accessed=flops, transcendentals=0),
    )(*args)


def source_row(place, t, rows):
    half = rows // 2
    if t < half:
        return place[2] * half + t
    return (1 - place[2]) * half + t - half


def first_col(place, chip, core, rows):
    half = rows // 2
    return pl.multiple_of(chip * 2 * rows + core * rows + place[2] * half, half)


def rows_kernel(place, pair, mask, cotangent, packed):
    rows, cols, width = pair.shape
    half = rows // 2
    packed[:rows] = pair[...]
    for chip in range(cols // (2 * rows)):
        block = cotangent[:, pl.ds(first_col(place, chip, 1 - place[1], rows), half), :]
        packed[rows + chip] = flat(block)
    packed[packed.shape[0] - 1, :rows] = mask[...].astype(F32)


def both_halves(place, mine, other):
    first = place[2] == 0
    a, b = jnp.where(first, mine, other), jnp.where(first, other, mine)
    return jnp.concatenate([a, b], axis=0)


def gated_weights(place, mine, other, which):
    return jnp.concatenate([both_halves(place, mine[p], other[p]) for p in (which, which + 1)], axis=0)


def gated(normed, keep_rows, w):
    count, cols = keep_rows.shape
    chans = w.shape[0] // 2
    spread = jnp.transpose(jnp.concatenate([keep_rows] * (8 // count), axis=0))
    keep = jnp.concatenate([spread[:, u : u + 1] for u in range(count)], axis=0)
    proj = dot_t(normed, w)
    sig = jax.nn.sigmoid(proj[:, chans:]) * keep
    return sig * proj[:, :chans], sig


def right_kernel(rows, place, pair, mask, mine, other, right, open_part, slope):
    half, cols, chans = right.shape
    w = gated_weights(place, mine, other, 2)
    for t in range(0, half, CHUNK):
        row = source_row(place, t, rows)
        normed, _ = norm(flat(pair[pl.ds(row, CHUNK)]))
        value, sig = gated(normed, mask[pl.ds(row, CHUNK), :].astype(F32), w)
        shape = (CHUNK, cols, chans)
        right[t : t + CHUNK] = value.reshape(shape)
        open_part[t : t + CHUNK] = sig.reshape(shape)
        slope[t : t + CHUNK] = (value * (1.0 - sig)).reshape(shape)


def prepare_kernel(rows, place, pair, mask, cotangent, there, mine, other, w_gate, mine_out, other_out, *refs):
    left_here, left_there, open_part, slope, gate, d_here, d_there, w_out, normed_rows = refs
    half, cols, chans = open_part.shape
    chips = cols // (2 * rows)
    shape = (CHUNK, cols, chans)
    w = gated_weights(place, mine, other, 0)
    w_out[...] = both_halves(place, mine_out[...], other_out[...])
    for t in range(0, rows, CHUNK):
        row = source_row(place, t, rows)
        at = slice(t, t + CHUNK)
        normed, _ = norm(flat(pair[pl.ds(row, CHUNK)]))
        value, sig = gated(normed, mask[pl.ds(row, CHUNK), :].astype(F32), w)
        left_here[at] = value.reshape(shape)
        if t < half:
            open_part[at] = sig.reshape(shape)
            slope[at] = (value * (1.0 - sig)).reshape(shape)
        gate[at] = jax.nn.sigmoid(dot(normed, w_gate[...])).reshape(CHUNK, cols, -1)
        for chip in range(chips):
            near = pl.ds(first_col(place, chip, place[1], rows), half)
            d_here[chip, at] = gate[at, near, :] * cotangent[pl.ds(row, CHUNK), near, :]
        normed, _ = norm(flat(there[pl.ds(row, CHUNK)]))
        value, _ = gated(normed, there[there.shape[0] - 1, pl.ds(row, CHUNK), :], w)
        left_there[at] = value.reshape(shape)
        normed_rows[...] = normed.reshape(CHUNK, cols, -1)
        picked = [
            normed_rows[:, pl.ds(first_col(place, chip, place[1], rows), half), :] for chip in range(chips)
        ]
        opened = jax.nn.sigmoid(dot(flat(jnp.stack(picked)), w_gate[...])).reshape(chips, CHUNK, half, -1)
        for chip in range(chips):
            d_out = there[rows + chip, pl.ds(row * half, CHUNK * half), :].reshape(CHUNK, half, -1)
            d_there[chip, at] = opened[chip] * d_out


def tile_body(step, place, right, left_here, left_there, d_here, d_there, w_out, out_here, out_there, d_x, d_right, partial, x):
    rows = left_here.shape[0]
    half, cols, chans = right.shape
    groups = cols // GROUP

    def forward(pair_at, _):
        for which, left in enumerate((left_here, left_there)):
            i = pair_at * 2
            value = [left[i], left[i + 1]]
            for j in range(half):
                block = right[j]
                for u in range(2):
                    product = (value[u] * block).reshape(groups, GROUP, chans)
                    partial[2 * which + u, j * GROUP : (j + 1) * GROUP] = jnp.sum(product, axis=0)
            for u in range(2):
                total = partial[2 * which + u, pl.ds(0, half, stride=GROUP), :]
                for s in range(1, GROUP):
                    total = total + partial[2 * which + u, pl.ds(s, half, stride=GROUP), :]
                x[pl.ds(pl.multiple_of((which * rows + i + u) * half, half), half), :] = total
        return 0

    lax.fori_loop(0, rows // 2, forward, 0)
    chip = jnp.bitwise_xor(place[0], step)
    d_out = jnp.concatenate([flat(d_here[chip]), flat(d_there[chip])], axis=0)
    normed, scale = norm(x[...])
    out = dot(normed, w_out[...])
    out_here[...] = out[: rows * half].reshape(rows, half, -1)
    out_there[...] = out[rows * half :].reshape(rows, half, -1)
    d_normed = dot_t(d_out, w_out[...])
    mean_one = jnp.mean(d_normed, axis=-1, keepdims=True)
    mean_two = jnp.mean(d_normed * normed, axis=-1, keepdims=True)
    d_x[...] = (d_normed - mean_one - normed * mean_two) * scale
    wide = 2 * GROUP

    def backward(at, _):
        here = pl.ds(pl.multiple_of(at * wide, wide), wide)

        def add(block, totals):
            totals = list(totals)
            for u in range(GROUP):
                for which, left in enumerate((left_here, left_there)):
                    i = block * GROUP + u
                    value = left[i, here, :]
                    for j in range(half):
                        totals[j] = totals[j] + value * d_x[pl.ds((which * rows + i) * half + j, 1), :]
            return tuple(totals)

        totals = lax.fori_loop(0, rows // GROUP, add, (jnp.zeros((wide, chans), F32),) * half)
        for j in range(half):
            d_right[j, here, :] = totals[j]
        return 0

    lax.fori_loop(0, cols // wide, backward, 0)


def tile_kernel(step, parts, place, *refs):
    rights, rest = refs[:parts], refs[parts:]
    if parts == 2:
        sum_out = rest[9]
        sum_out[...] = rights[0][...] + rights[1][...]
        tile_body(step, place, sum_out, *rest[:9], *rest[10:])
    else:
        tile_body(step, place, rights[0], *rest)


def left_kernel(tiles, bases, place, *refs):
    rights, d_xs = refs[:tiles], refs[tiles : 2 * tiles]
    base = refs[2 * tiles : 2 * tiles + bases]
    outs = refs[2 * tiles + bases :]
    half, cols, chans = rights[0].shape
    rows = outs[0].shape[0]
    for which, out in enumerate(outs):

        def body(pair_at, _):
            i = pair_at * 2
            if bases:
                totals = [base[which][i], base[which][i + 1]]
            else:
                totals = [jnp.zeros((cols, chans), F32)] * 2
            for right, d_x in zip(rights, d_xs):
                for j in range(half):
                    value = right[j]
                    for u in range(2):
                        at = (which * rows + i + u) * half + j
                        totals[u] = totals[u] + value * d_x[pl.ds(at, 1), :]
            out[i] = totals[0]
            out[i + 1] = totals[1]
            return 0

        lax.fori_loop(0, rows // 2, body, 0)
    for plane in range(2, bases):
        outs[1][rows + plane - 2] = flat(base[plane][...])


def share_kernel(place, kept, received, out_here, out_next, d_left, packed, packed_next, rest):
    half = d_left.shape[0]
    block = half * half
    d_left[...] = kept[:half] + received[:half]
    part = half // 2
    packed[:part] = kept[half : half + part] + received[half : half + part]
    packed_next[:part] = kept[half + part :] + received[half + part : 2 * half]
    for step, out in enumerate((out_here, out_next)):
        at = slice(step * block, (step + 1) * block)
        plane = 2 * half + step
        packed[part, at] = flat(out[half:])
        packed_next[part, at] = received[plane, block:]
        rest[0, at] = flat(out[:half])
        rest[1, at] = received[plane, :block]


def gather_out(place, rows, t, out, here, early_other, early_far, received, far):
    half = rows // 2
    block = half * half
    for far_half in (0, 1):
        source = (t + far_half * half) % rows
        at, wide = slice(source, source + half), slice(source * half, source * half + block)
        for far_core in (0, 1):
            core = place[1] + far_core * (1 - 2 * place[1])
            side = place[2] + far_half * (1 - 2 * place[2])
            for step in range(4):
                chip = jnp.bitwise_xor(place[0], step)
                first = pl.multiple_of(chip * 2 * rows + core * rows + side * half, half)
                if far_half:
                    if step < 2:
                        value = early_far[far_core, step, at]
                    else:
                        ref, plane = far[far_core]
                        value = ref[plane, (step - 2) * block : (step - 1) * block].reshape(half, half, -1)
                elif far_core:
                    if step < 2:
                        value = early_other[step, at]
                    else:
                        value = received[rows + step - 2, wide].reshape(half, half, -1)
                else:
                    value = here[step][at]
                out[t : t + half, pl.ds(first, half), :] = value


def update_kernel(rows, place, *refs):
    here, early_other, early_far, received, far, far_next, rest, gate, update, out = refs[:4], *refs[4:]
    half = rows // 2
    part = half // 2
    gather_out(place, rows, 0, out, here, early_other, early_far, received, ((far, part), (far_next, part)))
    gather_out(place, rows, half, out, here, early_other, early_far, received, ((rest, 0), (rest, 1)))
    for t in range(0, rows, CHUNK):
        update[pl.ds(source_row(place, t, rows), CHUNK)] = gate[t : t + CHUNK] * out[t : t + CHUNK]


def base_kernel(rows, place, *refs):
    here, early_other, early_far, received, far, far_next = refs[:4], *refs[4:9]
    gate, cotangent, w_gate, d_left, open_part, slope, mine, other, base, out = refs[9:]
    half, cols, chans = base.shape
    part = half // 2
    gather_out(place, rows, 0, out, here, early_other, early_far, received, ((far, part), (far_next, part)))
    w = gated_weights(place, mine, other, 0)
    for t in range(0, half, CHUNK):
        at = slice(t, t + CHUNK)
        opened = gate[at]
        d_gate = cotangent[pl.ds(source_row(place, t, rows), CHUNK)] * (opened * out[at]) * (1.0 - opened)
        from_other = (far if t < part else far_next)[t % part : t % part + CHUNK]
        grad = flat(d_left[at] + from_other)
        both = jnp.concatenate([grad * flat(open_part[at]), grad * flat(slope[at])], axis=1)
        base[at] = (dot_t(flat(d_gate), w_gate[...]) + dot(both, w)).reshape(CHUNK, cols, -1)


def pair_kernel(rows, place, pair, base, d_right, d_right_near, d_right_middle, d_right_far, open_part, slope, mine, other, d_mine, d_pair):
    half, cols, chans = base.shape
    w = gated_weights(place, mine, other, 2)
    for t in range(0, half, CHUNK):
        at = slice(t, t + CHUNK)
        grad = flat(d_right[at] + d_right_near[at] + (d_right_middle[at] + d_right_far[at]))
        both = jnp.concatenate([grad * flat(open_part[at]), grad * flat(slope[at])], axis=1)
        d_normed = flat(base[at]) + dot(both, w)
        normed, scale = norm(flat(pair[pl.ds(source_row(place, t, rows), CHUNK)]))
        mean_grad = jnp.mean(d_normed, axis=-1, keepdims=True)
        mean_cross = jnp.mean(d_normed * normed, axis=-1, keepdims=True)
        d_mine[at] = ((d_normed - mean_grad - normed * mean_cross) * scale).reshape(CHUNK, cols, -1)
        d_pair[pl.ds(source_row(place, t, rows), CHUNK)] = d_mine[at]


def along(block, pairs):
    return lax.ppermute(block, "row", [(2 * a + core, 2 * b + core) for a, b in pairs for core in (0, 1)])


def other_core(block):
    return lax.ppermute(block, "row", [(i, i ^ 1) for i in range(lax.axis_size("row"))])


def other_half(block):
    return lax.ppermute(block, "ch", [(0, 1), (1, 0)])


NEXT = [(0, 1), (1, 0), (2, 3), (3, 2)]
MIDDLE = [(1, 2), (2, 1)]
OUTWARD = [(1, 0), (2, 3)]
INWARD = [(0, 1), (3, 2)]
ENDS = [(0, 3), (3, 0)]


def on_tiles(pair, pair_mask, w_proj, w_gate, w_out, cotangent):
    rows, cols, width = pair.shape
    half = rows // 2
    chips = cols // (2 * rows)
    chans = 2 * w_out.shape[0]
    row, side = lax.axis_index("row"), lax.axis_index("ch")
    place = jnp.stack([row // 2, row % 2, side]).astype(jnp.int32)

    mine = jnp.swapaxes(w_proj, 1, 2)
    other = other_half(flat(mine)).reshape(mine.shape)
    other_out = other_half(w_out)
    (sent,) = call(rows_kernel, [(rows + chips + 1, cols, width)], (place, pair, pair_mask, cotangent), flops=10**9)
    there = other_core(sent)

    kept = (half, cols, chans)
    right, open_right, slope_right = call(
        functools.partial(right_kernel, rows), [kept] * 3, (place, pair, pair_mask, mine, other)
    )
    near = along(right, NEXT)
    middle = along(right, MIDDLE)
    quarter = (chips, rows, half, width)
    tile_outs = [(rows, half, width)] * 2 + [(2 * rows * half, chans), kept]
    tile_scratch = [(4, half * GROUP, chans), (2 * rows * half, chans)]
    out_here, out_there, d_x, d_right, rights = ([None] * 4 for _ in range(5))
    rights[0] = right
    left, left_there, open_left, slope_left, gate, d_here, d_there, w_all_out = call(
        functools.partial(prepare_kernel, rows),
        [(rows, cols, chans)] * 2 + [kept] * 2 + [(rows, cols, width), quarter, quarter, (chans, width)],
        (place, pair, pair_mask, cotangent, there, mine, other, w_gate, w_out, other_out),
        scratch=[(CHUNK, cols, width)],
    )

    def tile(step, *blocks):
        got = call(
            functools.partial(tile_kernel, step, len(blocks)),
            tile_outs + ([kept] if len(blocks) == 2 else []),
            (place, *blocks, left, left_there, d_here, d_there, w_all_out),
            scratch=tile_scratch,
        )
        out_here[step], out_there[step], d_x[step], d_right[step] = got[:4]
        rights[step] = got[4] if len(blocks) == 2 else blocks[0]

    near, middle, d_here = lax.optimization_barrier((near, middle, d_here))
    cross = along(near, MIDDLE)
    outer = along(middle, OUTWARD)
    tile(0, right)
    tile(1, near)
    early_other = other_core(jnp.stack(out_there[:2]))
    d_left_here, d_left_there = call(
        functools.partial(left_kernel, 2, 0),
        [(rows, cols, chans)] * 2,
        (place, *rights[:2], *d_x[:2]),
    )
    cross, outer, early_other, d_left_here = lax.optimization_barrier((cross, outer, early_other, d_left_here))
    far = along(cross, OUTWARD)
    early_far = other_half(jnp.stack([jnp.stack(out_here[:2]), early_other]))
    tile(2, cross, outer)
    inward = along(d_right[2], INWARD)
    swapped = along(d_right[2], MIDDLE)
    far, d_x[2] = lax.optimization_barrier((far, d_x[2]))
    tile(3, middle, far)
    from_far = along(d_right[3], ENDS)
    inward, swapped, early_far, d_x[3] = lax.optimization_barrier((inward, swapped, early_far, d_x[3]))
    d_left_kept, d_left_sent = call(
        functools.partial(left_kernel, 2, 4),
        [(rows, cols, chans), (rows + 2, cols, chans)],
        (place, *rights[2:], *d_x[2:], d_left_here, d_left_there, out_there[2], out_there[3]),
    )
    received = other_core(d_left_sent)
    from_near = along(d_right[1] + swapped, NEXT)
    from_middle = along(d_right[3] + inward, MIDDLE)
    packed_shape = (half // 2 + 1, cols, chans)
    d_left, shared, shared_next, rest = call(
        share_kernel,
        [kept, packed_shape, packed_shape, (2, cols, chans)],
        (place, d_left_kept, received, out_here[2], out_here[3]),
    )
    shared_other = other_half(shared)
    shared_other_next = other_half(shared_next)
    rest_other = other_half(rest)
    outs = (*out_here, early_other, early_far, received, shared_other, shared_other_next)
    (base,) = call(
        functools.partial(base_kernel, rows),
        [(half, cols, width)],
        (place, *outs, gate, cotangent, w_gate, d_left, open_left, slope_left, mine, other),
        scratch=[(half, cols, width)],
    )
    base, rest_other = lax.optimization_barrier((base, rest_other))
    d_mine, d_pair = call(
        functools.partial(pair_kernel, rows),
        [(half, cols, width), (rows, cols, width)],
        (place, pair, base, d_right[0], from_near, from_middle, from_far, open_right, slope_right, mine, other),
    )
    d_other = other_half(d_mine)
    _, gate_late = lax.optimization_barrier((d_mine, gate))
    (update,) = call(
        functools.partial(update_kernel, rows),
        [(rows, cols, width)],
        (place, *outs, rest_other, gate_late),
        scratch=[(rows, cols, width)],
    )
    d_other, update = lax.optimization_barrier((d_other, update))
    d_pair = lax.dynamic_update_slice_in_dim(d_pair, d_other, (1 - side) * half, 0)
    return (update, d_pair)


def passed_along(block, axis, distance):
    devices = range(lax.axis_size(axis))
    route = [((i - distance) % len(devices), i) for i in devices]
    return lax.ppermute(block, axis, route)


def normalize(values):
    mean = jnp.mean(values, axis=-1, keepdims=True)
    centered = values - mean
    variance = jnp.mean(centered * centered, axis=-1, keepdims=True)
    scale = lax.rsqrt(variance + 1e-05)
    return (centered * scale, scale)


def on_ring(pair, pair_mask, w_proj, w_gate, w_out, cotangent):
    highest = lax.Precision.HIGHEST
    normed, pair_scale = normalize(pair)
    proj = jnp.einsum("rqz,pzc->pcrq", normed, w_proj, precision=highest)
    keep = pair_mask.astype(jnp.float32)
    sig_left = jax.nn.sigmoid(proj[1])
    sig_right = jax.nn.sigmoid(proj[3])
    left = keep * sig_left * proj[0]
    right = keep * sig_right * proj[2]
    chans, rows, cols = left.shape
    count = lax.axis_size("row")
    here = lax.axis_index("row")

    def visit(step, carry):
        block, store, partial_value = carry
        source = (here - step) % count
        store = lax.dynamic_update_slice_in_dim(store, block, source * rows, 1)
        product = jnp.einsum("cik,cjk->cij", left, block, precision=highest)
        partial_value = lax.dynamic_update_slice_in_dim(partial_value, product, source * rows, 2)
        block = passed_along(block, "row", 1)
        return (block, store, partial_value)

    store = jnp.zeros((chans, rows * count, cols), jnp.float32)
    partial_value = jnp.zeros((chans, rows, rows * count), jnp.float32)
    block, store, partial_value = lax.fori_loop(0, count - 1, visit, (right, store, partial_value))
    source = (here + 1) % count
    right_all = lax.dynamic_update_slice_in_dim(store, block, source * rows, 1)
    product = jnp.einsum("cik,cjk->cij", left, block, precision=highest)
    partial_value = lax.dynamic_update_slice_in_dim(partial_value, product, source * rows, 2)
    mixed = lax.psum_scatter(partial_value, "sub", scatter_dimension=2, tiled=True)
    first = jnp.sum(mixed, axis=0)
    second = jnp.sum(mixed * mixed, axis=0)
    projected = jnp.einsum("crq,cd->rqd", mixed, w_out, precision=highest)
    col_total = jnp.sum(w_out, axis=0)
    projected, first, second, col_total = lax.psum((projected, first, second, col_total), "ch")
    center = first / C
    spread = lax.rsqrt(second / C - center * center + 1e-05)
    outgoing = (projected - center[..., None] * col_total) * spread[..., None]
    gate = jax.nn.sigmoid(jnp.einsum("rqz,zd->rqd", normed, w_gate, precision=highest))
    update = gate * outgoing
    d_outgoing = cotangent * gate
    d_gate_pre = cotangent * outgoing * gate * (1.0 - gate)
    d_mixed_norm = jnp.einsum("rqd,cd->crq", d_outgoing, w_out, precision=highest)
    mean_one = jnp.sum(d_outgoing * col_total, axis=-1) / C
    mean_two = jnp.sum(d_outgoing * outgoing, axis=-1) / C
    mixed_norm = (mixed - center) * spread
    d_mixed = (d_mixed_norm - mean_one - mixed_norm * mean_two) * spread
    d_mixed_full = lax.all_gather(d_mixed, "sub", axis=2, tiled=True)
    d_left = jnp.einsum("cij,cjk->cik", d_mixed_full, right_all, precision=highest)
    d_right = jnp.transpose(
        lax.psum_scatter(
            jnp.einsum("cij,cik->jck", d_mixed_full, left, precision=highest),
            "row",
            scatter_dimension=0,
            tiled=True,
        ),
        (1, 0, 2),
    )
    d_proj = jnp.stack(
        [
            d_left * keep * sig_left,
            d_left * keep * proj[0] * sig_left * (1.0 - sig_left),
            d_right * keep * sig_right,
            d_right * keep * proj[2] * sig_right * (1.0 - sig_right),
        ]
    )
    d_normed_part = jnp.einsum("pcrq,pzc->rqz", d_proj, w_proj, precision=highest)
    d_normed = lax.psum(d_normed_part, "ch")
    d_normed = d_normed + jnp.einsum("rqd,zd->rqz", d_gate_pre, w_gate, precision=highest)
    mean_grad = jnp.mean(d_normed, axis=-1, keepdims=True)
    mean_cross = jnp.mean(d_normed * normed, axis=-1, keepdims=True)
    d_pair = (d_normed - mean_grad - normed * mean_cross) * pair_scale
    return (update, d_pair)


def solution(mesh):
    sizes = mesh.shape
    tiled = sizes["row"] == 8 and sizes["ch"] == 2 and sizes["sub"] == 1
    return jax.shard_map(
        on_tiles if tiled else on_ring,
        mesh=mesh,
        in_specs=(
            P(("grp", "row"), "sub", None),
            P(("grp", "row"), "sub"),
            P(None, None, "ch"),
            P(),
            P("ch", None),
            P(("grp", "row"), "sub", None),
        ),
        out_specs=(P(("grp", "row"), "sub", None), P(("grp", "row"), "sub", None)),
        check_vma=False,
    )
```

```python
import functools
import jax
import jax.numpy as jnp
from jax import lax
from jax.experimental import pallas as pl
from jax.experimental.pallas import tpu as pltpu
from jax.sharding import PartitionSpec as P

C = 128
EPS = 1e-05
HIGHEST = lax.Precision.HIGHEST
F32 = jnp.float32
CHUNK = 4
GROUP = 8


def dot(a, b):
    return lax.dot_general(a, b, (((1,), (0,)), ((), ())), precision=HIGHEST, preferred_element_type=F32)


def dot_t(a, b):
    return lax.dot_general(a, b, (((1,), (1,)), ((), ())), precision=HIGHEST, preferred_element_type=F32)


def norm(values):
    mean = jnp.mean(values, axis=-1, keepdims=True)
    centered = values - mean
    variance = jnp.mean(centered * centered, axis=-1, keepdims=True)
    scale = lax.rsqrt(variance + EPS)
    return (centered * scale, scale)


def flat(values):
    return values.reshape(-1, values.shape[-1])


def call(kernel, outs, args, scratch=(), flops=1000):
    smem = pl.BlockSpec(memory_space=pltpu.SMEM)
    vmem = pl.BlockSpec(memory_space=pltpu.VMEM)
    return pl.pallas_call(
        kernel,
        out_shape=[jax.ShapeDtypeStruct(shape, F32) for shape in outs],
        in_specs=[smem] + [vmem] * (len(args) - 1),
        out_specs=[vmem] * len(outs),
        scratch_shapes=[pltpu.VMEM(shape, F32) for shape in scratch],
        compiler_params=pltpu.CompilerParams(vmem_limit_bytes=24 * 1024 * 1024),
        cost_estimate=pl.CostEstimate(flops=flops, bytes_accessed=flops, transcendentals=0),
    )(*args)


def source_row(place, t, rows):
    half = rows // 2
    if t < half:
        return place[2] * half + t
    return (1 - place[2]) * half + t - half


def first_col(place, chip, core, rows):
    half = rows // 2
    return pl.multiple_of(chip * 2 * rows + core * rows + place[2] * half, half)


def both_halves(place, mine, other):
    first = place[2] == 0
    a, b = jnp.where(first, mine, other), jnp.where(first, other, mine)
    return jnp.concatenate([a, b], axis=0)


def gated_weights(place, mine, other, which):
    return jnp.concatenate([both_halves(place, mine[p], other[p]) for p in (which, which + 1)], axis=0)


def gated(normed, keep_rows, w):
    count, cols = keep_rows.shape
    chans = w.shape[0] // 2
    spread = jnp.transpose(jnp.concatenate([keep_rows] * (8 // count), axis=0))
    keep = jnp.concatenate([spread[:, u : u + 1] for u in range(count)], axis=0)
    proj = dot_t(normed, w)
    sig = jax.nn.sigmoid(proj[:, chans:]) * keep
    return sig * proj[:, :chans], sig


def first_kernel(place, pair, mask, cotangent, w_proj, normed, scale, keep, mine, first, second, third):
    rows, cols, width = pair.shape
    half = rows // 2
    chips = cols // (2 * rows)
    mine[...] = w_proj[...]
    keep[...] = mask[...].astype(F32)
    for t in range(0, half, CHUNK):
        at = slice(t, t + CHUNK)
        value, factor = norm(pair[pl.ds(source_row(place, t, rows), CHUNK)])
        normed[at] = value
        scale[at] = jnp.broadcast_to(factor, value.shape)
    first[...] = pair[:half]
    second[...] = pair[half:]
    for chip in range(chips):
        third[chip] = flat(cotangent[:, pl.ds(first_col(place, chip, 1 - place[1], rows), half), :])
    third[chips, :rows] = keep[...]


def right_kernel(rows, place, normed, keep, mine, other, right, open_part, slope):
    half, cols, chans = right.shape
    w = gated_weights(place, mine, other, 2)
    for t in range(0, half, CHUNK):
        at = slice(t, t + CHUNK)
        value, sig = gated(flat(normed[at]), keep[pl.ds(source_row(place, t, rows), CHUNK), :], w)
        shape = (CHUNK, cols, chans)
        right[at] = value.reshape(shape)
        open_part[at] = sig.reshape(shape)
        slope[at] = (value * (1.0 - sig)).reshape(shape)


def prepare_kernel(rows, place, pair, keep, cotangent, first, second, third, mine, other, w_gate, mine_out, other_out, *refs):
    left_here, left_there, open_part, slope, gate, d_here, d_there, w_out, normed_rows = refs
    half, cols, chans = open_part.shape
    chips = cols // (2 * rows)
    shape = (CHUNK, cols, chans)
    w = gated_weights(place, mine, other, 0)
    w_out[...] = both_halves(place, mine_out[...], other_out[...])
    for t in range(0, rows, CHUNK):
        row = source_row(place, t, rows)
        at = slice(t, t + CHUNK)
        normed, _ = norm(flat(pair[pl.ds(row, CHUNK)]))
        value, sig = gated(normed, keep[pl.ds(row, CHUNK), :], w)
        left_here[at] = value.reshape(shape)
        if t < half:
            open_part[at] = sig.reshape(shape)
            slope[at] = (value * (1.0 - sig)).reshape(shape)
        gate[at] = jax.nn.sigmoid(dot(normed, w_gate[...])).reshape(CHUNK, cols, -1)
        for chip in range(chips):
            near = pl.ds(first_col(place, chip, place[1], rows), half)
            d_here[chip, at] = gate[at, near, :] * cotangent[pl.ds(row, CHUNK), near, :]
        their_row = row % half
        normed, _ = norm(flat(jnp.where(row < half, first[pl.ds(their_row, CHUNK)], second[pl.ds(their_row, CHUNK)])))
        value, _ = gated(normed, third[chips, pl.ds(row, CHUNK), :], w)
        left_there[at] = value.reshape(shape)
        normed_rows[...] = normed.reshape(CHUNK, cols, -1)
        picked = [
            normed_rows[:, pl.ds(first_col(place, chip, place[1], rows), half), :] for chip in range(chips)
        ]
        opened = jax.nn.sigmoid(dot(flat(jnp.stack(picked)), w_gate[...])).reshape(chips, CHUNK, half, -1)
        for chip in range(chips):
            d_out = third[chip, pl.ds(row * half, CHUNK * half), :].reshape(CHUNK, half, -1)
            d_there[chip, at] = opened[chip] * d_out


def tile_body(step, place, right, left_here, left_there, d_here, d_there, w_out, out_here, out_there, d_x, d_right, partial, x):
    rows = left_here.shape[0]
    half, cols, chans = right.shape
    groups = cols // GROUP

    def forward(pair_at, _):
        for which, left in enumerate((left_here, left_there)):
            i = pair_at * 2
            value = [left[i], left[i + 1]]
            for j in range(half):
                block = right[j]
                for u in range(2):
                    product = (value[u] * block).reshape(groups, GROUP, chans)
                    partial[2 * which + u, j * GROUP : (j + 1) * GROUP] = jnp.sum(product, axis=0)
            for u in range(2):
                total = partial[2 * which + u, pl.ds(0, half, stride=GROUP), :]
                for s in range(1, GROUP):
                    total = total + partial[2 * which + u, pl.ds(s, half, stride=GROUP), :]
                x[pl.ds(pl.multiple_of((which * rows + i + u) * half, half), half), :] = total
        return 0

    lax.fori_loop(0, rows // 2, forward, 0)
    chip = jnp.bitwise_xor(place[0], step)
    d_out = jnp.concatenate([flat(d_here[chip]), flat(d_there[chip])], axis=0)
    normed, scale = norm(x[...])
    out = dot(normed, w_out[...])
    out_here[...] = out[: rows * half].reshape(rows, half, -1)
    out_there[...] = out[rows * half :].reshape(rows, half, -1)
    d_normed = dot_t(d_out, w_out[...])
    mean_one = jnp.mean(d_normed, axis=-1, keepdims=True)
    mean_two = jnp.mean(d_normed * normed, axis=-1, keepdims=True)
    d_x[...] = (d_normed - mean_one - normed * mean_two) * scale
    wide = 2 * GROUP

    def backward(at, _):
        here = pl.ds(pl.multiple_of(at * wide, wide), wide)

        def add(block, totals):
            totals = list(totals)
            for u in range(GROUP):
                for which, left in enumerate((left_here, left_there)):
                    i = block * GROUP + u
                    value = left[i, here, :]
                    for j in range(half):
                        totals[j] = totals[j] + value * d_x[pl.ds((which * rows + i) * half + j, 1), :]
            return tuple(totals)

        totals = lax.fori_loop(0, rows // GROUP, add, (jnp.zeros((wide, chans), F32),) * half)
        for j in range(half):
            d_right[j, here, :] = totals[j]
        return 0

    lax.fori_loop(0, cols // wide, backward, 0)


def tile_kernel(step, parts, place, *refs):
    rights, rest = refs[:parts], refs[parts:]
    if parts == 2:
        sum_out = rest[9]
        sum_out[...] = rights[0][...] + rights[1][...]
        tile_body(step, place, sum_out, *rest[:9], *rest[10:])
    else:
        tile_body(step, place, rights[0], *rest)


def left_kernel(tiles, bases, place, *refs):
    rights, d_xs = refs[:tiles], refs[tiles : 2 * tiles]
    base = refs[2 * tiles : 2 * tiles + bases]
    outs = refs[2 * tiles + bases :]
    half, cols, chans = rights[0].shape
    rows = outs[0].shape[0]
    for which, out in enumerate(outs):

        def body(pair_at, _):
            i = pair_at * 2
            if bases:
                totals = [base[which][i], base[which][i + 1]]
            else:
                totals = [jnp.zeros((cols, chans), F32)] * 2
            for right, d_x in zip(rights, d_xs):
                for j in range(half):
                    value = right[j]
                    for u in range(2):
                        at = (which * rows + i + u) * half + j
                        totals[u] = totals[u] + value * d_x[pl.ds(at, 1), :]
            out[i] = totals[0]
            out[i + 1] = totals[1]
            return 0

        lax.fori_loop(0, rows // 2, body, 0)
    for plane in range(2, bases):
        outs[1][rows + plane - 2] = flat(base[plane][...])


def share_kernel(place, kept, *refs):
    received, outs, (d_left, *packed, rest) = refs[0], refs[1:3], refs[3:]
    half = d_left.shape[0]
    part = half // 2
    block = half * half
    d_left[...] = kept[:half] + received[:half]
    for at in range(2):
        here = slice(half + at * part, half + (at + 1) * part)
        packed[at][:part] = kept[here] + received[here]
    for step, out in enumerate(outs):
        at = slice(step * block, (step + 1) * block)
        packed[0][part, at] = flat(out[half:])
        packed[1][part, at] = received[2 * half + step, block:]
        rest[0, at] = flat(out[:half])
        rest[1, at] = received[2 * half + step, :block]


def gather_out(place, rows, t, out, here, early_other, early_far, received, far):
    half = rows // 2
    block = half * half
    for far_half in (0, 1):
        source = (t + far_half * half) % rows
        at, wide = slice(source, source + half), slice(source * half, source * half + block)
        for far_core in (0, 1):
            core = place[1] + far_core * (1 - 2 * place[1])
            side = place[2] + far_half * (1 - 2 * place[2])
            for step in range(4):
                chip = jnp.bitwise_xor(place[0], step)
                first = pl.multiple_of(chip * 2 * rows + core * rows + side * half, half)
                if far_half:
                    if step < 2:
                        value = early_far[far_core, step, at]
                    else:
                        ref, plane = far[far_core]
                        value = ref[plane, (step - 2) * block : (step - 1) * block].reshape(half, half, -1)
                elif far_core:
                    if step < 2:
                        value = early_other[step, at]
                    else:
                        value = received[rows + step - 2, wide].reshape(half, half, -1)
                else:
                    value = here[step][at]
                out[t : t + half, pl.ds(first, half), :] = value


def update_kernel(rows, place, *refs):
    here, early_other, early_far, received, far, far_next, rest, gate, update, out = refs[:4], *refs[4:]
    half = rows // 2
    part = half // 2
    gather_out(place, rows, 0, out, here, early_other, early_far, received, ((far, part), (far_next, part)))
    gather_out(place, rows, half, out, here, early_other, early_far, received, ((rest, 0), (rest, 1)))
    for t in range(0, rows, CHUNK):
        update[pl.ds(source_row(place, t, rows), CHUNK)] = gate[t : t + CHUNK] * out[t : t + CHUNK]


def base_kernel(rows, place, *refs):
    here, early_other, early_far, received, far, far_next = refs[:4], *refs[4:9]
    gate, cotangent, w_gate, d_left, open_part, slope, mine, other, base, out = refs[9:]
    half, cols, chans = base.shape
    part = half // 2
    gather_out(place, rows, 0, out, here, early_other, early_far, received, ((far, part), (far_next, part)))
    w = gated_weights(place, mine, other, 0)
    for t in range(0, half, CHUNK):
        at = slice(t, t + CHUNK)
        opened = gate[at]
        d_gate = cotangent[pl.ds(source_row(place, t, rows), CHUNK)] * (opened * out[at]) * (1.0 - opened)
        grad = flat(d_left[at] + (far, far_next)[t // part][t % part : t % part + CHUNK])
        both = jnp.concatenate([grad * flat(open_part[at]), grad * flat(slope[at])], axis=1)
        base[at] = (dot_t(flat(d_gate), w_gate[...]) + dot(both, w)).reshape(CHUNK, cols, -1)


def pair_kernel(rows, place, normed, scale, base, d_right, d_right_near, d_right_middle, d_right_far, open_part, slope, mine, other, d_mine, d_pair):
    half, cols, chans = base.shape
    w = gated_weights(place, mine, other, 2)
    for t in range(0, half, CHUNK):
        at = slice(t, t + CHUNK)
        grad = flat(d_right[at] + d_right_near[at] + (d_right_middle[at] + d_right_far[at]))
        both = jnp.concatenate([grad * flat(open_part[at]), grad * flat(slope[at])], axis=1)
        d_normed = flat(base[at]) + dot(both, w)
        value = flat(normed[at])
        mean_grad = jnp.mean(d_normed, axis=-1, keepdims=True)
        mean_cross = jnp.mean(d_normed * value, axis=-1, keepdims=True)
        d_mine[at] = ((d_normed - mean_grad - value * mean_cross) * flat(scale[at])).reshape(CHUNK, cols, -1)
        d_pair[pl.ds(source_row(place, t, rows), CHUNK)] = d_mine[at]


def join_kernel(place, other, whole, joined, sem):
    half = other.shape[0]
    copy = pltpu.make_async_copy(other, joined.at[pl.ds((1 - lax.axis_index("ch")) * half, half)], sem)
    copy.start()
    copy.wait()


def join(place, other, whole):
    anywhere = pl.BlockSpec(memory_space=pl.ANY)
    return pl.pallas_call(
        join_kernel,
        out_shape=jax.ShapeDtypeStruct(whole.shape, F32),
        in_specs=[pl.BlockSpec(memory_space=pltpu.SMEM), pl.BlockSpec(memory_space=pltpu.VMEM), anywhere],
        out_specs=anywhere,
        input_output_aliases={2: 0},
        compiler_params=pltpu.CompilerParams(vmem_limit_bytes=2 * 1024 * 1024),
        scratch_shapes=[pltpu.SemaphoreType.DMA],
    )(place, other, whole)


def along(block, pairs):
    return lax.ppermute(block, "row", [(2 * a + core, 2 * b + core) for a, b in pairs for core in (0, 1)])


def other_core(block):
    return lax.ppermute(block, "row", [(i, i ^ 1) for i in range(lax.axis_size("row"))])


def other_half(block):
    return lax.ppermute(block, "ch", [(0, 1), (1, 0)])


NEXT = [(0, 1), (1, 0), (2, 3), (3, 2)]
MIDDLE = [(1, 2), (2, 1)]
OUTWARD = [(1, 0), (2, 3)]
INWARD = [(0, 1), (3, 2)]
ENDS = [(0, 3), (3, 0)]


def on_tiles(pair, pair_mask, w_proj, w_gate, w_out, cotangent):
    rows, cols, width = pair.shape
    half = rows // 2
    chips = cols // (2 * rows)
    chans = 2 * w_out.shape[0]
    row, side = lax.axis_index("row"), lax.axis_index("ch")
    place = jnp.stack([row // 2, row % 2, side]).astype(jnp.int32)

    w_mine = jnp.swapaxes(w_proj, 1, 2)
    other = other_half(flat(w_mine)).reshape(w_mine.shape)
    kept = (half, cols, chans)
    normed, scale, keep, mine, *sent = call(
        first_kernel,
        [(half, cols, width)] * 2 + [(rows, cols), w_mine.shape] + [(half, cols, width)] * 2 + [(chips + 1, cols, width)],
        (place, pair, pair_mask, cotangent, w_mine),
    )
    theirs = [other_core(block) for block in sent]
    other_out = other_half(w_out)
    right, open_right, slope_right = call(
        functools.partial(right_kernel, rows), [kept] * 3, (place, normed, keep, mine, other)
    )
    near = along(right, NEXT)
    middle = along(right, MIDDLE)
    quarter = (chips, rows, half, width)
    tile_outs = [(rows, half, width)] * 2 + [(2 * rows * half, chans), kept]
    tile_scratch = [(4, half * GROUP, chans), (2 * rows * half, chans)]
    out_here, out_there, d_x, d_right, rights = ([None] * 4 for _ in range(5))
    rights[0] = right
    left, left_there, open_left, slope_left, gate, d_here, d_there, w_all_out = call(
        functools.partial(prepare_kernel, rows),
        [(rows, cols, chans)] * 2 + [kept] * 2 + [(rows, cols, width), quarter, quarter, (chans, width)],
        (place, pair, keep, cotangent, *theirs, mine, other, w_gate, w_out, other_out),
        scratch=[(CHUNK, cols, width)],
    )

    def tile(step, *blocks):
        got = call(
            functools.partial(tile_kernel, step, len(blocks)),
            tile_outs + ([kept] if len(blocks) == 2 else []),
            (place, *blocks, left, left_there, d_here, d_there, w_all_out),
            scratch=tile_scratch,
        )
        out_here[step], out_there[step], d_x[step], d_right[step] = got[:4]
        rights[step] = got[4] if len(blocks) == 2 else blocks[0]

    near, middle, d_here = lax.optimization_barrier((near, middle, d_here))
    cross = along(near, MIDDLE)
    outer = along(middle, OUTWARD)
    tile(0, right)
    tile(1, near)
    early_other = other_core(jnp.stack(out_there[:2]))
    d_left_here, d_left_there = call(
        functools.partial(left_kernel, 2, 0),
        [(rows, cols, chans)] * 2,
        (place, *rights[:2], *d_x[:2]),
    )
    cross, early_other, d_left_here = lax.optimization_barrier((cross, early_other, d_left_here))
    far = along(cross, OUTWARD)
    early_far = other_half(jnp.stack([jnp.stack(out_here[:2]), early_other]))
    tile(2, cross, outer)
    inward = along(d_right[2], INWARD)
    swapped = along(d_right[2], MIDDLE)
    far, d_x[2] = lax.optimization_barrier((far, d_x[2]))
    tile(3, middle, far)
    d_left_kept, d_left_sent = call(
        functools.partial(left_kernel, 2, 4),
        [(rows, cols, chans), (rows + 2, cols, chans)],
        (place, *rights[2:], *d_x[2:], d_left_here, d_left_there, out_there[2], out_there[3]),
    )
    to_near, to_middle, early_far, d_left_sent = lax.optimization_barrier(
        (d_right[1] + swapped, d_right[3] + inward, early_far, d_left_sent)
    )
    received = other_core(d_left_sent)
    from_near = along(to_near, NEXT)
    from_middle = along(to_middle, MIDDLE)
    from_far = along(d_right[3], ENDS)
    packed_shape = (half // 2 + 1, cols, chans)
    d_left, *shared, rest = call(
        share_kernel,
        [kept, packed_shape, packed_shape, (2, cols, chans)],
        (place, d_left_kept, received, out_here[2], out_here[3]),
    )
    shared = [other_half(part) for part in shared]
    *shared, rest, from_far = lax.optimization_barrier((*shared, rest, from_far))
    rest_other = other_half(rest)
    outs = (*out_here, early_other, early_far, received, *shared)
    (base,) = call(
        functools.partial(base_kernel, rows),
        [(half, cols, width)],
        (place, *outs, gate, cotangent, w_gate, d_left, open_left, slope_left, mine, other),
        scratch=[(half, cols, width)],
    )
    base, rest_other = lax.optimization_barrier((base, rest_other))
    d_mine, d_pair = call(
        functools.partial(pair_kernel, rows),
        [(half, cols, width), (rows, cols, width)],
        (place, normed, scale, base, d_right[0], from_near, from_middle, from_far, open_right, slope_right, mine, other),
    )
    d_other = other_half(d_mine)
    _, gate_late = lax.optimization_barrier((d_mine, gate))
    (update,) = call(
        functools.partial(update_kernel, rows),
        [(rows, cols, width)],
        (place, *outs, rest_other, gate_late),
        scratch=[(rows, cols, width)],
    )
    d_other, update = lax.optimization_barrier((d_other, update))
    d_pair = join(place, d_other, d_pair)
    return (update, d_pair)


def passed_along(block, axis, distance):
    devices = range(lax.axis_size(axis))
    route = [((i - distance) % len(devices), i) for i in devices]
    return lax.ppermute(block, axis, route)


def normalize(values):
    mean = jnp.mean(values, axis=-1, keepdims=True)
    centered = values - mean
    variance = jnp.mean(centered * centered, axis=-1, keepdims=True)
    scale = lax.rsqrt(variance + 1e-05)
    return (centered * scale, scale)


def on_ring(pair, pair_mask, w_proj, w_gate, w_out, cotangent):
    highest = lax.Precision.HIGHEST
    normed, pair_scale = normalize(pair)
    proj = jnp.einsum("rqz,pzc->pcrq", normed, w_proj, precision=highest)
    keep = pair_mask.astype(jnp.float32)
    sig_left = jax.nn.sigmoid(proj[1])
    sig_right = jax.nn.sigmoid(proj[3])
    left = keep * sig_left * proj[0]
    right = keep * sig_right * proj[2]
    chans, rows, cols = left.shape
    count = lax.axis_size("row")
    here = lax.axis_index("row")

    def visit(step, carry):
        block, store, partial_value = carry
        source = (here - step) % count
        store = lax.dynamic_update_slice_in_dim(store, block, source * rows, 1)
        product = jnp.einsum("cik,cjk->cij", left, block, precision=highest)
        partial_value = lax.dynamic_update_slice_in_dim(partial_value, product, source * rows, 2)
        block = passed_along(block, "row", 1)
        return (block, store, partial_value)

    store = jnp.zeros((chans, rows * count, cols), jnp.float32)
    partial_value = jnp.zeros((chans, rows, rows * count), jnp.float32)
    block, store, partial_value = lax.fori_loop(0, count - 1, visit, (right, store, partial_value))
    source = (here + 1) % count
    right_all = lax.dynamic_update_slice_in_dim(store, block, source * rows, 1)
    product = jnp.einsum("cik,cjk->cij", left, block, precision=highest)
    partial_value = lax.dynamic_update_slice_in_dim(partial_value, product, source * rows, 2)
    mixed = lax.psum_scatter(partial_value, "sub", scatter_dimension=2, tiled=True)
    first = jnp.sum(mixed, axis=0)
    second = jnp.sum(mixed * mixed, axis=0)
    projected = jnp.einsum("crq,cd->rqd", mixed, w_out, precision=highest)
    col_total = jnp.sum(w_out, axis=0)
    projected, first, second, col_total = lax.psum((projected, first, second, col_total), "ch")
    center = first / C
    spread = lax.rsqrt(second / C - center * center + 1e-05)
    outgoing = (projected - center[..., None] * col_total) * spread[..., None]
    gate = jax.nn.sigmoid(jnp.einsum("rqz,zd->rqd", normed, w_gate, precision=highest))
    update = gate * outgoing
    d_outgoing = cotangent * gate
    d_gate_pre = cotangent * outgoing * gate * (1.0 - gate)
    d_mixed_norm = jnp.einsum("rqd,cd->crq", d_outgoing, w_out, precision=highest)
    mean_one = jnp.sum(d_outgoing * col_total, axis=-1) / C
    mean_two = jnp.sum(d_outgoing * outgoing, axis=-1) / C
    mixed_norm = (mixed - center) * spread
    d_mixed = (d_mixed_norm - mean_one - mixed_norm * mean_two) * spread
    d_mixed_full = lax.all_gather(d_mixed, "sub", axis=2, tiled=True)
    d_left = jnp.einsum("cij,cjk->cik", d_mixed_full, right_all, precision=highest)
    d_right = jnp.transpose(
        lax.psum_scatter(
            jnp.einsum("cij,cik->jck", d_mixed_full, left, precision=highest),
            "row",
            scatter_dimension=0,
            tiled=True,
        ),
        (1, 0, 2),
    )
    d_proj = jnp.stack(
        [
            d_left * keep * sig_left,
            d_left * keep * proj[0] * sig_left * (1.0 - sig_left),
            d_right * keep * sig_right,
            d_right * keep * proj[2] * sig_right * (1.0 - sig_right),
        ]
    )
    d_normed_part = jnp.einsum("pcrq,pzc->rqz", d_proj, w_proj, precision=highest)
    d_normed = lax.psum(d_normed_part, "ch")
    d_normed = d_normed + jnp.einsum("rqd,zd->rqz", d_gate_pre, w_gate, precision=highest)
    mean_grad = jnp.mean(d_normed, axis=-1, keepdims=True)
    mean_cross = jnp.mean(d_normed * normed, axis=-1, keepdims=True)
    d_pair = (d_normed - mean_grad - normed * mean_cross) * pair_scale
    return (update, d_pair)


def solution(mesh):
    sizes = mesh.shape
    tiled = sizes["row"] == 8 and sizes["ch"] == 2 and sizes["sub"] == 1
    return jax.shard_map(
        on_tiles if tiled else on_ring,
        mesh=mesh,
        in_specs=(
            P(("grp", "row"), "sub", None),
            P(("grp", "row"), "sub"),
            P(None, None, "ch"),
            P(),
            P("ch", None),
            P(("grp", "row"), "sub", None),
        ),
        out_specs=(P(("grp", "row"), "sub", None), P(("grp", "row"), "sub", None)),
        check_vma=False,
    )
```

```python
import functools
import jax
import jax.numpy as jnp
from jax import lax
from jax.experimental import pallas as pl
from jax.experimental.pallas import tpu as pltpu
from jax.sharding import PartitionSpec as P

C = 128
EPS = 1e-05
HIGHEST = lax.Precision.HIGHEST
F32 = jnp.float32
CHUNK = 4
GROUP = 8


def halves(values):
    high = values.astype(jnp.bfloat16)
    return high, (values - high.astype(F32)).astype(jnp.bfloat16)


def contract(a, b, dims):
    (a_high, a_low), (b_high, b_low) = halves(a), halves(b)
    one = lambda x, y: lax.dot_general(x, y, (dims, ((), ())), preferred_element_type=F32)
    return one(a_high, b_high) + (one(a_high, b_low) + one(a_low, b_high))


def dot(a, b):
    return contract(a, b, ((1,), (0,)))


def dot_t(a, b):
    return contract(a, b, ((1,), (1,)))


def norm(values):
    mean = jnp.mean(values, axis=-1, keepdims=True)
    centered = values - mean
    variance = jnp.mean(centered * centered, axis=-1, keepdims=True)
    scale = lax.rsqrt(variance + EPS)
    return (centered * scale, scale)


def flat(values):
    return values.reshape(-1, values.shape[-1])


def call(kernel, outs, args, scratch=(), distant=0, sems=0):
    vmem = pl.BlockSpec(memory_space=pltpu.VMEM)
    spaces = [pl.BlockSpec(memory_space=pltpu.SMEM)] + [pl.BlockSpec(memory_space=pltpu.HBM)] * distant
    args = list(args)
    args[1 : 1 + distant] = [pltpu.with_memory_space_constraint(a, pltpu.HBM) for a in args[1 : 1 + distant]]
    return pl.pallas_call(
        kernel,
        out_shape=[jax.ShapeDtypeStruct(shape, F32) for shape in outs],
        in_specs=spaces + [vmem] * (len(args) - len(spaces)),
        out_specs=[vmem] * len(outs),
        scratch_shapes=[pltpu.VMEM(*shape) if isinstance(shape[0], tuple) else pltpu.VMEM(shape, F32) for shape in scratch]
        + ([pltpu.SemaphoreType.DMA((sems,))] if sems else []),
        compiler_params=pltpu.CompilerParams(vmem_limit_bytes=24 * 1024 * 1024),
        cost_estimate=pl.CostEstimate(flops=1000, bytes_accessed=1000, transcendentals=0),
    )(*args)


def source_row(place, t, rows):
    half = rows // 2
    if t < half:
        return place[2] * half + t
    return (1 - place[2]) * half + t - half


def first_col(place, chip, core, rows):
    half = rows // 2
    return pl.multiple_of(chip * 2 * rows + core * rows + place[2] * half, half)


def both_halves(place, mine, other):
    first = place[2] == 0
    a, b = jnp.where(first, mine, other), jnp.where(first, other, mine)
    return jnp.concatenate([a, b], axis=0)


def gated_weights(place, mine, other, which):
    return jnp.concatenate([both_halves(place, mine[p], other[p]) for p in (which, which + 1)], axis=0)


def gated(normed, keep_rows, w):
    count, cols = keep_rows.shape
    chans = w.shape[0] // 2
    spread = jnp.transpose(jnp.concatenate([keep_rows] * (8 // count), axis=0))
    keep = jnp.concatenate([spread[:, u : u + 1] for u in range(count)], axis=0)
    proj = dot_t(normed, w)
    sig = jax.nn.sigmoid(proj[:, chans:]) * keep
    return sig * proj[:, :chans], sig


def first_kernel(place, pair, mask, w_proj, normed, scale, keep, mine, first, second, flags, sems):
    half = first.shape[0]
    moves = ((pair.at[:half], first), (pair.at[half:], second), (mask, flags), (w_proj, mine))
    copies = [pltpu.make_async_copy(source, target, sems.at[at]) for at, (source, target) in enumerate(moves)]
    for copy in copies:
        copy.start()
    for copy in copies:
        copy.wait()
    keep[...] = flags[...].astype(F32)
    for t in range(0, half, CHUNK):
        at = slice(t, t + CHUNK)
        value, factor = norm(jnp.where(place[2] == 0, first[at], second[at]))
        normed[at] = value
        scale[at] = jnp.broadcast_to(factor, value.shape)


def third_kernel(place, cotangent, keep, packed, sems):
    rows = cotangent.shape[0]
    half, chips = rows // 2, packed.shape[0] - 1
    copies = []
    for chip in range(chips):
        source = cotangent.at[:, pl.ds(first_col(place, chip, 1 - place[1], rows), half), :]
        copies.append(pltpu.make_async_copy(source, packed.at[chip], sems.at[chip]))
    for copy in copies:
        copy.start()
    packed[chips, :, 0, :] = keep[...]
    for copy in copies:
        copy.wait()


def right_kernel(rows, place, normed, keep, mine, other, right, open_part, slope):
    half, cols, chans = right.shape
    w = gated_weights(place, mine, other, 2)
    for t in range(0, half, CHUNK):
        at = slice(t, t + CHUNK)
        value, sig = gated(flat(normed[at]), keep[pl.ds(source_row(place, t, rows), CHUNK), :], w)
        shape = (CHUNK, cols, chans)
        right[at] = value.reshape(shape)
        open_part[at] = sig.reshape(shape)
        slope[at] = (value * (1.0 - sig)).reshape(shape)


def prepare_kernel(rows, place, pair, keep, cotangent, first, second, third, mine, other, w_gate, mine_out, other_out, *refs):
    left_here, left_there, open_part, slope, gate, d_here, d_there, w_out, normed_rows = refs
    half, cols, chans = open_part.shape
    chips = cols // (2 * rows)
    shape = (CHUNK, cols, chans)
    w = gated_weights(place, mine, other, 0)
    w_out[...] = both_halves(place, mine_out[...], other_out[...])
    for t in range(0, rows, CHUNK):
        row = source_row(place, t, rows)
        at = slice(t, t + CHUNK)
        normed, _ = norm(flat(pair[pl.ds(row, CHUNK)]))
        value, sig = gated(normed, keep[pl.ds(row, CHUNK), :], w)
        left_here[at] = value.reshape(shape)
        if t < half:
            open_part[at] = sig.reshape(shape)
            slope[at] = (value * (1.0 - sig)).reshape(shape)
        gate[at] = jax.nn.sigmoid(dot(normed, w_gate[...])).reshape(CHUNK, cols, -1)
        for chip in range(chips):
            near = pl.ds(first_col(place, chip, place[1], rows), half)
            d_here[chip, at] = gate[at, near, :] * cotangent[pl.ds(row, CHUNK), near, :]
        their_row = row % half
        normed, _ = norm(flat(jnp.where(row < half, first[pl.ds(their_row, CHUNK)], second[pl.ds(their_row, CHUNK)])))
        value, _ = gated(normed, third[chips, pl.ds(row, CHUNK), 0, :], w)
        left_there[at] = value.reshape(shape)
        normed_rows[...] = normed.reshape(CHUNK, cols, -1)
        picked = [
            normed_rows[:, pl.ds(first_col(place, chip, place[1], rows), half), :] for chip in range(chips)
        ]
        opened = jax.nn.sigmoid(dot(flat(jnp.stack(picked)), w_gate[...])).reshape(chips, CHUNK, half, -1)
        for chip in range(chips):
            d_there[chip, at] = opened[chip] * third[chip, pl.ds(row, CHUNK)]


def tile_body(step, place, right, left_here, left_there, d_here, d_there, w_out, out_here, out_there, d_x, d_right, partial, x):
    rows = left_here.shape[0]
    half, cols, chans = right.shape
    groups = cols // GROUP

    def forward(pair_at, _):
        for which, left in enumerate((left_here, left_there)):
            i = pair_at * 2
            value = [left[i], left[i + 1]]
            for j in range(half):
                block = right[j]
                for u in range(2):
                    product = (value[u] * block).reshape(groups, GROUP, chans)
                    partial[2 * which + u, j * GROUP : (j + 1) * GROUP] = jnp.sum(product, axis=0)
            for u in range(2):
                total = partial[2 * which + u, pl.ds(0, half, stride=GROUP), :]
                for s in range(1, GROUP):
                    total = total + partial[2 * which + u, pl.ds(s, half, stride=GROUP), :]
                x[pl.ds(pl.multiple_of((which * rows + i + u) * half, half), half), :] = total
        return 0

    lax.fori_loop(0, rows // 2, forward, 0)
    chip = jnp.bitwise_xor(place[0], step)
    d_out = jnp.concatenate([flat(d_here[chip]), flat(d_there[chip])], axis=0)
    normed, scale = norm(x[...])
    out = dot(normed, w_out[...])
    out_here[...] = out[: rows * half].reshape(rows, half, -1)
    out_there[...] = out[rows * half :].reshape(rows, half, -1)
    d_normed = dot_t(d_out, w_out[...])
    mean_one = jnp.mean(d_normed, axis=-1, keepdims=True)
    mean_two = jnp.mean(d_normed * normed, axis=-1, keepdims=True)
    d_x[...] = (d_normed - mean_one - normed * mean_two) * scale
    wide = 2 * GROUP

    def backward(at, _):
        here = pl.ds(pl.multiple_of(at * wide, wide), wide)

        def add(block, totals):
            totals = list(totals)
            for u in range(GROUP):
                for which, left in enumerate((left_here, left_there)):
                    i = block * GROUP + u
                    value = left[i, here, :]
                    for j in range(half):
                        totals[j] = totals[j] + value * d_x[pl.ds((which * rows + i) * half + j, 1), :]
            return tuple(totals)

        totals = lax.fori_loop(0, rows // GROUP, add, (jnp.zeros((wide, chans), F32),) * half)
        for j in range(half):
            d_right[j, here, :] = totals[j]
        return 0

    lax.fori_loop(0, cols // wide, backward, 0)


def tile_kernel(step, parts, place, *refs):
    rights, rest = refs[:parts], refs[parts:]
    if parts == 2:
        sum_out = rest[9]
        sum_out[...] = rights[0][...] + rights[1][...]
        tile_body(step, place, sum_out, *rest[:9], *rest[10:])
    else:
        tile_body(step, place, rights[0], *rest)


def left_rows(tiles, base, out, first, count, start):
    half, cols, chans = tiles[0][0].shape

    def body(pair_at, _):
        i = pair_at * 2
        totals = [jnp.zeros((cols, chans), F32)] * 2 if base is None else [base[start + i], base[start + i + 1]]
        for right, d_x in tiles:
            for j in range(half):
                value = right[j]
                for u in range(2):
                    totals[u] = totals[u] + value * d_x[pl.ds((first + i + u) * half + j, 1), :]
        out[start + i] = totals[0]
        out[start + i + 1] = totals[1]
        return 0

    lax.fori_loop(0, count // 2, body, 0)


def left_kernel(tiles, based, place, *refs):
    pairs = tuple(zip(refs[:tiles], refs[tiles : 2 * tiles]))
    bases = refs[2 * tiles : 2 * tiles + 2] if based else (None, None)
    rows = refs[-1].shape[0]
    for which, out in enumerate(refs[-2:]):
        left_rows(pairs, bases[which], out, which * rows, rows, 0)


def last_left_kernel(place, right, d_x, here, there, out_next, out_last, kept, sent):
    tiles = ((right, d_x),)
    rows = here.shape[0]
    left_rows(tiles, here, kept, 0, rows, 0)
    left_rows(tiles, there, sent, rows, rows, 0)
    sent[rows] = flat(out_next[...])
    sent[rows + 1] = flat(out_last[...])


def share_kernel(place, kept, received, out_next, out_last, d_left, packed, rest):
    half = d_left.shape[0]
    block = half * half
    d_left[...] = kept[:half] + received[:half]
    packed[...] = kept[half:] + received[half : 2 * half]
    for step, out in enumerate((out_next, out_last)):
        at = slice(step * block, (step + 1) * block)
        plane = 2 * half + step
        rest[0, at] = flat(out[half:])
        rest[1, at] = received[plane, block:]
        rest[2, at] = flat(out[:half])
        rest[3, at] = received[plane, :block]


def gather_out(place, rows, t, out, here, early_other, early_far, received, far):
    half = rows // 2
    block = half * half
    for far_half in (0, 1):
        source = (t + far_half * half) % rows
        at, wide = slice(source, source + half), slice(source * half, source * half + block)
        for far_core in (0, 1):
            core = place[1] + far_core * (1 - 2 * place[1])
            side = place[2] + far_half * (1 - 2 * place[2])
            for step in range(4):
                chip = jnp.bitwise_xor(place[0], step)
                first = pl.multiple_of(chip * 2 * rows + core * rows + side * half, half)
                if far_half:
                    if step < 2:
                        value = early_far[far_core, step, at]
                    else:
                        ref, plane = far[far_core]
                        value = ref[plane, (step - 2) * block : (step - 1) * block].reshape(half, half, -1)
                elif far_core:
                    if step < 2:
                        value = early_other[step, at]
                    else:
                        value = received[rows + step - 2, wide].reshape(half, half, -1)
                else:
                    value = here[step][at]
                out[t : t + half, pl.ds(first, half), :] = value


def update_kernel(rows, place, *refs):
    here, early_other, early_far, received, rest, gate, update, out = refs[:4], *refs[4:]
    half = rows // 2
    gather_out(place, rows, 0, out, here, early_other, early_far, received, ((rest, 0), (rest, 1)))
    gather_out(place, rows, half, out, here, early_other, early_far, received, ((rest, 2), (rest, 3)))
    for t in range(0, rows, CHUNK):
        update[pl.ds(source_row(place, t, rows), CHUNK)] = gate[t : t + CHUNK] * out[t : t + CHUNK]


def base_kernel(rows, place, *refs):
    here, early_other, early_far, received, rest = refs[:4], *refs[4:8]
    gate, cotangent, w_gate, d_left, far, open_part, slope, mine, other, base, out = refs[8:]
    half, cols, chans = base.shape
    gather_out(place, rows, 0, out, here, early_other, early_far, received, ((rest, 0), (rest, 1)))
    w = gated_weights(place, mine, other, 0)
    for t in range(0, half, CHUNK):
        at = slice(t, t + CHUNK)
        opened = gate[at]
        d_gate = cotangent[pl.ds(source_row(place, t, rows), CHUNK)] * (opened * out[at]) * (1.0 - opened)
        grad = flat(d_left[at] + far[at])
        both = jnp.concatenate([grad * flat(open_part[at]), grad * flat(slope[at])], axis=1)
        base[at] = (dot_t(flat(d_gate), w_gate[...]) + dot(both, w)).reshape(CHUNK, cols, -1)


def pair_kernel(rows, place, normed, scale, base, d_right, d_right_near, d_right_middle, d_right_far, open_part, slope, mine, other, d_mine, d_pair):
    half, cols, chans = base.shape
    w = gated_weights(place, mine, other, 2)
    for t in range(0, half, CHUNK):
        at = slice(t, t + CHUNK)
        grad = flat(d_right[at] + d_right_near[at] + (d_right_middle[at] + d_right_far[at]))
        both = jnp.concatenate([grad * flat(open_part[at]), grad * flat(slope[at])], axis=1)
        d_normed = flat(base[at]) + dot(both, w)
        value = flat(normed[at])
        mean_grad = jnp.mean(d_normed, axis=-1, keepdims=True)
        mean_cross = jnp.mean(d_normed * value, axis=-1, keepdims=True)
        d_mine[at] = ((d_normed - mean_grad - value * mean_cross) * flat(scale[at])).reshape(CHUNK, cols, -1)
        d_pair[pl.ds(source_row(place, t, rows), CHUNK)] = d_mine[at]


def join_kernel(place, other, whole, joined, sem):
    half = other.shape[0]
    copy = pltpu.make_async_copy(other, joined.at[pl.ds((1 - lax.axis_index("ch")) * half, half)], sem)
    copy.start()
    copy.wait()


def join(place, other, whole):
    anywhere = pl.BlockSpec(memory_space=pl.ANY)
    return pl.pallas_call(
        join_kernel,
        out_shape=jax.ShapeDtypeStruct(whole.shape, F32),
        in_specs=[pl.BlockSpec(memory_space=pltpu.SMEM), pl.BlockSpec(memory_space=pltpu.VMEM), anywhere],
        out_specs=anywhere,
        input_output_aliases={2: 0},
        compiler_params=pltpu.CompilerParams(vmem_limit_bytes=2 * 1024 * 1024),
        scratch_shapes=[pltpu.SemaphoreType.DMA],
    )(place, other, whole)


def along(block, pairs):
    return lax.ppermute(block, "row", [(2 * a + core, 2 * b + core) for a, b in pairs for core in (0, 1)])


def other_core(block):
    return lax.ppermute(block, "row", [(i, i ^ 1) for i in range(lax.axis_size("row"))])


def other_half(block):
    return lax.ppermute(block, "ch", [(0, 1), (1, 0)])


NEXT = [(0, 1), (1, 0), (2, 3), (3, 2)]
MIDDLE = [(1, 2), (2, 1)]
OUTWARD = [(1, 0), (2, 3)]
INWARD = [(0, 1), (3, 2)]
ENDS = [(0, 3), (3, 0)]


def on_tiles(pair, pair_mask, w_proj, w_gate, w_out, cotangent):
    rows, cols, width = pair.shape
    half = rows // 2
    chips = cols // (2 * rows)
    chans = 2 * w_out.shape[0]
    row, side = lax.axis_index("row"), lax.axis_index("ch")
    place = jnp.stack([row // 2, row % 2, side]).astype(jnp.int32)

    w_mine = jnp.swapaxes(w_proj, 1, 2)
    other = other_half(flat(w_mine)).reshape(w_mine.shape)
    kept = (half, cols, chans)
    other_out = other_half(w_out)
    normed, scale, keep, mine, *sent = call(
        first_kernel,
        [(half, cols, width)] * 2 + [(rows, cols), w_mine.shape] + [(half, cols, width)] * 2,
        (place, pair, pair_mask, w_mine),
        scratch=[((rows, cols), jnp.int32)],
        distant=3,
        sems=4,
    )
    theirs = [other_core(block) for block in sent]
    other, other_out = lax.optimization_barrier((other, other_out))
    right, open_right, slope_right = call(
        functools.partial(right_kernel, rows), [kept] * 3, (place, normed, keep, mine, other)
    )
    near = along(right, NEXT)
    middle = along(right, MIDDLE)
    _, cotangent_late = lax.optimization_barrier((right, cotangent))
    (third,) = call(
        third_kernel, [(chips + 1, rows, half, width)], (place, cotangent_late, keep), distant=1, sems=chips
    )
    theirs.append(other_core(third))
    quarter = (chips, rows, half, width)
    tile_outs = [(rows, half, width)] * 2 + [(2 * rows * half, chans), kept]
    tile_scratch = [(4, half * GROUP, chans), (2 * rows * half, chans)]
    out_here, out_there, d_x, d_right, rights = ([None] * 4 for _ in range(5))
    rights[0] = right
    left, left_there, open_left, slope_left, gate, d_here, d_there, w_all_out = call(
        functools.partial(prepare_kernel, rows),
        [(rows, cols, chans)] * 2 + [kept] * 2 + [(rows, cols, width), quarter, quarter, (chans, width)],
        (place, pair, keep, cotangent, *theirs, mine, other, w_gate, w_out, other_out),
        scratch=[(CHUNK, cols, width)],
    )

    def tile(step, *blocks):
        got = call(
            functools.partial(tile_kernel, step, len(blocks)),
            tile_outs + ([kept] if len(blocks) == 2 else []),
            (place, *blocks, left, left_there, d_here, d_there, w_all_out),
            scratch=tile_scratch,
        )
        out_here[step], out_there[step], d_x[step], d_right[step] = got[:4]
        rights[step] = got[4] if len(blocks) == 2 else blocks[0]

    near, d_here = lax.optimization_barrier((near, d_here))
    cross = along(near, MIDDLE)
    outer = along(middle, OUTWARD)
    tile(0, right)
    tile(1, near)
    early_other = other_core(jnp.stack(out_there[:2]))
    d_left_here, d_left_there = call(
        functools.partial(left_kernel, 2, False),
        [(rows, cols, chans)] * 2,
        (place, *rights[:2], *d_x[:2]),
    )
    cross, early_other, d_left_here = lax.optimization_barrier((cross, early_other, d_left_here))
    far = along(cross, OUTWARD)
    early_far = other_half(jnp.stack([jnp.stack(out_here[:2]), early_other]))
    tile(2, cross, outer)
    inward = along(d_right[2], INWARD)
    swapped = along(d_right[2], MIDDLE)
    d_left_here, d_left_there = call(
        functools.partial(left_kernel, 1, True),
        [(rows, cols, chans)] * 2,
        (place, rights[2], d_x[2], d_left_here, d_left_there),
    )
    far, d_left_here = lax.optimization_barrier((far, d_left_here))
    tile(3, middle, far)
    from_far = along(d_right[3], ENDS)
    d_left_kept, d_left_sent = call(
        last_left_kernel,
        [(rows, cols, chans), (rows + 2, cols, chans)],
        (place, rights[3], d_x[3], d_left_here, d_left_there, out_there[2], out_there[3]),
    )
    to_middle, to_near, early_far, d_left_sent = lax.optimization_barrier(
        (d_right[3] + inward, d_right[1] + swapped, early_far, d_left_sent)
    )
    received = other_core(d_left_sent)
    d_left, packed, rest = call(
        share_kernel,
        [kept, kept, (4, cols, chans)],
        (place, d_left_kept, received, out_here[2], out_here[3]),
    )
    d_left_other = other_half(packed)
    to_near, to_middle, _ = lax.optimization_barrier((to_near, to_middle, packed))
    from_near = along(to_near, NEXT)
    from_middle = along(to_middle, MIDDLE)
    rest, from_far = lax.optimization_barrier((rest, from_far))
    rest_other = other_half(rest)
    outs = (*out_here, early_other, early_far, received, rest_other)
    (base,) = call(
        functools.partial(base_kernel, rows),
        [(half, cols, width)],
        (place, *outs, gate, cotangent, w_gate, d_left, d_left_other, open_left, slope_left, mine, other),
        scratch=[(half, cols, width)],
    )
    d_mine, d_pair = call(
        functools.partial(pair_kernel, rows),
        [(half, cols, width), (rows, cols, width)],
        (place, normed, scale, base, d_right[0], from_near, from_middle, from_far, open_right, slope_right, mine, other),
    )
    d_other = other_half(d_mine)
    _, gate_late = lax.optimization_barrier((d_mine, gate))
    (update,) = call(
        functools.partial(update_kernel, rows),
        [(rows, cols, width)],
        (place, *outs, gate_late),
        scratch=[(rows, cols, width)],
    )
    d_other, update = lax.optimization_barrier((d_other, update))
    d_pair = join(place, d_other, d_pair)
    return (update, d_pair)


def passed_along(block, axis, distance):
    devices = range(lax.axis_size(axis))
    route = [((i - distance) % len(devices), i) for i in devices]
    return lax.ppermute(block, axis, route)


def normalize(values):
    mean = jnp.mean(values, axis=-1, keepdims=True)
    centered = values - mean
    variance = jnp.mean(centered * centered, axis=-1, keepdims=True)
    scale = lax.rsqrt(variance + 1e-05)
    return (centered * scale, scale)


def on_ring(pair, pair_mask, w_proj, w_gate, w_out, cotangent):
    highest = lax.Precision.HIGHEST
    normed, pair_scale = normalize(pair)
    proj = jnp.einsum("rqz,pzc->pcrq", normed, w_proj, precision=highest)
    keep = pair_mask.astype(jnp.float32)
    sig_left = jax.nn.sigmoid(proj[1])
    sig_right = jax.nn.sigmoid(proj[3])
    left = keep * sig_left * proj[0]
    right = keep * sig_right * proj[2]
    chans, rows, cols = left.shape
    count = lax.axis_size("row")
    here = lax.axis_index("row")

    def visit(step, carry):
        block, store, partial_value = carry
        source = (here - step) % count
        store = lax.dynamic_update_slice_in_dim(store, block, source * rows, 1)
        product = jnp.einsum("cik,cjk->cij", left, block, precision=highest)
        partial_value = lax.dynamic_update_slice_in_dim(partial_value, product, source * rows, 2)
        block = passed_along(block, "row", 1)
        return (block, store, partial_value)

    store = jnp.zeros((chans, rows * count, cols), jnp.float32)
    partial_value = jnp.zeros((chans, rows, rows * count), jnp.float32)
    block, store, partial_value = lax.fori_loop(0, count - 1, visit, (right, store, partial_value))
    source = (here + 1) % count
    right_all = lax.dynamic_update_slice_in_dim(store, block, source * rows, 1)
    product = jnp.einsum("cik,cjk->cij", left, block, precision=highest)
    partial_value = lax.dynamic_update_slice_in_dim(partial_value, product, source * rows, 2)
    mixed = lax.psum_scatter(partial_value, "sub", scatter_dimension=2, tiled=True)
    first = jnp.sum(mixed, axis=0)
    second = jnp.sum(mixed * mixed, axis=0)
    projected = jnp.einsum("crq,cd->rqd", mixed, w_out, precision=highest)
    col_total = jnp.sum(w_out, axis=0)
    projected, first, second, col_total = lax.psum((projected, first, second, col_total), "ch")
    center = first / C
    spread = lax.rsqrt(second / C - center * center + 1e-05)
    outgoing = (projected - center[..., None] * col_total) * spread[..., None]
    gate = jax.nn.sigmoid(jnp.einsum("rqz,zd->rqd", normed, w_gate, precision=highest))
    update = gate * outgoing
    d_outgoing = cotangent * gate
    d_gate_pre = cotangent * outgoing * gate * (1.0 - gate)
    d_mixed_norm = jnp.einsum("rqd,cd->crq", d_outgoing, w_out, precision=highest)
    mean_one = jnp.sum(d_outgoing * col_total, axis=-1) / C
    mean_two = jnp.sum(d_outgoing * outgoing, axis=-1) / C
    mixed_norm = (mixed - center) * spread
    d_mixed = (d_mixed_norm - mean_one - mixed_norm * mean_two) * spread
    d_mixed_full = lax.all_gather(d_mixed, "sub", axis=2, tiled=True)
    d_left = jnp.einsum("cij,cjk->cik", d_mixed_full, right_all, precision=highest)
    d_right = jnp.transpose(
        lax.psum_scatter(
            jnp.einsum("cij,cik->jck", d_mixed_full, left, precision=highest),
            "row",
            scatter_dimension=0,
            tiled=True,
        ),
        (1, 0, 2),
    )
    d_proj = jnp.stack(
        [
            d_left * keep * sig_left,
            d_left * keep * proj[0] * sig_left * (1.0 - sig_left),
            d_right * keep * sig_right,
            d_right * keep * proj[2] * sig_right * (1.0 - sig_right),
        ]
    )
    d_normed_part = jnp.einsum("pcrq,pzc->rqz", d_proj, w_proj, precision=highest)
    d_normed = lax.psum(d_normed_part, "ch")
    d_normed = d_normed + jnp.einsum("rqd,zd->rqz", d_gate_pre, w_gate, precision=highest)
    mean_grad = jnp.mean(d_normed, axis=-1, keepdims=True)
    mean_cross = jnp.mean(d_normed * normed, axis=-1, keepdims=True)
    d_pair = (d_normed - mean_grad - normed * mean_cross) * pair_scale
    return (update, d_pair)


def solution(mesh):
    sizes = mesh.shape
    tiled = sizes["row"] == 8 and sizes["ch"] == 2 and sizes["sub"] == 1
    return jax.shard_map(
        on_tiles if tiled else on_ring,
        mesh=mesh,
        in_specs=(
            P(("grp", "row"), "sub", None),
            P(("grp", "row"), "sub"),
            P(None, None, "ch"),
            P(),
            P("ch", None),
            P(("grp", "row"), "sub", None),
        ),
        out_specs=(P(("grp", "row"), "sub", None), P(("grp", "row"), "sub", None)),
        check_vma=False,
    )
```

```python
import functools
import jax
import jax.numpy as jnp
from jax import lax
from jax.experimental import pallas as pl
from jax.experimental.pallas import tpu as pltpu
from jax.sharding import PartitionSpec as P

C = 128
EPS = 1e-05
HIGHEST = lax.Precision.HIGHEST
F32 = jnp.float32
CHUNK = 4
GROUP = 8


def halves(values):
    high = values.astype(jnp.bfloat16)
    return high, (values - high.astype(F32)).astype(jnp.bfloat16)


def contract(a, b, dims):
    (a_high, a_low), (b_high, b_low) = halves(a), halves(b)
    one = lambda x, y: lax.dot_general(x, y, (dims, ((), ())), preferred_element_type=F32)
    return one(a_high, b_high) + (one(a_high, b_low) + one(a_low, b_high))


def dot(a, b):
    return contract(a, b, ((1,), (0,)))


def dot_t(a, b):
    return contract(a, b, ((1,), (1,)))


def norm(values):
    mean = jnp.mean(values, axis=-1, keepdims=True)
    centered = values - mean
    variance = jnp.mean(centered * centered, axis=-1, keepdims=True)
    scale = lax.rsqrt(variance + EPS)
    return (centered * scale, scale)


def flat(values):
    return values.reshape(-1, values.shape[-1])


def call(kernel, outs, args, scratch=(), distant=0, sems=0):
    vmem = pl.BlockSpec(memory_space=pltpu.VMEM)
    spaces = [pl.BlockSpec(memory_space=pltpu.SMEM)] + [pl.BlockSpec(memory_space=pltpu.HBM)] * distant
    args = list(args)
    args[1 : 1 + distant] = [pltpu.with_memory_space_constraint(a, pltpu.HBM) for a in args[1 : 1 + distant]]
    return pl.pallas_call(
        kernel,
        out_shape=[jax.ShapeDtypeStruct(shape, F32) for shape in outs],
        in_specs=spaces + [vmem] * (len(args) - len(spaces)),
        out_specs=[vmem] * len(outs),
        scratch_shapes=[pltpu.VMEM(*shape) if isinstance(shape[0], tuple) else pltpu.VMEM(shape, F32) for shape in scratch]
        + ([pltpu.SemaphoreType.DMA((sems,))] if sems else []),
        compiler_params=pltpu.CompilerParams(vmem_limit_bytes=24 * 1024 * 1024),
        cost_estimate=pl.CostEstimate(flops=1000, bytes_accessed=1000, transcendentals=0),
    )(*args)


def source_row(place, t, rows):
    half = rows // 2
    if t < half:
        return place[2] * half + t
    return (1 - place[2]) * half + t - half


def first_col(place, chip, core, rows):
    half = rows // 2
    return pl.multiple_of(chip * 2 * rows + core * rows + place[2] * half, half)


def both_halves(place, mine, other):
    first = place[2] == 0
    a, b = jnp.where(first, mine, other), jnp.where(first, other, mine)
    return jnp.concatenate([a, b], axis=0)


def gated_weights(place, mine, other, which):
    return jnp.concatenate([both_halves(place, mine[p], other[p]) for p in (which, which + 1)], axis=0)


def gated(normed, keep_rows, w):
    count, cols = keep_rows.shape
    chans = w.shape[0] // 2
    spread = jnp.transpose(jnp.concatenate([keep_rows] * (8 // count), axis=0))
    keep = jnp.concatenate([spread[:, u : u + 1] for u in range(count)], axis=0)
    proj = dot_t(normed, w)
    sig = jax.nn.sigmoid(proj[:, chans:]) * keep
    return sig * proj[:, :chans], sig


def first_kernel(place, pair, mask, w_proj, normed, scale, keep, mine, first, second, flags, sems):
    half = first.shape[0]
    moves = ((pair.at[:half], first), (pair.at[half:], second), (mask, flags), (w_proj, mine))
    copies = [pltpu.make_async_copy(source, target, sems.at[at]) for at, (source, target) in enumerate(moves)]
    for copy in copies:
        copy.start()
    for copy in copies:
        copy.wait()
    keep[...] = flags[...].astype(F32)
    for t in range(0, half, CHUNK):
        at = slice(t, t + CHUNK)
        value, factor = norm(jnp.where(place[2] == 0, first[at], second[at]))
        normed[at] = value
        scale[at] = jnp.broadcast_to(factor, value.shape)


def third_kernel(place, cotangent, keep, packed, sems):
    rows = cotangent.shape[0]
    half, chips = rows // 2, packed.shape[0] - 1
    copies = []
    for chip in range(chips):
        source = cotangent.at[:, pl.ds(first_col(place, chip, 1 - place[1], rows), half), :]
        copies.append(pltpu.make_async_copy(source, packed.at[chip], sems.at[chip]))
    for copy in copies:
        copy.start()
    packed[chips, :, 0, :] = keep[...]
    for copy in copies:
        copy.wait()


def right_kernel(rows, place, normed, keep, mine, other, right, open_part, slope):
    half, cols, chans = right.shape
    w = gated_weights(place, mine, other, 2)
    for t in range(0, half, CHUNK):
        at = slice(t, t + CHUNK)
        value, sig = gated(flat(normed[at]), keep[pl.ds(source_row(place, t, rows), CHUNK), :], w)
        shape = (CHUNK, cols, chans)
        right[at] = value.reshape(shape)
        open_part[at] = sig.reshape(shape)
        slope[at] = (value * (1.0 - sig)).reshape(shape)


def prepare_kernel(rows, place, pair, keep, cotangent, first, second, third, mine, other, w_gate, mine_out, other_out, *refs):
    left_here, left_there, open_part, slope, gate, d_here, d_there, w_out, normed_rows = refs
    half, cols, chans = open_part.shape
    chips = cols // (2 * rows)
    shape = (CHUNK, cols, chans)
    w = gated_weights(place, mine, other, 0)
    w_out[...] = both_halves(place, mine_out[...], other_out[...])
    for t in range(0, rows, CHUNK):
        row = source_row(place, t, rows)
        at = slice(t, t + CHUNK)
        normed, _ = norm(flat(pair[pl.ds(row, CHUNK)]))
        value, sig = gated(normed, keep[pl.ds(row, CHUNK), :], w)
        left_here[at] = value.reshape(shape)
        if t < half:
            open_part[at] = sig.reshape(shape)
            slope[at] = (value * (1.0 - sig)).reshape(shape)
        gate[at] = jax.nn.sigmoid(dot(normed, w_gate[...])).reshape(CHUNK, cols, -1)
        for chip in range(chips):
            near = pl.ds(first_col(place, chip, place[1], rows), half)
            d_here[chip, at] = gate[at, near, :] * cotangent[pl.ds(row, CHUNK), near, :]
        their_row = row % half
        normed, _ = norm(flat(jnp.where(row < half, first[pl.ds(their_row, CHUNK)], second[pl.ds(their_row, CHUNK)])))
        value, _ = gated(normed, third[chips, pl.ds(row, CHUNK), 0, :], w)
        left_there[at] = value.reshape(shape)
        normed_rows[...] = normed.reshape(CHUNK, cols, -1)
        picked = [
            normed_rows[:, pl.ds(first_col(place, chip, place[1], rows), half), :] for chip in range(chips)
        ]
        opened = jax.nn.sigmoid(dot(flat(jnp.stack(picked)), w_gate[...])).reshape(chips, CHUNK, half, -1)
        for chip in range(chips):
            d_there[chip, at] = opened[chip] * third[chip, pl.ds(row, CHUNK)]


def tile_body(step, place, right, left_here, left_there, d_here, d_there, w_out, out_here, out_there, d_x, d_right, partial, x):
    rows = left_here.shape[0]
    half, cols, chans = right.shape
    groups = cols // GROUP

    def forward(pair_at, _):
        for which, left in enumerate((left_here, left_there)):
            i = pair_at * 2
            value = [left[i], left[i + 1]]
            for j in range(half):
                block = right[j]
                for u in range(2):
                    product = (value[u] * block).reshape(groups, GROUP, chans)
                    partial[2 * which + u, j * GROUP : (j + 1) * GROUP] = jnp.sum(product, axis=0)
            for u in range(2):
                total = partial[2 * which + u, pl.ds(0, half, stride=GROUP), :]
                for s in range(1, GROUP):
                    total = total + partial[2 * which + u, pl.ds(s, half, stride=GROUP), :]
                x[pl.ds(pl.multiple_of((which * rows + i + u) * half, half), half), :] = total
        return 0

    lax.fori_loop(0, rows // 2, forward, 0)
    chip = jnp.bitwise_xor(place[0], step)
    d_out = jnp.concatenate([flat(d_here[chip]), flat(d_there[chip])], axis=0)
    normed, scale = norm(x[...])
    out = dot(normed, w_out[...])
    out_here[...] = out[: rows * half].reshape(rows, half, -1)
    out_there[...] = out[rows * half :].reshape(rows, half, -1)
    d_normed = dot_t(d_out, w_out[...])
    mean_one = jnp.mean(d_normed, axis=-1, keepdims=True)
    mean_two = jnp.mean(d_normed * normed, axis=-1, keepdims=True)
    d_x[...] = (d_normed - mean_one - normed * mean_two) * scale
    wide = 2 * GROUP

    def backward(at, _):
        here = pl.ds(pl.multiple_of(at * wide, wide), wide)

        def add(block, totals):
            totals = list(totals)
            for u in range(GROUP):
                for which, left in enumerate((left_here, left_there)):
                    i = block * GROUP + u
                    value = left[i, here, :]
                    for j in range(half):
                        totals[j] = totals[j] + value * d_x[pl.ds((which * rows + i) * half + j, 1), :]
            return tuple(totals)

        totals = lax.fori_loop(0, rows // GROUP, add, (jnp.zeros((wide, chans), F32),) * half)
        for j in range(half):
            d_right[j, here, :] = totals[j]
        return 0

    lax.fori_loop(0, cols // wide, backward, 0)


def tile_kernel(step, parts, place, *refs):
    rights, rest = refs[:parts], refs[parts:]
    if parts == 2:
        sum_out = rest[9]
        sum_out[...] = rights[0][...] + rights[1][...]
        tile_body(step, place, sum_out, *rest[:9], *rest[10:])
    else:
        tile_body(step, place, rights[0], *rest)


def left_rows(tiles, base, out, first, count, start):
    half, cols, chans = tiles[0][0].shape

    def body(pair_at, _):
        i = pair_at * 2
        totals = [jnp.zeros((cols, chans), F32)] * 2 if base is None else [base[start + i], base[start + i + 1]]
        for right, d_x in tiles:
            for j in range(half):
                value = right[j]
                for u in range(2):
                    totals[u] = totals[u] + value * d_x[pl.ds((first + i + u) * half + j, 1), :]
        out[start + i] = totals[0]
        out[start + i + 1] = totals[1]
        return 0

    lax.fori_loop(0, count // 2, body, 0)


def left_kernel(tiles, based, place, *refs):
    pairs = tuple(zip(refs[:tiles], refs[tiles : 2 * tiles]))
    bases = refs[2 * tiles : 2 * tiles + 2] if based else (None, None)
    rows = refs[-1].shape[0]
    for which, out in enumerate(refs[-2:]):
        left_rows(pairs, bases[which], out, which * rows, rows, 0)


def last_sent_kernel(place, right, d_x, there, out_next, out_last, sent):
    rows = there.shape[0]
    left_rows(((right, d_x),), there, sent, rows, rows, 0)
    sent[rows] = flat(out_next[...])
    sent[rows + 1] = flat(out_last[...])


def last_kept_kernel(place, right, d_x, here, kept):
    left_rows(((right, d_x),), here, kept, 0, here.shape[0], 0)


def share_kernel(place, kept, received, out_next, out_last, d_left, packed, rest):
    half = d_left.shape[0]
    block = half * half
    d_left[...] = kept[:half] + received[:half]
    packed[...] = kept[half:] + received[half : 2 * half]
    for step, out in enumerate((out_next, out_last)):
        at = slice(step * block, (step + 1) * block)
        plane = 2 * half + step
        rest[0, at] = flat(out[half:])
        rest[1, at] = received[plane, block:]
        rest[2, at] = flat(out[:half])
        rest[3, at] = received[plane, :block]


def gather_out(place, rows, t, out, here, early_other, early_far, received, far):
    half = rows // 2
    block = half * half
    for far_half in (0, 1):
        source = (t + far_half * half) % rows
        at, wide = slice(source, source + half), slice(source * half, source * half + block)
        for far_core in (0, 1):
            core = place[1] + far_core * (1 - 2 * place[1])
            side = place[2] + far_half * (1 - 2 * place[2])
            for step in range(4):
                chip = jnp.bitwise_xor(place[0], step)
                first = pl.multiple_of(chip * 2 * rows + core * rows + side * half, half)
                if far_half:
                    if step < 2:
                        value = early_far[far_core, step, at]
                    else:
                        ref, plane = far[far_core]
                        value = ref[plane, (step - 2) * block : (step - 1) * block].reshape(half, half, -1)
                elif far_core:
                    if step < 2:
                        value = early_other[step, at]
                    else:
                        value = received[rows + step - 2, wide].reshape(half, half, -1)
                else:
                    value = here[step][at]
                out[t : t + half, pl.ds(first, half), :] = value


def update_kernel(rows, place, *refs):
    here, early_other, early_far, received, rest, gate, update, out = refs[:4], *refs[4:]
    half = rows // 2
    gather_out(place, rows, 0, out, here, early_other, early_far, received, ((rest, 0), (rest, 1)))
    gather_out(place, rows, half, out, here, early_other, early_far, received, ((rest, 2), (rest, 3)))
    for t in range(0, rows, CHUNK):
        update[pl.ds(source_row(place, t, rows), CHUNK)] = gate[t : t + CHUNK] * out[t : t + CHUNK]


def base_kernel(rows, place, *refs):
    here, early_other, early_far, received, rest = refs[:4], *refs[4:8]
    gate, cotangent, w_gate, d_left, far, open_part, slope, mine, other, base, out = refs[8:]
    half, cols, chans = base.shape
    gather_out(place, rows, 0, out, here, early_other, early_far, received, ((rest, 0), (rest, 1)))
    w = gated_weights(place, mine, other, 0)
    for t in range(0, half, CHUNK):
        at = slice(t, t + CHUNK)
        opened = gate[at]
        d_gate = cotangent[pl.ds(source_row(place, t, rows), CHUNK)] * (opened * out[at]) * (1.0 - opened)
        grad = flat(d_left[at] + far[at])
        both = jnp.concatenate([grad * flat(open_part[at]), grad * flat(slope[at])], axis=1)
        base[at] = (dot_t(flat(d_gate), w_gate[...]) + dot(both, w)).reshape(CHUNK, cols, -1)


def pair_kernel(first, place, normed, scale, base, d_right, d_right_near, d_right_middle, d_right_far, open_part, slope, mine, other, d_mine):
    count, cols, chans = d_mine.shape
    w = gated_weights(place, mine, other, 2)
    at = slice(first, first + count)
    grad = flat(d_right[at] + d_right_near[at] + (d_right_middle[at] + d_right_far[at]))
    both = jnp.concatenate([grad * flat(open_part[at]), grad * flat(slope[at])], axis=1)
    d_normed = flat(base[at]) + dot(both, w)
    value = flat(normed[at])
    mean_grad = jnp.mean(d_normed, axis=-1, keepdims=True)
    mean_cross = jnp.mean(d_normed * value, axis=-1, keepdims=True)
    d_mine[...] = ((d_normed - mean_grad - value * mean_cross) * flat(scale[at])).reshape(count, cols, -1)


def join_kernel(firsts, sides, *refs):
    blocks, whole, sems = refs[: len(firsts)], refs[-2], refs[-1]
    side = lax.axis_index("ch")
    half = whole.shape[0] // 2
    copies = []
    for at, (block, first, mine) in enumerate(zip(blocks, firsts, sides)):
        start = (side if mine else 1 - side) * half + first
        copies.append(pltpu.make_async_copy(block, whole.at[pl.ds(start, block.shape[0])], sems.at[at]))
    for copy in copies:
        copy.start()
    for copy in copies:
        copy.wait()


def join(blocks, firsts, sides, shape, whole=None):
    anywhere = pl.BlockSpec(memory_space=pl.ANY)
    vmem = pl.BlockSpec(memory_space=pltpu.VMEM)
    given = [] if whole is None else [whole]
    return pl.pallas_call(
        functools.partial(join_kernel, firsts, sides),
        out_shape=jax.ShapeDtypeStruct(shape, F32),
        in_specs=[vmem] * len(blocks) + [anywhere] * len(given),
        out_specs=anywhere,
        input_output_aliases={len(blocks): 0} if given else {},
        scratch_shapes=[pltpu.SemaphoreType.DMA((len(blocks),))],
        compiler_params=pltpu.CompilerParams(vmem_limit_bytes=2 * 1024 * 1024),
    )(*blocks, *given)


def along(block, pairs):
    return lax.ppermute(block, "row", [(2 * a + core, 2 * b + core) for a, b in pairs for core in (0, 1)])


def other_core(block):
    return lax.ppermute(block, "row", [(i, i ^ 1) for i in range(lax.axis_size("row"))])


def other_half(block):
    return lax.ppermute(block, "ch", [(0, 1), (1, 0)])


NEXT = [(0, 1), (1, 0), (2, 3), (3, 2)]
MIDDLE = [(1, 2), (2, 1)]
OUTWARD = [(1, 0), (2, 3)]
INWARD = [(0, 1), (3, 2)]
ENDS = [(0, 3), (3, 0)]


def on_tiles(pair, pair_mask, w_proj, w_gate, w_out, cotangent):
    rows, cols, width = pair.shape
    half = rows // 2
    chips = cols // (2 * rows)
    chans = 2 * w_out.shape[0]
    row, side = lax.axis_index("row"), lax.axis_index("ch")
    place = jnp.stack([row // 2, row % 2, side]).astype(jnp.int32)

    w_mine = jnp.swapaxes(w_proj, 1, 2)
    other = other_half(flat(w_mine)).reshape(w_mine.shape)
    kept = (half, cols, chans)
    other_out = other_half(w_out)
    normed, scale, keep, mine, *sent = call(
        first_kernel,
        [(half, cols, width)] * 2 + [(rows, cols), w_mine.shape] + [(half, cols, width)] * 2,
        (place, pair, pair_mask, w_mine),
        scratch=[((rows, cols), jnp.int32)],
        distant=3,
        sems=4,
    )
    theirs = [other_core(block) for block in sent]
    other, other_out = lax.optimization_barrier((other, other_out))
    right, open_right, slope_right = call(
        functools.partial(right_kernel, rows), [kept] * 3, (place, normed, keep, mine, other)
    )
    near = along(right, NEXT)
    middle = along(right, MIDDLE)
    _, cotangent_late = lax.optimization_barrier((right, cotangent))
    (third,) = call(
        third_kernel, [(chips + 1, rows, half, width)], (place, cotangent_late, keep), distant=1, sems=chips
    )
    theirs.append(other_core(third))
    quarter = (chips, rows, half, width)
    tile_outs = [(rows, half, width)] * 2 + [(2 * rows * half, chans), kept]
    tile_scratch = [(4, half * GROUP, chans), (2 * rows * half, chans)]
    out_here, out_there, d_x, d_right, rights = ([None] * 4 for _ in range(5))
    rights[0] = right
    left, left_there, open_left, slope_left, gate, d_here, d_there, w_all_out = call(
        functools.partial(prepare_kernel, rows),
        [(rows, cols, chans)] * 2 + [kept] * 2 + [(rows, cols, width), quarter, quarter, (chans, width)],
        (place, pair, keep, cotangent, *theirs, mine, other, w_gate, w_out, other_out),
        scratch=[(CHUNK, cols, width)],
    )

    def tile(step, *blocks):
        got = call(
            functools.partial(tile_kernel, step, len(blocks)),
            tile_outs + ([kept] if len(blocks) == 2 else []),
            (place, *blocks, left, left_there, d_here, d_there, w_all_out),
            scratch=tile_scratch,
        )
        out_here[step], out_there[step], d_x[step], d_right[step] = got[:4]
        rights[step] = got[4] if len(blocks) == 2 else blocks[0]

    near, d_here = lax.optimization_barrier((near, d_here))
    cross = along(near, MIDDLE)
    outer = along(middle, OUTWARD)
    tile(0, right)
    tile(1, near)
    early_other = other_core(jnp.stack(out_there[:2]))
    d_left_here, d_left_there = call(
        functools.partial(left_kernel, 2, False),
        [(rows, cols, chans)] * 2,
        (place, *rights[:2], *d_x[:2]),
    )
    cross, early_other, d_left_here = lax.optimization_barrier((cross, early_other, d_left_here))
    far = along(cross, OUTWARD)
    early_far = other_half(jnp.stack([jnp.stack(out_here[:2]), early_other]))
    tile(2, cross, outer)
    inward = along(d_right[2], INWARD)
    swapped = along(d_right[2], MIDDLE)
    d_left_here, d_left_there = call(
        functools.partial(left_kernel, 1, True),
        [(rows, cols, chans)] * 2,
        (place, rights[2], d_x[2], d_left_here, d_left_there),
    )
    far, d_left_here = lax.optimization_barrier((far, d_left_here))
    tile(3, middle, far)
    from_far = along(d_right[3], ENDS)
    (d_left_sent,) = call(
        last_sent_kernel,
        [(rows + 2, cols, chans)],
        (place, rights[3], d_x[3], d_left_there, out_there[2], out_there[3]),
    )
    to_middle, to_near, early_far, d_left_sent = lax.optimization_barrier(
        (d_right[3] + inward, d_right[1] + swapped, early_far, d_left_sent)
    )
    received = other_core(d_left_sent)
    _, d_left_here = lax.optimization_barrier((d_left_sent, d_left_here))
    (d_left_kept,) = call(last_kept_kernel, [(rows, cols, chans)], (place, rights[3], d_x[3], d_left_here))
    d_left, packed, rest = call(
        share_kernel,
        [kept, kept, (4, cols, chans)],
        (place, d_left_kept, received, out_here[2], out_here[3]),
    )
    d_left_other = other_half(packed)
    to_near, to_middle, _ = lax.optimization_barrier((to_near, to_middle, packed))
    from_near = along(to_near, NEXT)
    from_middle = along(to_middle, MIDDLE)
    rest, from_far = lax.optimization_barrier((rest, from_far))
    rest_other = other_half(rest)
    outs = (*out_here, early_other, early_far, received, rest_other)
    (base,) = call(
        functools.partial(base_kernel, rows),
        [(half, cols, width)],
        (place, *outs, gate, cotangent, w_gate, d_left, d_left_other, open_left, slope_left, mine, other),
        scratch=[(half, cols, width)],
    )
    cut = (5 * half) // 8
    mine_parts, other_parts = [], []
    for first, last in ((0, cut), (cut, half)):
        (part,) = call(
            functools.partial(pair_kernel, first),
            [(last - first, cols, width)],
            (place, normed, scale, base, d_right[0], from_near, from_middle, from_far, open_right, slope_right, mine, other),
        )
        mine_parts.append(part)
        other_parts.append(other_half(part))
    _, gate_late = lax.optimization_barrier((mine_parts[1], gate))
    (update,) = call(
        functools.partial(update_kernel, rows),
        [(rows, cols, width)],
        (place, *outs, gate_late),
        scratch=[(rows, cols, width)],
    )
    firsts = (0, cut)
    d_pair = join(mine_parts, firsts, (True, True), pair.shape)
    other_parts[0], update, d_pair = lax.optimization_barrier((other_parts[0], update, d_pair))
    d_pair = join(other_parts[:1], firsts[:1], (False,), pair.shape, d_pair)
    other_parts[1], d_pair = lax.optimization_barrier((other_parts[1], d_pair))
    d_pair = join(other_parts[1:], firsts[1:], (False,), pair.shape, d_pair)
    return (update, d_pair)


def passed_along(block, axis, distance):
    devices = range(lax.axis_size(axis))
    route = [((i - distance) % len(devices), i) for i in devices]
    return lax.ppermute(block, axis, route)


def normalize(values):
    mean = jnp.mean(values, axis=-1, keepdims=True)
    centered = values - mean
    variance = jnp.mean(centered * centered, axis=-1, keepdims=True)
    scale = lax.rsqrt(variance + 1e-05)
    return (centered * scale, scale)


def on_ring(pair, pair_mask, w_proj, w_gate, w_out, cotangent):
    highest = lax.Precision.HIGHEST
    normed, pair_scale = normalize(pair)
    proj = jnp.einsum("rqz,pzc->pcrq", normed, w_proj, precision=highest)
    keep = pair_mask.astype(jnp.float32)
    sig_left = jax.nn.sigmoid(proj[1])
    sig_right = jax.nn.sigmoid(proj[3])
    left = keep * sig_left * proj[0]
    right = keep * sig_right * proj[2]
    chans, rows, cols = left.shape
    count = lax.axis_size("row")
    here = lax.axis_index("row")

    def visit(step, carry):
        block, store, partial_value = carry
        source = (here - step) % count
        store = lax.dynamic_update_slice_in_dim(store, block, source * rows, 1)
        product = jnp.einsum("cik,cjk->cij", left, block, precision=highest)
        partial_value = lax.dynamic_update_slice_in_dim(partial_value, product, source * rows, 2)
        block = passed_along(block, "row", 1)
        return (block, store, partial_value)

    store = jnp.zeros((chans, rows * count, cols), jnp.float32)
    partial_value = jnp.zeros((chans, rows, rows * count), jnp.float32)
    block, store, partial_value = lax.fori_loop(0, count - 1, visit, (right, store, partial_value))
    source = (here + 1) % count
    right_all = lax.dynamic_update_slice_in_dim(store, block, source * rows, 1)
    product = jnp.einsum("cik,cjk->cij", left, block, precision=highest)
    partial_value = lax.dynamic_update_slice_in_dim(partial_value, product, source * rows, 2)
    mixed = lax.psum_scatter(partial_value, "sub", scatter_dimension=2, tiled=True)
    first = jnp.sum(mixed, axis=0)
    second = jnp.sum(mixed * mixed, axis=0)
    projected = jnp.einsum("crq,cd->rqd", mixed, w_out, precision=highest)
    col_total = jnp.sum(w_out, axis=0)
    projected, first, second, col_total = lax.psum((projected, first, second, col_total), "ch")
    center = first / C
    spread = lax.rsqrt(second / C - center * center + 1e-05)
    outgoing = (projected - center[..., None] * col_total) * spread[..., None]
    gate = jax.nn.sigmoid(jnp.einsum("rqz,zd->rqd", normed, w_gate, precision=highest))
    update = gate * outgoing
    d_outgoing = cotangent * gate
    d_gate_pre = cotangent * outgoing * gate * (1.0 - gate)
    d_mixed_norm = jnp.einsum("rqd,cd->crq", d_outgoing, w_out, precision=highest)
    mean_one = jnp.sum(d_outgoing * col_total, axis=-1) / C
    mean_two = jnp.sum(d_outgoing * outgoing, axis=-1) / C
    mixed_norm = (mixed - center) * spread
    d_mixed = (d_mixed_norm - mean_one - mixed_norm * mean_two) * spread
    d_mixed_full = lax.all_gather(d_mixed, "sub", axis=2, tiled=True)
    d_left = jnp.einsum("cij,cjk->cik", d_mixed_full, right_all, precision=highest)
    d_right = jnp.transpose(
        lax.psum_scatter(
            jnp.einsum("cij,cik->jck", d_mixed_full, left, precision=highest),
            "row",
            scatter_dimension=0,
            tiled=True,
        ),
        (1, 0, 2),
    )
    d_proj = jnp.stack(
        [
            d_left * keep * sig_left,
            d_left * keep * proj[0] * sig_left * (1.0 - sig_left),
            d_right * keep * sig_right,
            d_right * keep * proj[2] * sig_right * (1.0 - sig_right),
        ]
    )
    d_normed_part = jnp.einsum("pcrq,pzc->rqz", d_proj, w_proj, precision=highest)
    d_normed = lax.psum(d_normed_part, "ch")
    d_normed = d_normed + jnp.einsum("rqd,zd->rqz", d_gate_pre, w_gate, precision=highest)
    mean_grad = jnp.mean(d_normed, axis=-1, keepdims=True)
    mean_cross = jnp.mean(d_normed * normed, axis=-1, keepdims=True)
    d_pair = (d_normed - mean_grad - normed * mean_cross) * pair_scale
    return (update, d_pair)


def solution(mesh):
    sizes = mesh.shape
    tiled = sizes["row"] == 8 and sizes["ch"] == 2 and sizes["sub"] == 1
    return jax.shard_map(
        on_tiles if tiled else on_ring,
        mesh=mesh,
        in_specs=(
            P(("grp", "row"), "sub", None),
            P(("grp", "row"), "sub"),
            P(None, None, "ch"),
            P(),
            P("ch", None),
            P(("grp", "row"), "sub", None),
        ),
        out_specs=(P(("grp", "row"), "sub", None), P(("grp", "row"), "sub", None)),
        check_vma=False,
    )
```

```python
import functools
import jax
import jax.numpy as jnp
from jax import lax
from jax.experimental import pallas as pl
from jax.experimental.pallas import tpu as pltpu
from jax.sharding import PartitionSpec as P

C = 128
EPS = 1e-05
HIGHEST = lax.Precision.HIGHEST
F32 = jnp.float32
CHUNK = 4
GROUP = 8


def halves(values):
    high = values.astype(jnp.bfloat16)
    return high, (values - high.astype(F32)).astype(jnp.bfloat16)


def contract(a, b, dims):
    (a_high, a_low), (b_high, b_low) = halves(a), halves(b)
    one = lambda x, y: lax.dot_general(x, y, (dims, ((), ())), preferred_element_type=F32)
    return one(a_high, b_high) + (one(a_high, b_low) + one(a_low, b_high))


def dot(a, b):
    return contract(a, b, ((1,), (0,)))


def dot_t(a, b):
    return contract(a, b, ((1,), (1,)))


def norm(values):
    mean = jnp.mean(values, axis=-1, keepdims=True)
    centered = values - mean
    variance = jnp.mean(centered * centered, axis=-1, keepdims=True)
    scale = lax.rsqrt(variance + EPS)
    return (centered * scale, scale)


def flat(values):
    return values.reshape(-1, values.shape[-1])


def call(kernel, outs, args, scratch=(), distant=0, sems=0):
    vmem = pl.BlockSpec(memory_space=pltpu.VMEM)
    spaces = [pl.BlockSpec(memory_space=pltpu.SMEM)] + [pl.BlockSpec(memory_space=pltpu.HBM)] * distant
    args = list(args)
    args[1 : 1 + distant] = [pltpu.with_memory_space_constraint(a, pltpu.HBM) for a in args[1 : 1 + distant]]
    return pl.pallas_call(
        kernel,
        out_shape=[jax.ShapeDtypeStruct(shape, F32) for shape in outs],
        in_specs=spaces + [vmem] * (len(args) - len(spaces)),
        out_specs=[vmem] * len(outs),
        scratch_shapes=[pltpu.VMEM(*shape) if isinstance(shape[0], tuple) else pltpu.VMEM(shape, F32) for shape in scratch]
        + ([pltpu.SemaphoreType.DMA((sems,))] if sems else []),
        compiler_params=pltpu.CompilerParams(vmem_limit_bytes=24 * 1024 * 1024),
        cost_estimate=pl.CostEstimate(flops=1000, bytes_accessed=1000, transcendentals=0),
    )(*args)


def source_row(place, t, rows):
    half = rows // 2
    if t < half:
        return place[2] * half + t
    return (1 - place[2]) * half + t - half


def first_col(place, chip, core, rows):
    half = rows // 2
    return pl.multiple_of(chip * 2 * rows + core * rows + place[2] * half, half)


def both_halves(place, mine, other):
    first = place[2] == 0
    a, b = jnp.where(first, mine, other), jnp.where(first, other, mine)
    return jnp.concatenate([a, b], axis=0)


def gated_weights(place, mine, other, which):
    return jnp.concatenate([both_halves(place, mine[p], other[p]) for p in (which, which + 1)], axis=0)


def gated(normed, keep_rows, w):
    count, cols = keep_rows.shape
    chans = w.shape[0] // 2
    spread = jnp.transpose(jnp.concatenate([keep_rows] * (8 // count), axis=0))
    keep = jnp.concatenate([spread[:, u : u + 1] for u in range(count)], axis=0)
    proj = dot_t(normed, w)
    sig = jax.nn.sigmoid(proj[:, chans:]) * keep
    return sig * proj[:, :chans], sig


def first_kernel(place, pair, mask, w_proj, normed, scale, keep, mine, first, second, flags, sems):
    half = first.shape[0]
    moves = ((pair.at[:half], first), (pair.at[half:], second), (mask, flags), (w_proj, mine))
    copies = [pltpu.make_async_copy(source, target, sems.at[at]) for at, (source, target) in enumerate(moves)]
    for copy in copies:
        copy.start()
    for copy in copies:
        copy.wait()
    keep[...] = flags[...].astype(F32)
    for t in range(0, half, CHUNK):
        at = slice(t, t + CHUNK)
        value, factor = norm(jnp.where(place[2] == 0, first[at], second[at]))
        normed[at] = value
        scale[at] = jnp.broadcast_to(factor, value.shape)


def third_kernel(place, cotangent, keep, packed, sems):
    rows = cotangent.shape[0]
    half, chips = rows // 2, packed.shape[0] - 1
    copies = []
    for chip in range(chips):
        source = cotangent.at[:, pl.ds(first_col(place, chip, 1 - place[1], rows), half), :]
        copies.append(pltpu.make_async_copy(source, packed.at[chip], sems.at[chip]))
    for copy in copies:
        copy.start()
    packed[chips, :, 0, :] = keep[...]
    for copy in copies:
        copy.wait()


def right_kernel(rows, place, normed, keep, mine, other, right, open_part, slope):
    half, cols, chans = right.shape
    w = gated_weights(place, mine, other, 2)
    for t in range(0, half, CHUNK):
        at = slice(t, t + CHUNK)
        value, sig = gated(flat(normed[at]), keep[pl.ds(source_row(place, t, rows), CHUNK), :], w)
        shape = (CHUNK, cols, chans)
        right[at] = value.reshape(shape)
        open_part[at] = sig.reshape(shape)
        slope[at] = (value * (1.0 - sig)).reshape(shape)


def prepare_kernel(rows, place, pair, keep, cotangent, first, second, third, mine, other, w_gate, mine_out, other_out, *refs):
    left_here, left_there, open_part, slope, gate, d_here, d_there, w_out, normed_rows = refs
    half, cols, chans = open_part.shape
    chips = cols // (2 * rows)
    shape = (CHUNK, cols, chans)
    w = gated_weights(place, mine, other, 0)
    w_out[...] = both_halves(place, mine_out[...], other_out[...])
    for t in range(0, rows, CHUNK):
        row = source_row(place, t, rows)
        at = slice(t, t + CHUNK)
        normed, _ = norm(flat(pair[pl.ds(row, CHUNK)]))
        value, sig = gated(normed, keep[pl.ds(row, CHUNK), :], w)
        left_here[at] = value.reshape(shape)
        if t < half:
            open_part[at] = sig.reshape(shape)
            slope[at] = (value * (1.0 - sig)).reshape(shape)
        gate[at] = jax.nn.sigmoid(dot(normed, w_gate[...])).reshape(CHUNK, cols, -1)
        for chip in range(chips):
            near = pl.ds(first_col(place, chip, place[1], rows), half)
            d_here[chip, at] = gate[at, near, :] * cotangent[pl.ds(row, CHUNK), near, :]
        their_row = row % half
        normed, _ = norm(flat(jnp.where(row < half, first[pl.ds(their_row, CHUNK)], second[pl.ds(their_row, CHUNK)])))
        value, _ = gated(normed, third[chips, pl.ds(row, CHUNK), 0, :], w)
        left_there[at] = value.reshape(shape)
        normed_rows[...] = normed.reshape(CHUNK, cols, -1)
        picked = [
            normed_rows[:, pl.ds(first_col(place, chip, place[1], rows), half), :] for chip in range(chips)
        ]
        opened = jax.nn.sigmoid(dot(flat(jnp.stack(picked)), w_gate[...])).reshape(chips, CHUNK, half, -1)
        for chip in range(chips):
            d_there[chip, at] = opened[chip] * third[chip, pl.ds(row, CHUNK)]


def tile_body(step, place, right, left_here, left_there, d_here, d_there, w_out, out_here, out_there, d_x, d_right, partial, x):
    rows = left_here.shape[0]
    half, cols, chans = right.shape
    groups = cols // GROUP

    def forward(pair_at, _):
        for which, left in enumerate((left_here, left_there)):
            i = pair_at * 2
            value = [left[i], left[i + 1]]
            for j in range(half):
                block = right[j]
                for u in range(2):
                    product = (value[u] * block).reshape(groups, GROUP, chans)
                    partial[2 * which + u, j * GROUP : (j + 1) * GROUP] = jnp.sum(product, axis=0)
            for u in range(2):
                total = partial[2 * which + u, pl.ds(0, half, stride=GROUP), :]
                for s in range(1, GROUP):
                    total = total + partial[2 * which + u, pl.ds(s, half, stride=GROUP), :]
                x[pl.ds(pl.multiple_of((which * rows + i + u) * half, half), half), :] = total
        return 0

    lax.fori_loop(0, rows // 2, forward, 0)
    chip = jnp.bitwise_xor(place[0], step)
    d_out = jnp.concatenate([flat(d_here[chip]), flat(d_there[chip])], axis=0)
    normed, scale = norm(x[...])
    out = dot(normed, w_out[...])
    out_here[...] = out[: rows * half].reshape(rows, half, -1)
    out_there[...] = out[rows * half :].reshape(rows, half, -1)
    d_normed = dot_t(d_out, w_out[...])
    mean_one = jnp.mean(d_normed, axis=-1, keepdims=True)
    mean_two = jnp.mean(d_normed * normed, axis=-1, keepdims=True)
    d_x[...] = (d_normed - mean_one - normed * mean_two) * scale
    wide = 2 * GROUP

    def backward(at, _):
        here = pl.ds(pl.multiple_of(at * wide, wide), wide)

        def add(block, totals):
            totals = list(totals)
            for u in range(GROUP):
                for which, left in enumerate((left_here, left_there)):
                    i = block * GROUP + u
                    value = left[i, here, :]
                    for j in range(half):
                        totals[j] = totals[j] + value * d_x[pl.ds((which * rows + i) * half + j, 1), :]
            return tuple(totals)

        totals = lax.fori_loop(0, rows // GROUP, add, (jnp.zeros((wide, chans), F32),) * half)
        for j in range(half):
            d_right[j, here, :] = totals[j]
        return 0

    lax.fori_loop(0, cols // wide, backward, 0)


def tile_kernel(step, parts, place, *refs):
    rights, rest = refs[:parts], refs[parts:]
    if parts == 2:
        sum_out = rest[9]
        sum_out[...] = rights[0][...] + rights[1][...]
        tile_body(step, place, sum_out, *rest[:9], *rest[10:])
    else:
        tile_body(step, place, rights[0], *rest)


def left_rows(tiles, base, out, first, count, start):
    half, cols, chans = tiles[0][0].shape

    def body(pair_at, _):
        i = pair_at * 2
        totals = [jnp.zeros((cols, chans), F32)] * 2 if base is None else [base[start + i], base[start + i + 1]]
        for right, d_x in tiles:
            for j in range(half):
                value = right[j]
                for u in range(2):
                    totals[u] = totals[u] + value * d_x[pl.ds((first + i + u) * half + j, 1), :]
        out[start + i] = totals[0]
        out[start + i + 1] = totals[1]
        return 0

    lax.fori_loop(0, count // 2, body, 0)


def left_kernel(tiles, based, place, *refs):
    pairs = tuple(zip(refs[:tiles], refs[tiles : 2 * tiles]))
    bases = refs[2 * tiles : 2 * tiles + 2] if based else (None, None)
    rows = refs[-1].shape[0]
    for which, out in enumerate(refs[-2:]):
        left_rows(pairs, bases[which], out, which * rows, rows, 0)


def last_sent_kernel(place, right, d_x, there, out_next, out_last, sent):
    rows = there.shape[0]
    left_rows(((right, d_x),), there, sent, rows, rows, 0)
    sent[rows] = flat(out_next[...])
    sent[rows + 1] = flat(out_last[...])


def last_kept_kernel(place, right, d_x, here, kept):
    left_rows(((right, d_x),), here, kept, 0, here.shape[0], 0)


def share_kernel(place, kept, received, out_next, out_last, d_left, packed, packed_next):
    half = d_left.shape[0]
    part, block = half // 2, half * half
    d_left[...] = kept[:half] + received[:half]
    packed[:part] = kept[half : half + part] + received[half : half + part]
    packed_next[:part] = kept[half + part :] + received[half + part : 2 * half]
    for step, out in enumerate((out_next, out_last)):
        at = slice(step * block, (step + 1) * block)
        plane = 2 * half + step
        packed[part, at] = flat(out[half:])
        packed[part + 1, at] = received[plane, block:]
        packed_next[part, at] = flat(out[:half])
        packed_next[part + 1, at] = received[plane, :block]


def gather_out(place, rows, t, count, start, out, here, early_other, early_far, received, far):
    half = rows // 2
    part, block = half // 2, half * half
    for far_half in (0, 1):
        source = (t + far_half * half) % rows
        at, wide = slice(source, source + count), slice(source * half, (source + count) * half)
        for far_core in (0, 1):
            core = place[1] + far_core * (1 - 2 * place[1])
            side = place[2] + far_half * (1 - 2 * place[2])
            for step in range(4):
                chip = jnp.bitwise_xor(place[0], step)
                first = pl.multiple_of(chip * 2 * rows + core * rows + side * half, half)
                if far_half:
                    if step < 2:
                        value = early_far[far_core, step, at]
                    else:
                        begin = (step - 2) * block + (t % half) * half
                        value = far[part + far_core, begin : begin + count * half].reshape(count, half, -1)
                elif far_core:
                    if step < 2:
                        value = early_other[step, at]
                    else:
                        value = received[rows + step - 2, wide].reshape(count, half, -1)
                else:
                    value = here[step][at]
                out[start : start + count, pl.ds(first, half), :] = value


def update_kernel(rows, place, *refs):
    here, early_other, early_far, received, far, far_next, gate, update, out = refs[:4], *refs[4:]
    half = rows // 2
    gather_out(place, rows, 0, half, 0, out, here, early_other, early_far, received, far)
    gather_out(place, rows, half, half, half, out, here, early_other, early_far, received, far_next)
    for t in range(0, rows, CHUNK):
        update[pl.ds(source_row(place, t, rows), CHUNK)] = gate[t : t + CHUNK] * out[t : t + CHUNK]


def base_kernel(rows, t, place, *refs):
    here, early_other, early_far, received, far, far_rows = refs[:4], *refs[4:9]
    gate, cotangent, w_gate, d_left, open_part, slope, mine, other, base, out = refs[9:]
    count, cols, chans = base.shape
    gather_out(place, rows, t, count, 0, out, here, early_other, early_far, received, far)
    w = gated_weights(place, mine, other, 0)
    at = slice(t, t + count)
    opened = gate[at]
    d_gate = cotangent[pl.ds(source_row(place, t, rows), count)] * (opened * out[...]) * (1.0 - opened)
    grad = flat(d_left[at] + far_rows[:count])
    both = jnp.concatenate([grad * flat(open_part[at]), grad * flat(slope[at])], axis=1)
    base[...] = (dot_t(flat(d_gate), w_gate[...]) + dot(both, w)).reshape(count, cols, -1)


def pair_kernel(first, place, normed, scale, base, d_right, d_right_near, d_right_across, open_part, slope, mine, other, d_mine):
    count, cols, chans = d_mine.shape
    w = gated_weights(place, mine, other, 2)
    at = slice(first, first + count)
    grad = flat(d_right[at] + d_right_near[...] + d_right_across[...])
    both = jnp.concatenate([grad * flat(open_part[at]), grad * flat(slope[at])], axis=1)
    d_normed = flat(base[...]) + dot(both, w)
    value = flat(normed[at])
    mean_grad = jnp.mean(d_normed, axis=-1, keepdims=True)
    mean_cross = jnp.mean(d_normed * value, axis=-1, keepdims=True)
    d_mine[...] = ((d_normed - mean_grad - value * mean_cross) * flat(scale[at])).reshape(count, cols, -1)


def join_kernel(firsts, sides, *refs):
    blocks, whole, sems = refs[: len(firsts)], refs[-2], refs[-1]
    side = lax.axis_index("ch")
    half = whole.shape[0] // 2
    copies = []
    for at, (block, first, mine) in enumerate(zip(blocks, firsts, sides)):
        start = (side if mine else 1 - side) * half + first
        copies.append(pltpu.make_async_copy(block, whole.at[pl.ds(start, block.shape[0])], sems.at[at]))
    for copy in copies:
        copy.start()
    for copy in copies:
        copy.wait()


def join(blocks, firsts, sides, shape, whole=None):
    anywhere = pl.BlockSpec(memory_space=pl.ANY)
    vmem = pl.BlockSpec(memory_space=pltpu.VMEM)
    given = [] if whole is None else [whole]
    return pl.pallas_call(
        functools.partial(join_kernel, firsts, sides),
        out_shape=jax.ShapeDtypeStruct(shape, F32),
        in_specs=[vmem] * len(blocks) + [anywhere] * len(given),
        out_specs=anywhere,
        input_output_aliases={len(blocks): 0} if given else {},
        scratch_shapes=[pltpu.SemaphoreType.DMA((len(blocks),))],
        compiler_params=pltpu.CompilerParams(vmem_limit_bytes=2 * 1024 * 1024),
    )(*blocks, *given)


def along(block, pairs):
    return lax.ppermute(block, "row", [(2 * a + core, 2 * b + core) for a, b in pairs for core in (0, 1)])


def other_core(block):
    return lax.ppermute(block, "row", [(i, i ^ 1) for i in range(lax.axis_size("row"))])


def other_half(block):
    return lax.ppermute(block, "ch", [(0, 1), (1, 0)])


NEXT = [(0, 1), (1, 0), (2, 3), (3, 2)]
MIDDLE = [(1, 2), (2, 1)]
OUTWARD = [(1, 0), (2, 3)]
INWARD = [(0, 1), (3, 2)]
ACROSS = [(0, 3), (3, 0), (1, 2), (2, 1)]


def on_tiles(pair, pair_mask, w_proj, w_gate, w_out, cotangent):
    rows, cols, width = pair.shape
    half = rows // 2
    chips = cols // (2 * rows)
    chans = 2 * w_out.shape[0]
    row, side = lax.axis_index("row"), lax.axis_index("ch")
    place = jnp.stack([row // 2, row % 2, side]).astype(jnp.int32)

    w_mine = jnp.swapaxes(w_proj, 1, 2)
    other = other_half(flat(w_mine)).reshape(w_mine.shape)
    kept = (half, cols, chans)
    other_out = other_half(w_out)
    normed, scale, keep, mine, *sent = call(
        first_kernel,
        [(half, cols, width)] * 2 + [(rows, cols), w_mine.shape] + [(half, cols, width)] * 2,
        (place, pair, pair_mask, w_mine),
        scratch=[((rows, cols), jnp.int32)],
        distant=3,
        sems=4,
    )
    theirs = [other_core(block) for block in sent]
    other, other_out = lax.optimization_barrier((other, other_out))
    right, open_right, slope_right = call(
        functools.partial(right_kernel, rows), [kept] * 3, (place, normed, keep, mine, other)
    )
    near = along(right, NEXT)
    middle = along(right, MIDDLE)
    _, cotangent_late = lax.optimization_barrier((right, cotangent))
    (third,) = call(
        third_kernel, [(chips + 1, rows, half, width)], (place, cotangent_late, keep), distant=1, sems=chips
    )
    theirs.append(other_core(third))
    quarter = (chips, rows, half, width)
    tile_outs = [(rows, half, width)] * 2 + [(2 * rows * half, chans), kept]
    tile_scratch = [(4, half * GROUP, chans), (2 * rows * half, chans)]
    out_here, out_there, d_x, d_right, rights = ([None] * 4 for _ in range(5))
    rights[0] = right
    left, left_there, open_left, slope_left, gate, d_here, d_there, w_all_out = call(
        functools.partial(prepare_kernel, rows),
        [(rows, cols, chans)] * 2 + [kept] * 2 + [(rows, cols, width), quarter, quarter, (chans, width)],
        (place, pair, keep, cotangent, *theirs, mine, other, w_gate, w_out, other_out),
        scratch=[(CHUNK, cols, width)],
    )

    def tile(step, *blocks):
        got = call(
            functools.partial(tile_kernel, step, len(blocks)),
            tile_outs + ([kept] if len(blocks) == 2 else []),
            (place, *blocks, left, left_there, d_here, d_there, w_all_out),
            scratch=tile_scratch,
        )
        out_here[step], out_there[step], d_x[step], d_right[step] = got[:4]
        rights[step] = got[4] if len(blocks) == 2 else blocks[0]

    near, d_here = lax.optimization_barrier((near, d_here))
    cross = along(near, MIDDLE)
    outer = along(middle, OUTWARD)
    tile(0, right)
    tile(1, near)
    early_other = other_core(jnp.stack(out_there[:2]))
    d_left_here, d_left_there = call(
        functools.partial(left_kernel, 2, False),
        [(rows, cols, chans)] * 2,
        (place, *rights[:2], *d_x[:2]),
    )
    cross, early_other, d_left_here = lax.optimization_barrier((cross, early_other, d_left_here))
    far = along(cross, OUTWARD)
    early_far = other_half(jnp.stack([jnp.stack(out_here[:2]), early_other]))
    tile(2, cross, outer)
    inward = along(d_right[2], INWARD)
    swapped = along(d_right[2], MIDDLE)
    d_left_here, d_left_there = call(
        functools.partial(left_kernel, 1, True),
        [(rows, cols, chans)] * 2,
        (place, rights[2], d_x[2], d_left_here, d_left_there),
    )
    far, d_left_here = lax.optimization_barrier((far, d_left_here))
    tile(3, middle, far)
    (d_left_sent,) = call(
        last_sent_kernel,
        [(rows + 2, cols, chans)],
        (place, rights[3], d_x[3], d_left_there, out_there[2], out_there[3]),
    )
    part = half // 2
    to_across, to_near, early_far, d_left_sent = lax.optimization_barrier(
        (d_right[3] + inward, d_right[1] + swapped, early_far, d_left_sent)
    )
    from_across, from_near = [along(to_across[:part], ACROSS)], [along(to_near[:part], NEXT)]
    received = other_core(d_left_sent)
    _, d_left_here = lax.optimization_barrier((d_left_sent, d_left_here))
    (d_left_kept,) = call(last_kept_kernel, [(rows, cols, chans)], (place, rights[3], d_x[3], d_left_here))
    packed_shape = (part + 2, cols, chans)
    d_left, *packed = call(
        share_kernel,
        [kept, packed_shape, packed_shape],
        (place, d_left_kept, received, out_here[2], out_here[3]),
    )
    far_parts = [other_half(block) for block in packed]
    from_across.append(along(to_across[part:], ACROSS))
    from_across[0], last_near = lax.optimization_barrier((from_across[0], to_near[part:]))
    from_near.append(along(last_near, NEXT))
    outs = (*out_here, early_other, early_far, received)
    mine_parts, other_parts = [], []
    for at, first in enumerate((0, part)):
        (base,) = call(
            functools.partial(base_kernel, rows, first),
            [(part, cols, width)],
            (place, *outs, far_parts[0], far_parts[at], gate, cotangent, w_gate, d_left, open_left, slope_left, mine, other),
            scratch=[(part, cols, width)],
        )
        if at:
            base, mine_parts[0] = lax.optimization_barrier((base, mine_parts[0]))
        (rows_done,) = call(
            functools.partial(pair_kernel, first),
            [(part, cols, width)],
            (place, normed, scale, base, d_right[0], from_near[at], from_across[at], open_right, slope_right, mine, other),
        )
        mine_parts.append(rows_done)
        other_parts.append(other_half(rows_done))
    _, gate_late = lax.optimization_barrier((mine_parts[1], gate))
    (update,) = call(
        functools.partial(update_kernel, rows),
        [(rows, cols, width)],
        (place, *outs, *far_parts, gate_late),
        scratch=[(rows, cols, width)],
    )
    firsts = (0, part)
    d_pair = join(mine_parts, firsts, (True, True), pair.shape)
    other_parts[0], update, d_pair = lax.optimization_barrier((other_parts[0], update, d_pair))
    d_pair = join(other_parts[:1], firsts[:1], (False,), pair.shape, d_pair)
    other_parts[1], d_pair = lax.optimization_barrier((other_parts[1], d_pair))
    d_pair = join(other_parts[1:], firsts[1:], (False,), pair.shape, d_pair)
    return (update, d_pair)


def passed_along(block, axis, distance):
    devices = range(lax.axis_size(axis))
    route = [((i - distance) % len(devices), i) for i in devices]
    return lax.ppermute(block, axis, route)


def normalize(values):
    mean = jnp.mean(values, axis=-1, keepdims=True)
    centered = values - mean
    variance = jnp.mean(centered * centered, axis=-1, keepdims=True)
    scale = lax.rsqrt(variance + 1e-05)
    return (centered * scale, scale)


def on_ring(pair, pair_mask, w_proj, w_gate, w_out, cotangent):
    highest = lax.Precision.HIGHEST
    normed, pair_scale = normalize(pair)
    proj = jnp.einsum("rqz,pzc->pcrq", normed, w_proj, precision=highest)
    keep = pair_mask.astype(jnp.float32)
    sig_left = jax.nn.sigmoid(proj[1])
    sig_right = jax.nn.sigmoid(proj[3])
    left = keep * sig_left * proj[0]
    right = keep * sig_right * proj[2]
    chans, rows, cols = left.shape
    count = lax.axis_size("row")
    here = lax.axis_index("row")

    def visit(step, carry):
        block, store, partial_value = carry
        source = (here - step) % count
        store = lax.dynamic_update_slice_in_dim(store, block, source * rows, 1)
        product = jnp.einsum("cik,cjk->cij", left, block, precision=highest)
        partial_value = lax.dynamic_update_slice_in_dim(partial_value, product, source * rows, 2)
        block = passed_along(block, "row", 1)
        return (block, store, partial_value)

    store = jnp.zeros((chans, rows * count, cols), jnp.float32)
    partial_value = jnp.zeros((chans, rows, rows * count), jnp.float32)
    block, store, partial_value = lax.fori_loop(0, count - 1, visit, (right, store, partial_value))
    source = (here + 1) % count
    right_all = lax.dynamic_update_slice_in_dim(store, block, source * rows, 1)
    product = jnp.einsum("cik,cjk->cij", left, block, precision=highest)
    partial_value = lax.dynamic_update_slice_in_dim(partial_value, product, source * rows, 2)
    mixed = lax.psum_scatter(partial_value, "sub", scatter_dimension=2, tiled=True)
    first = jnp.sum(mixed, axis=0)
    second = jnp.sum(mixed * mixed, axis=0)
    projected = jnp.einsum("crq,cd->rqd", mixed, w_out, precision=highest)
    col_total = jnp.sum(w_out, axis=0)
    projected, first, second, col_total = lax.psum((projected, first, second, col_total), "ch")
    center = first / C
    spread = lax.rsqrt(second / C - center * center + 1e-05)
    outgoing = (projected - center[..., None] * col_total) * spread[..., None]
    gate = jax.nn.sigmoid(jnp.einsum("rqz,zd->rqd", normed, w_gate, precision=highest))
    update = gate * outgoing
    d_outgoing = cotangent * gate
    d_gate_pre = cotangent * outgoing * gate * (1.0 - gate)
    d_mixed_norm = jnp.einsum("rqd,cd->crq", d_outgoing, w_out, precision=highest)
    mean_one = jnp.sum(d_outgoing * col_total, axis=-1) / C
    mean_two = jnp.sum(d_outgoing * outgoing, axis=-1) / C
    mixed_norm = (mixed - center) * spread
    d_mixed = (d_mixed_norm - mean_one - mixed_norm * mean_two) * spread
    d_mixed_full = lax.all_gather(d_mixed, "sub", axis=2, tiled=True)
    d_left = jnp.einsum("cij,cjk->cik", d_mixed_full, right_all, precision=highest)
    d_right = jnp.transpose(
        lax.psum_scatter(
            jnp.einsum("cij,cik->jck", d_mixed_full, left, precision=highest),
            "row",
            scatter_dimension=0,
            tiled=True,
        ),
        (1, 0, 2),
    )
    d_proj = jnp.stack(
        [
            d_left * keep * sig_left,
            d_left * keep * proj[0] * sig_left * (1.0 - sig_left),
            d_right * keep * sig_right,
            d_right * keep * proj[2] * sig_right * (1.0 - sig_right),
        ]
    )
    d_normed_part = jnp.einsum("pcrq,pzc->rqz", d_proj, w_proj, precision=highest)
    d_normed = lax.psum(d_normed_part, "ch")
    d_normed = d_normed + jnp.einsum("rqd,zd->rqz", d_gate_pre, w_gate, precision=highest)
    mean_grad = jnp.mean(d_normed, axis=-1, keepdims=True)
    mean_cross = jnp.mean(d_normed * normed, axis=-1, keepdims=True)
    d_pair = (d_normed - mean_grad - normed * mean_cross) * pair_scale
    return (update, d_pair)


def solution(mesh):
    sizes = mesh.shape
    tiled = sizes["row"] == 8 and sizes["ch"] == 2 and sizes["sub"] == 1
    return jax.shard_map(
        on_tiles if tiled else on_ring,
        mesh=mesh,
        in_specs=(
            P(("grp", "row"), "sub", None),
            P(("grp", "row"), "sub"),
            P(None, None, "ch"),
            P(),
            P("ch", None),
            P(("grp", "row"), "sub", None),
        ),
        out_specs=(P(("grp", "row"), "sub", None), P(("grp", "row"), "sub", None)),
        check_vma=False,
    )
```

```python
import functools
import jax
import jax.numpy as jnp
from jax import lax
from jax.experimental import pallas as pl
from jax.experimental.pallas import tpu as pltpu
from jax.sharding import PartitionSpec as P

C = 128
EPS = 1e-05
HIGHEST = lax.Precision.HIGHEST
F32 = jnp.float32
CHUNK = 4
CUTS = (0, 4, 8)
GROUP = 8


def halves(values):
    high = values.astype(jnp.bfloat16)
    return high, (values - high.astype(F32)).astype(jnp.bfloat16)


def contract(a, b, dims):
    (a_high, a_low), (b_high, b_low) = halves(a), halves(b)
    one = lambda x, y: lax.dot_general(x, y, (dims, ((), ())), preferred_element_type=F32)
    return one(a_high, b_high) + (one(a_high, b_low) + one(a_low, b_high))


def dot(a, b):
    return contract(a, b, ((1,), (0,)))


def dot_t(a, b):
    return contract(a, b, ((1,), (1,)))


def norm(values):
    mean = jnp.mean(values, axis=-1, keepdims=True)
    centered = values - mean
    variance = jnp.mean(centered * centered, axis=-1, keepdims=True)
    scale = lax.rsqrt(variance + EPS)
    return (centered * scale, scale)


def flat(values):
    return values.reshape(-1, values.shape[-1])


def call(kernel, outs, args, scratch=(), distant=0, sems=0):
    vmem = pl.BlockSpec(memory_space=pltpu.VMEM)
    spaces = [pl.BlockSpec(memory_space=pltpu.SMEM)] + [pl.BlockSpec(memory_space=pltpu.HBM)] * distant
    args = list(args)
    args[1 : 1 + distant] = [pltpu.with_memory_space_constraint(a, pltpu.HBM) for a in args[1 : 1 + distant]]
    return pl.pallas_call(
        kernel,
        out_shape=[jax.ShapeDtypeStruct(shape, F32) for shape in outs],
        in_specs=spaces + [vmem] * (len(args) - len(spaces)),
        out_specs=[vmem] * len(outs),
        scratch_shapes=[pltpu.VMEM(*shape) if isinstance(shape[0], tuple) else pltpu.VMEM(shape, F32) for shape in scratch]
        + ([pltpu.SemaphoreType.DMA((sems,))] if sems else []),
        compiler_params=pltpu.CompilerParams(vmem_limit_bytes=24 * 1024 * 1024),
        cost_estimate=pl.CostEstimate(flops=1000, bytes_accessed=1000, transcendentals=0),
    )(*args)


def source_row(place, t, rows):
    half = rows // 2
    if t < half:
        return place[2] * half + t
    return (1 - place[2]) * half + t - half


def first_col(place, chip, core, rows):
    half = rows // 2
    return pl.multiple_of(chip * 2 * rows + core * rows + place[2] * half, half)


def both_halves(place, mine, other):
    first = place[2] == 0
    a, b = jnp.where(first, mine, other), jnp.where(first, other, mine)
    return jnp.concatenate([a, b], axis=0)


def gated_weights(place, mine, other, which):
    return jnp.concatenate([both_halves(place, mine[p], other[p]) for p in (which, which + 1)], axis=0)


def gated(normed, keep_rows, w):
    count, cols = keep_rows.shape
    chans = w.shape[0] // 2
    spread = jnp.transpose(jnp.concatenate([keep_rows] * (8 // count), axis=0))
    keep = jnp.concatenate([spread[:, u : u + 1] for u in range(count)], axis=0)
    proj = dot_t(normed, w)
    sig = jax.nn.sigmoid(proj[:, chans:]) * keep
    return sig * proj[:, :chans], sig


def first_kernel(place, pair, mask, w_proj, normed, scale, keep, mine, first, second, flags, sems):
    half = first.shape[0]
    moves = ((pair.at[:half], first), (pair.at[half:], second), (mask, flags), (w_proj, mine))
    copies = [pltpu.make_async_copy(source, target, sems.at[at]) for at, (source, target) in enumerate(moves)]
    for copy in copies:
        copy.start()
    for copy in copies:
        copy.wait()
    keep[...] = flags[...].astype(F32)
    for t in range(0, half, CHUNK):
        at = slice(t, t + CHUNK)
        value, factor = norm(jnp.where(place[2] == 0, first[at], second[at]))
        normed[at] = value
        scale[at] = jnp.broadcast_to(factor, value.shape)


def third_kernel(place, cotangent, keep, packed, sems):
    rows = cotangent.shape[0]
    half, chips = rows // 2, packed.shape[0] - 1
    copies = []
    for chip in range(chips):
        source = cotangent.at[:, pl.ds(first_col(place, chip, 1 - place[1], rows), half), :]
        copies.append(pltpu.make_async_copy(source, packed.at[chip], sems.at[chip]))
    for copy in copies:
        copy.start()
    packed[chips, :, 0, :] = keep[...]
    for copy in copies:
        copy.wait()


def right_kernel(rows, place, normed, keep, mine, other, right, open_part, slope):
    half, cols, chans = right.shape
    w = gated_weights(place, mine, other, 2)
    for t in range(0, half, CHUNK):
        at = slice(t, t + CHUNK)
        value, sig = gated(flat(normed[at]), keep[pl.ds(source_row(place, t, rows), CHUNK), :], w)
        shape = (CHUNK, cols, chans)
        right[at] = value.reshape(shape)
        open_part[at] = sig.reshape(shape)
        slope[at] = (value * (1.0 - sig)).reshape(shape)


def prepare_kernel(rows, place, pair, keep, cotangent, first, second, third, mine, other, w_gate, mine_out, other_out, *refs):
    left_here, left_there, open_part, slope, gate, d_here, d_there, w_out, normed_rows = refs
    half, cols, chans = open_part.shape
    chips = cols // (2 * rows)
    shape = (CHUNK, cols, chans)
    w = gated_weights(place, mine, other, 0)
    w_out[...] = both_halves(place, mine_out[...], other_out[...])
    for t in range(0, rows, CHUNK):
        row = source_row(place, t, rows)
        at = slice(t, t + CHUNK)
        normed, _ = norm(flat(pair[pl.ds(row, CHUNK)]))
        value, sig = gated(normed, keep[pl.ds(row, CHUNK), :], w)
        left_here[at] = value.reshape(shape)
        if t < half:
            open_part[at] = sig.reshape(shape)
            slope[at] = (value * (1.0 - sig)).reshape(shape)
        gate[at] = jax.nn.sigmoid(dot(normed, w_gate[...])).reshape(CHUNK, cols, -1)
        for chip in range(chips):
            near = pl.ds(first_col(place, chip, place[1], rows), half)
            d_here[chip, at] = gate[at, near, :] * cotangent[pl.ds(row, CHUNK), near, :]
        their_row = row % half
        normed, _ = norm(flat(jnp.where(row < half, first[pl.ds(their_row, CHUNK)], second[pl.ds(their_row, CHUNK)])))
        value, _ = gated(normed, third[chips, pl.ds(row, CHUNK), 0, :], w)
        left_there[at] = value.reshape(shape)
        normed_rows[...] = normed.reshape(CHUNK, cols, -1)
        picked = [
            normed_rows[:, pl.ds(first_col(place, chip, place[1], rows), half), :] for chip in range(chips)
        ]
        opened = jax.nn.sigmoid(dot(flat(jnp.stack(picked)), w_gate[...])).reshape(chips, CHUNK, half, -1)
        for chip in range(chips):
            d_there[chip, at] = opened[chip] * third[chip, pl.ds(row, CHUNK)]


def tile_body(step, place, right, left_here, left_there, d_here, d_there, w_out, out_here, out_there, d_x, d_right, partial, x):
    rows = left_here.shape[0]
    half, cols, chans = right.shape
    groups = cols // GROUP

    def forward(pair_at, _):
        for which, left in enumerate((left_here, left_there)):
            i = pair_at * 2
            value = [left[i], left[i + 1]]
            for j in range(half):
                block = right[j]
                for u in range(2):
                    product = (value[u] * block).reshape(groups, GROUP, chans)
                    partial[2 * which + u, j * GROUP : (j + 1) * GROUP] = jnp.sum(product, axis=0)
            for u in range(2):
                total = partial[2 * which + u, pl.ds(0, half, stride=GROUP), :]
                for s in range(1, GROUP):
                    total = total + partial[2 * which + u, pl.ds(s, half, stride=GROUP), :]
                x[pl.ds(pl.multiple_of((which * rows + i + u) * half, half), half), :] = total
        return 0

    lax.fori_loop(0, rows // 2, forward, 0)
    chip = jnp.bitwise_xor(place[0], step)
    d_out = jnp.concatenate([flat(d_here[chip]), flat(d_there[chip])], axis=0)
    normed, scale = norm(x[...])
    out = dot(normed, w_out[...])
    out_here[...] = out[: rows * half].reshape(rows, half, -1)
    out_there[...] = out[rows * half :].reshape(rows, half, -1)
    d_normed = dot_t(d_out, w_out[...])
    mean_one = jnp.mean(d_normed, axis=-1, keepdims=True)
    mean_two = jnp.mean(d_normed * normed, axis=-1, keepdims=True)
    d_x[...] = (d_normed - mean_one - normed * mean_two) * scale
    wide = 2 * GROUP

    def backward(at, _):
        here = pl.ds(pl.multiple_of(at * wide, wide), wide)

        def add(block, totals):
            totals = list(totals)
            for u in range(GROUP):
                for which, left in enumerate((left_here, left_there)):
                    i = block * GROUP + u
                    value = left[i, here, :]
                    for j in range(half):
                        totals[j] = totals[j] + value * d_x[pl.ds((which * rows + i) * half + j, 1), :]
            return tuple(totals)

        totals = lax.fori_loop(0, rows // GROUP, add, (jnp.zeros((wide, chans), F32),) * half)
        for j in range(half):
            d_right[j, here, :] = totals[j]
        return 0

    lax.fori_loop(0, cols // wide, backward, 0)


def tile_kernel(step, parts, place, *refs):
    rights, rest = refs[:parts], refs[parts:]
    if parts == 2:
        sum_out = rest[9]
        sum_out[...] = rights[0][...] + rights[1][...]
        tile_body(step, place, sum_out, *rest[:9], *rest[10:])
    else:
        tile_body(step, place, rights[0], *rest)


def left_rows(tiles, base, out, first, count, start):
    half, cols, chans = tiles[0][0].shape

    def body(pair_at, _):
        i = pair_at * 2
        totals = [jnp.zeros((cols, chans), F32)] * 2 if base is None else [base[start + i], base[start + i + 1]]
        for right, d_x in tiles:
            for j in range(half):
                value = right[j]
                for u in range(2):
                    totals[u] = totals[u] + value * d_x[pl.ds((first + i + u) * half + j, 1), :]
        out[start + i] = totals[0]
        out[start + i + 1] = totals[1]
        return 0

    lax.fori_loop(0, count // 2, body, 0)


def left_kernel(tiles, place, *refs):
    pairs = tuple(zip(refs[:tiles], refs[tiles : 2 * tiles]))
    rows = refs[-1].shape[0]
    for which, out in enumerate(refs[-2:]):
        left_rows(pairs, None, out, which * rows, rows, 0)


def last_tile_kernel(step, place, one, two, left_here, left_there, d_here, d_there, w_out, there, out_next, *refs):
    out_here, out_there, d_x, d_right, right, sent, partial, x = refs
    rows = there.shape[0]
    right[...] = one[...] + two[...]
    tile_body(step, place, right, left_here, left_there, d_here, d_there, w_out, out_here, out_there, d_x, d_right, partial, x)
    left_rows(((right, d_x),), there, sent, rows, rows, 0)
    sent[rows] = flat(out_next[...])
    sent[rows + 1] = flat(out_there[...])


def last_kept_kernel(place, right, d_x, here, kept):
    left_rows(((right, d_x),), here, kept, 0, here.shape[0], 0)


def share_kernel(cuts, place, kept, received, out_next, out_last, d_left, *packed):
    half = d_left.shape[0]
    block = half * half
    d_left[...] = kept[:half] + received[:half]
    for first, last, part in zip(cuts, cuts[1:], packed):
        at = slice(half + first, half + last)
        part[: last - first] = kept[at] + received[at]
    early, late = packed[0], packed[-1]
    for step, out in enumerate((out_next, out_last)):
        at = slice(step * block, (step + 1) * block)
        plane = 2 * half + step
        early[early.shape[0] - 2, at] = flat(out[half:])
        early[early.shape[0] - 1, at] = received[plane, block:]
        late[late.shape[0] - 2, at] = flat(out[:half])
        late[late.shape[0] - 1, at] = received[plane, :block]


def gather_out(place, rows, t, count, start, out, here, early_other, early_far, received, far):
    half = rows // 2
    block = half * half
    for far_half in (0, 1):
        source = (t + far_half * half) % rows
        at, wide = slice(source, source + count), slice(source * half, (source + count) * half)
        for far_core in (0, 1):
            core = place[1] + far_core * (1 - 2 * place[1])
            side = place[2] + far_half * (1 - 2 * place[2])
            for step in range(4):
                chip = jnp.bitwise_xor(place[0], step)
                first = pl.multiple_of(chip * 2 * rows + core * rows + side * half, half)
                if far_half:
                    if step < 2:
                        value = early_far[far_core, step, at]
                    else:
                        begin = (step - 2) * block + (t % half) * half
                        value = far[far.shape[0] - 2 + far_core, begin : begin + count * half].reshape(count, half, -1)
                elif far_core:
                    if step < 2:
                        value = early_other[step, at]
                    else:
                        value = received[rows + step - 2, wide].reshape(count, half, -1)
                else:
                    value = here[step][at]
                out[start : start + count, pl.ds(first, half), :] = value


def update_kernel(rows, place, *refs):
    here, early_other, early_far, received, far, far_next, gate, update, out = refs[:4], *refs[4:]
    half = rows // 2
    gather_out(place, rows, 0, half, 0, out, here, early_other, early_far, received, far)
    gather_out(place, rows, half, half, half, out, here, early_other, early_far, received, far_next)
    for t in range(0, rows, CHUNK):
        update[pl.ds(source_row(place, t, rows), CHUNK)] = gate[t : t + CHUNK] * out[t : t + CHUNK]


def base_kernel(rows, t, place, *refs):
    here, early_other, early_far, received, far, far_rows = refs[:4], *refs[4:9]
    gate, cotangent, w_gate, d_left, open_part, slope, mine, other, base, out = refs[9:]
    count, cols, chans = base.shape
    gather_out(place, rows, t, count, 0, out, here, early_other, early_far, received, far)
    w = gated_weights(place, mine, other, 0)
    at = slice(t, t + count)
    opened = gate[at]
    d_gate = cotangent[pl.ds(source_row(place, t, rows), count)] * (opened * out[...]) * (1.0 - opened)
    grad = flat(d_left[at] + far_rows[:count])
    both = jnp.concatenate([grad * flat(open_part[at]), grad * flat(slope[at])], axis=1)
    base[...] = (dot_t(flat(d_gate), w_gate[...]) + dot(both, w)).reshape(count, cols, -1)


def pair_kernel(first, place, normed, scale, base, d_right, d_right_near, d_right_across, open_part, slope, mine, other, d_mine):
    count, cols, chans = d_mine.shape
    w = gated_weights(place, mine, other, 2)
    at = slice(first, first + count)
    grad = flat(d_right[at] + d_right_near[...] + d_right_across[...])
    both = jnp.concatenate([grad * flat(open_part[at]), grad * flat(slope[at])], axis=1)
    d_normed = flat(base[...]) + dot(both, w)
    value = flat(normed[at])
    mean_grad = jnp.mean(d_normed, axis=-1, keepdims=True)
    mean_cross = jnp.mean(d_normed * value, axis=-1, keepdims=True)
    d_mine[...] = ((d_normed - mean_grad - value * mean_cross) * flat(scale[at])).reshape(count, cols, -1)


def join_kernel(firsts, sides, *refs):
    blocks, whole, sems = refs[: len(firsts)], refs[-2], refs[-1]
    side = lax.axis_index("ch")
    half = whole.shape[0] // 2
    copies = []
    for at, (block, first, mine) in enumerate(zip(blocks, firsts, sides)):
        start = (side if mine else 1 - side) * half + first
        copies.append(pltpu.make_async_copy(block, whole.at[pl.ds(start, block.shape[0])], sems.at[at]))
    for copy in copies:
        copy.start()
    for copy in copies:
        copy.wait()


def join(blocks, firsts, sides, shape, whole=None):
    anywhere = pl.BlockSpec(memory_space=pl.ANY)
    vmem = pl.BlockSpec(memory_space=pltpu.VMEM)
    given = [] if whole is None else [whole]
    return pl.pallas_call(
        functools.partial(join_kernel, firsts, sides),
        out_shape=jax.ShapeDtypeStruct(shape, F32),
        in_specs=[vmem] * len(blocks) + [anywhere] * len(given),
        out_specs=anywhere,
        input_output_aliases={len(blocks): 0} if given else {},
        scratch_shapes=[pltpu.SemaphoreType.DMA((len(blocks),))],
        compiler_params=pltpu.CompilerParams(vmem_limit_bytes=2 * 1024 * 1024),
    )(*blocks, *given)


def along(block, pairs):
    return lax.ppermute(block, "row", [(2 * a + core, 2 * b + core) for a, b in pairs for core in (0, 1)])


def other_core(block):
    return lax.ppermute(block, "row", [(i, i ^ 1) for i in range(lax.axis_size("row"))])


def other_half(block):
    return lax.ppermute(block, "ch", [(0, 1), (1, 0)])


NEXT = [(0, 1), (1, 0), (2, 3), (3, 2)]
MIDDLE = [(1, 2), (2, 1)]
OUTWARD = [(1, 0), (2, 3)]
INWARD = [(0, 1), (3, 2)]
ACROSS = [(0, 3), (3, 0), (1, 2), (2, 1)]


def on_tiles(pair, pair_mask, w_proj, w_gate, w_out, cotangent):
    rows, cols, width = pair.shape
    half = rows // 2
    chips = cols // (2 * rows)
    chans = 2 * w_out.shape[0]
    row, side = lax.axis_index("row"), lax.axis_index("ch")
    place = jnp.stack([row // 2, row % 2, side]).astype(jnp.int32)

    w_mine = jnp.swapaxes(w_proj, 1, 2)
    other = other_half(flat(w_mine)).reshape(w_mine.shape)
    kept = (half, cols, chans)
    other_out = other_half(w_out)
    normed, scale, keep, mine, *sent = call(
        first_kernel,
        [(half, cols, width)] * 2 + [(rows, cols), w_mine.shape] + [(half, cols, width)] * 2,
        (place, pair, pair_mask, w_mine),
        scratch=[((rows, cols), jnp.int32)],
        distant=3,
        sems=4,
    )
    theirs = [other_core(block) for block in sent]
    right, open_right, slope_right = call(
        functools.partial(right_kernel, rows), [kept] * 3, (place, normed, keep, mine, other)
    )
    right, other_out = lax.optimization_barrier((right, other_out))
    near = along(right, NEXT)
    middle = along(right, MIDDLE)
    _, cotangent_late = lax.optimization_barrier((right, cotangent))
    (third,) = call(
        third_kernel, [(chips + 1, rows, half, width)], (place, cotangent_late, keep), distant=1, sems=chips
    )
    theirs.append(other_core(third))
    quarter = (chips, rows, half, width)
    tile_outs = [(rows, half, width)] * 2 + [(2 * rows * half, chans), kept]
    tile_scratch = [(4, half * GROUP, chans), (2 * rows * half, chans)]
    out_here, out_there, d_x, d_right, rights = ([None] * 4 for _ in range(5))
    rights[0] = right
    left, left_there, open_left, slope_left, gate, d_here, d_there, w_all_out = call(
        functools.partial(prepare_kernel, rows),
        [(rows, cols, chans)] * 2 + [kept] * 2 + [(rows, cols, width), quarter, quarter, (chans, width)],
        (place, pair, keep, cotangent, *theirs, mine, other, w_gate, w_out, other_out),
        scratch=[(CHUNK, cols, width)],
    )

    def tile(step, *blocks):
        got = call(
            functools.partial(tile_kernel, step, len(blocks)),
            tile_outs + ([kept] if len(blocks) == 2 else []),
            (place, *blocks, left, left_there, d_here, d_there, w_all_out),
            scratch=tile_scratch,
        )
        out_here[step], out_there[step], d_x[step], d_right[step] = got[:4]
        rights[step] = got[4] if len(blocks) == 2 else blocks[0]

    near, d_here = lax.optimization_barrier((near, d_here))
    cross = along(near, MIDDLE)
    outer = along(middle, OUTWARD)
    tile(0, right)
    tile(1, near)
    early_other = other_core(jnp.stack(out_there[:2]))
    cross, early_other, d_x[1] = lax.optimization_barrier((cross, early_other, d_x[1]))
    far = along(cross, OUTWARD)
    early_far = other_half(jnp.stack([jnp.stack(out_here[:2]), early_other]))
    tile(2, cross, outer)
    inward = along(d_right[2], INWARD)
    swapped = along(d_right[2], MIDDLE)
    d_left_here, d_left_there = call(
        functools.partial(left_kernel, 3),
        [(rows, cols, chans)] * 2,
        (place, *rights[:3], *d_x[:3]),
    )
    far, d_left_here = lax.optimization_barrier((far, d_left_here))
    out_here[3], out_there[3], d_x[3], d_right[3], rights[3], d_left_sent = call(
        functools.partial(last_tile_kernel, 3),
        tile_outs + [kept, (rows + 2, cols, chans)],
        (place, middle, far, left, left_there, d_here, d_there, w_all_out, d_left_there, out_there[2]),
        scratch=tile_scratch,
    )
    cuts = [half * eighths // 8 for eighths in CUTS]
    spans = list(zip(cuts, cuts[1:]))
    swapped, to_across = lax.optimization_barrier((swapped, d_right[3] + inward))
    to_across, to_near, early_far, d_left_sent = lax.optimization_barrier(
        (to_across, d_right[1] + swapped, early_far, d_left_sent)
    )
    from_across, from_near = [along(to_across[: cuts[1]], ACROSS)], [along(to_near[: cuts[1]], NEXT)]
    received = other_core(d_left_sent)
    _, d_left_here = lax.optimization_barrier((d_left_sent, d_left_here))
    (d_left_kept,) = call(last_kept_kernel, [(rows, cols, chans)], (place, rights[3], d_x[3], d_left_here))
    sizes = [last - first for first, last in spans]
    sizes[0] += 2
    sizes[-1] += 2
    d_left, *packed = call(
        functools.partial(share_kernel, cuts),
        [kept] + [(size, cols, chans) for size in sizes],
        (place, d_left_kept, received, out_here[2], out_here[3]),
    )
    far_parts = [other_half(block) for block in packed]
    for first, last in spans[1:]:
        from_across.append(along(to_across[first:last], ACROSS))
        from_across[-2], last_near = lax.optimization_barrier((from_across[-2], to_near[first:last]))
        from_near.append(along(last_near, NEXT))
    outs = (*out_here, early_other, early_far, received)
    mine_parts, other_parts = [], []
    for at, (first, last) in enumerate(spans):
        (base,) = call(
            functools.partial(base_kernel, rows, first),
            [(last - first, cols, width)],
            (place, *outs, far_parts[0], far_parts[at], gate, cotangent, w_gate, d_left, open_left, slope_left, mine, other),
            scratch=[(last - first, cols, width)],
        )
        if at:
            base, mine_parts[-1] = lax.optimization_barrier((base, mine_parts[-1]))
        (rows_done,) = call(
            functools.partial(pair_kernel, first),
            [(last - first, cols, width)],
            (place, normed, scale, base, d_right[0], from_near[at], from_across[at], open_right, slope_right, mine, other),
        )
        mine_parts.append(rows_done)
        other_parts.append(other_half(rows_done))
    _, gate_late = lax.optimization_barrier((mine_parts[-1], gate))
    (update,) = call(
        functools.partial(update_kernel, rows),
        [(rows, cols, width)],
        (place, *outs, far_parts[0], far_parts[-1], gate_late),
        scratch=[(rows, cols, width)],
    )
    d_pair = join(mine_parts, cuts[:-1], (True,) * len(spans), pair.shape)
    d_pair, update = lax.optimization_barrier((d_pair, update))
    for first, part in zip(cuts, other_parts):
        d_pair, part = lax.optimization_barrier((d_pair, part))
        d_pair = join([part], (first,), (False,), pair.shape, d_pair)
    return (update, d_pair)


def passed_along(block, axis, distance):
    devices = range(lax.axis_size(axis))
    route = [((i - distance) % len(devices), i) for i in devices]
    return lax.ppermute(block, axis, route)


def normalize(values):
    mean = jnp.mean(values, axis=-1, keepdims=True)
    centered = values - mean
    variance = jnp.mean(centered * centered, axis=-1, keepdims=True)
    scale = lax.rsqrt(variance + 1e-05)
    return (centered * scale, scale)


def on_ring(pair, pair_mask, w_proj, w_gate, w_out, cotangent):
    highest = lax.Precision.HIGHEST
    normed, pair_scale = normalize(pair)
    proj = jnp.einsum("rqz,pzc->pcrq", normed, w_proj, precision=highest)
    keep = pair_mask.astype(jnp.float32)
    sig_left = jax.nn.sigmoid(proj[1])
    sig_right = jax.nn.sigmoid(proj[3])
    left = keep * sig_left * proj[0]
    right = keep * sig_right * proj[2]
    chans, rows, cols = left.shape
    count = lax.axis_size("row")
    here = lax.axis_index("row")

    def visit(step, carry):
        block, store, partial_value = carry
        source = (here - step) % count
        store = lax.dynamic_update_slice_in_dim(store, block, source * rows, 1)
        product = jnp.einsum("cik,cjk->cij", left, block, precision=highest)
        partial_value = lax.dynamic_update_slice_in_dim(partial_value, product, source * rows, 2)
        block = passed_along(block, "row", 1)
        return (block, store, partial_value)

    store = jnp.zeros((chans, rows * count, cols), jnp.float32)
    partial_value = jnp.zeros((chans, rows, rows * count), jnp.float32)
    block, store, partial_value = lax.fori_loop(0, count - 1, visit, (right, store, partial_value))
    source = (here + 1) % count
    right_all = lax.dynamic_update_slice_in_dim(store, block, source * rows, 1)
    product = jnp.einsum("cik,cjk->cij", left, block, precision=highest)
    partial_value = lax.dynamic_update_slice_in_dim(partial_value, product, source * rows, 2)
    mixed = lax.psum_scatter(partial_value, "sub", scatter_dimension=2, tiled=True)
    first = jnp.sum(mixed, axis=0)
    second = jnp.sum(mixed * mixed, axis=0)
    projected = jnp.einsum("crq,cd->rqd", mixed, w_out, precision=highest)
    col_total = jnp.sum(w_out, axis=0)
    projected, first, second, col_total = lax.psum((projected, first, second, col_total), "ch")
    center = first / C
    spread = lax.rsqrt(second / C - center * center + 1e-05)
    outgoing = (projected - center[..., None] * col_total) * spread[..., None]
    gate = jax.nn.sigmoid(jnp.einsum("rqz,zd->rqd", normed, w_gate, precision=highest))
    update = gate * outgoing
    d_outgoing = cotangent * gate
    d_gate_pre = cotangent * outgoing * gate * (1.0 - gate)
    d_mixed_norm = jnp.einsum("rqd,cd->crq", d_outgoing, w_out, precision=highest)
    mean_one = jnp.sum(d_outgoing * col_total, axis=-1) / C
    mean_two = jnp.sum(d_outgoing * outgoing, axis=-1) / C
    mixed_norm = (mixed - center) * spread
    d_mixed = (d_mixed_norm - mean_one - mixed_norm * mean_two) * spread
    d_mixed_full = lax.all_gather(d_mixed, "sub", axis=2, tiled=True)
    d_left = jnp.einsum("cij,cjk->cik", d_mixed_full, right_all, precision=highest)
    d_right = jnp.transpose(
        lax.psum_scatter(
            jnp.einsum("cij,cik->jck", d_mixed_full, left, precision=highest),
            "row",
            scatter_dimension=0,
            tiled=True,
        ),
        (1, 0, 2),
    )
    d_proj = jnp.stack(
        [
            d_left * keep * sig_left,
            d_left * keep * proj[0] * sig_left * (1.0 - sig_left),
            d_right * keep * sig_right,
            d_right * keep * proj[2] * sig_right * (1.0 - sig_right),
        ]
    )
    d_normed_part = jnp.einsum("pcrq,pzc->rqz", d_proj, w_proj, precision=highest)
    d_normed = lax.psum(d_normed_part, "ch")
    d_normed = d_normed + jnp.einsum("rqd,zd->rqz", d_gate_pre, w_gate, precision=highest)
    mean_grad = jnp.mean(d_normed, axis=-1, keepdims=True)
    mean_cross = jnp.mean(d_normed * normed, axis=-1, keepdims=True)
    d_pair = (d_normed - mean_grad - normed * mean_cross) * pair_scale
    return (update, d_pair)


def solution(mesh):
    sizes = mesh.shape
    tiled = sizes["row"] == 8 and sizes["ch"] == 2 and sizes["sub"] == 1
    return jax.shard_map(
        on_tiles if tiled else on_ring,
        mesh=mesh,
        in_specs=(
            P(("grp", "row"), "sub", None),
            P(("grp", "row"), "sub"),
            P(None, None, "ch"),
            P(),
            P("ch", None),
            P(("grp", "row"), "sub", None),
        ),
        out_specs=(P(("grp", "row"), "sub", None), P(("grp", "row"), "sub", None)),
        check_vma=False,
    )
```

```python
import functools
import jax
import jax.numpy as jnp
from jax import lax
from jax.experimental import pallas as pl
from jax.experimental.pallas import tpu as pltpu
from jax.sharding import PartitionSpec as P

C = 128
EPS = 1e-05
HIGHEST = lax.Precision.HIGHEST
F32 = jnp.float32
CHUNK = 4
CUTS = (0, 4, 8)
GROUP = 8


def halves(values):
    high = values.astype(jnp.bfloat16)
    return high, (values - high.astype(F32)).astype(jnp.bfloat16)


def contract(a, b, dims):
    (a_high, a_low), (b_high, b_low) = halves(a), halves(b)
    one = lambda x, y: lax.dot_general(x, y, (dims, ((), ())), preferred_element_type=F32)
    return one(a_high, b_high) + (one(a_high, b_low) + one(a_low, b_high))


def dot(a, b):
    return contract(a, b, ((1,), (0,)))


def dot_t(a, b):
    return contract(a, b, ((1,), (1,)))


def norm(values):
    mean = jnp.mean(values, axis=-1, keepdims=True)
    centered = values - mean
    variance = jnp.mean(centered * centered, axis=-1, keepdims=True)
    scale = lax.rsqrt(variance + EPS)
    return (centered * scale, scale)


def flat(values):
    return values.reshape(-1, values.shape[-1])


def call(kernel, outs, args, scratch=(), distant=0, sems=0):
    vmem = pl.BlockSpec(memory_space=pltpu.VMEM)
    spaces = [pl.BlockSpec(memory_space=pltpu.SMEM)] + [pl.BlockSpec(memory_space=pltpu.HBM)] * distant
    args = list(args)
    args[1 : 1 + distant] = [pltpu.with_memory_space_constraint(a, pltpu.HBM) for a in args[1 : 1 + distant]]
    return pl.pallas_call(
        kernel,
        out_shape=[jax.ShapeDtypeStruct(shape, F32) for shape in outs],
        in_specs=spaces + [vmem] * (len(args) - len(spaces)),
        out_specs=[vmem] * len(outs),
        scratch_shapes=[pltpu.VMEM(*shape) if isinstance(shape[0], tuple) else pltpu.VMEM(shape, F32) for shape in scratch]
        + ([pltpu.SemaphoreType.DMA((sems,))] if sems else []),
        compiler_params=pltpu.CompilerParams(vmem_limit_bytes=24 * 1024 * 1024),
        cost_estimate=pl.CostEstimate(flops=1000, bytes_accessed=1000, transcendentals=0),
    )(*args)


def source_row(place, t, rows):
    half = rows // 2
    if t < half:
        return place[2] * half + t
    return (1 - place[2]) * half + t - half


def first_col(place, chip, core, rows):
    half = rows // 2
    return pl.multiple_of(chip * 2 * rows + core * rows + place[2] * half, half)


def both_halves(place, mine, other):
    first = place[2] == 0
    a, b = jnp.where(first, mine, other), jnp.where(first, other, mine)
    return jnp.concatenate([a, b], axis=0)


def gated_weights(place, mine, other, which):
    return jnp.concatenate([both_halves(place, mine[p], other[p]) for p in (which, which + 1)], axis=0)


def gated(normed, keep_rows, w):
    count, cols = keep_rows.shape
    chans = w.shape[0] // 2
    spread = jnp.transpose(jnp.concatenate([keep_rows] * (8 // count), axis=0))
    keep = jnp.concatenate([spread[:, u : u + 1] for u in range(count)], axis=0)
    proj = dot_t(normed, w)
    sig = jax.nn.sigmoid(proj[:, chans:]) * keep
    return sig * proj[:, :chans], sig


def first_kernel(place, pair, mask, w_proj, normed, scale, keep, mine, first, second, flags, sems):
    half = first.shape[0]
    moves = ((pair.at[:half], first), (pair.at[half:], second), (mask, flags), (w_proj, mine))
    copies = [pltpu.make_async_copy(source, target, sems.at[at]) for at, (source, target) in enumerate(moves)]
    for copy in copies:
        copy.start()
    for copy in copies:
        copy.wait()
    keep[...] = flags[...].astype(F32)
    for t in range(0, half, CHUNK):
        at = slice(t, t + CHUNK)
        value, factor = norm(jnp.where(place[2] == 0, first[at], second[at]))
        normed[at] = value
        scale[at] = jnp.broadcast_to(factor, value.shape)


def third_kernel(place, cotangent, keep, packed, sems):
    rows = cotangent.shape[0]
    half, chips = rows // 2, packed.shape[0] - 1
    copies = []
    for chip in range(chips):
        source = cotangent.at[:, pl.ds(first_col(place, chip, 1 - place[1], rows), half), :]
        copies.append(pltpu.make_async_copy(source, packed.at[chip], sems.at[chip]))
    for copy in copies:
        copy.start()
    packed[chips, :, 0, :] = keep[...]
    for copy in copies:
        copy.wait()


def right_kernel(rows, place, normed, keep, mine, other, right, open_part, slope):
    half, cols, chans = right.shape
    w = gated_weights(place, mine, other, 2)
    for t in range(0, half, CHUNK):
        at = slice(t, t + CHUNK)
        value, sig = gated(flat(normed[at]), keep[pl.ds(source_row(place, t, rows), CHUNK), :], w)
        shape = (CHUNK, cols, chans)
        right[at] = value.reshape(shape)
        open_part[at] = sig.reshape(shape)
        slope[at] = (value * (1.0 - sig)).reshape(shape)


def prepare_kernel(rows, place, pair, keep, cotangent, first, second, third, mine, other, w_gate, mine_out, other_out, *refs):
    left_here, left_there, open_part, slope, gate, d_here, d_there, w_out, normed_rows = refs
    half, cols, chans = open_part.shape
    chips = cols // (2 * rows)
    shape = (CHUNK, cols, chans)
    w = gated_weights(place, mine, other, 0)
    w_out[...] = both_halves(place, mine_out[...], other_out[...])
    for t in range(0, rows, CHUNK):
        row = source_row(place, t, rows)
        at = slice(t, t + CHUNK)
        normed, _ = norm(flat(pair[pl.ds(row, CHUNK)]))
        value, sig = gated(normed, keep[pl.ds(row, CHUNK), :], w)
        left_here[at] = value.reshape(shape)
        if t < half:
            open_part[at] = sig.reshape(shape)
            slope[at] = (value * (1.0 - sig)).reshape(shape)
        gate[at] = jax.nn.sigmoid(dot(normed, w_gate[...])).reshape(CHUNK, cols, -1)
        for chip in range(chips):
            near = pl.ds(first_col(place, chip, place[1], rows), half)
            d_here[chip, at] = gate[at, near, :] * cotangent[pl.ds(row, CHUNK), near, :]
        their_row = row % half
        normed, _ = norm(flat(jnp.where(row < half, first[pl.ds(their_row, CHUNK)], second[pl.ds(their_row, CHUNK)])))
        value, _ = gated(normed, third[chips, pl.ds(row, CHUNK), 0, :], w)
        left_there[at] = value.reshape(shape)
        normed_rows[...] = normed.reshape(CHUNK, cols, -1)
        picked = [
            normed_rows[:, pl.ds(first_col(place, chip, place[1], rows), half), :] for chip in range(chips)
        ]
        opened = jax.nn.sigmoid(dot(flat(jnp.stack(picked)), w_gate[...])).reshape(chips, CHUNK, half, -1)
        for chip in range(chips):
            d_there[chip, at] = opened[chip] * third[chip, pl.ds(row, CHUNK)]


def tile_body(step, place, right, left_here, left_there, d_here, d_there, w_out, out_here, out_there, d_x, d_right, partial, x):
    rows = left_here.shape[0]
    half, cols, chans = right.shape
    groups = cols // GROUP

    def forward(pair_at, _):
        for which, left in enumerate((left_here, left_there)):
            i = pair_at * 2
            value = [left[i], left[i + 1]]
            for j in range(half):
                block = right[j]
                for u in range(2):
                    product = (value[u] * block).reshape(groups, GROUP, chans)
                    partial[2 * which + u, j * GROUP : (j + 1) * GROUP] = jnp.sum(product, axis=0)
            for u in range(2):
                total = partial[2 * which + u, pl.ds(0, half, stride=GROUP), :]
                for s in range(1, GROUP):
                    total = total + partial[2 * which + u, pl.ds(s, half, stride=GROUP), :]
                x[pl.ds(pl.multiple_of((which * rows + i + u) * half, half), half), :] = total
        return 0

    lax.fori_loop(0, rows // 2, forward, 0)
    chip = jnp.bitwise_xor(place[0], step)
    d_out = jnp.concatenate([flat(d_here[chip]), flat(d_there[chip])], axis=0)
    normed, scale = norm(x[...])
    out = dot(normed, w_out[...])
    out_here[...] = out[: rows * half].reshape(rows, half, -1)
    out_there[...] = out[rows * half :].reshape(rows, half, -1)
    d_normed = dot_t(d_out, w_out[...])
    mean_one = jnp.mean(d_normed, axis=-1, keepdims=True)
    mean_two = jnp.mean(d_normed * normed, axis=-1, keepdims=True)
    d_x[...] = (d_normed - mean_one - normed * mean_two) * scale
    wide = 2 * GROUP

    def backward(at, _):
        here = pl.ds(pl.multiple_of(at * wide, wide), wide)

        def add(block, totals):
            totals = list(totals)
            for u in range(GROUP):
                for which, left in enumerate((left_here, left_there)):
                    i = block * GROUP + u
                    value = left[i, here, :]
                    for j in range(half):
                        totals[j] = totals[j] + value * d_x[pl.ds((which * rows + i) * half + j, 1), :]
            return tuple(totals)

        totals = lax.fori_loop(0, rows // GROUP, add, (jnp.zeros((wide, chans), F32),) * half)
        for j in range(half):
            d_right[j, here, :] = totals[j]
        return 0

    lax.fori_loop(0, cols // wide, backward, 0)


def tile_kernel(step, parts, place, *refs):
    rights, rest = refs[:parts], refs[parts:]
    if parts == 2:
        sum_out = rest[9]
        sum_out[...] = rights[0][...] + rights[1][...]
        tile_body(step, place, sum_out, *rest[:9], *rest[10:])
    else:
        tile_body(step, place, rights[0], *rest)


def left_rows(tiles, base, out, first, count, start):
    half, cols, chans = tiles[0][0].shape

    def body(pair_at, _):
        i = pair_at * 2
        totals = [jnp.zeros((cols, chans), F32)] * 2 if base is None else [base[start + i], base[start + i + 1]]
        for right, d_x in tiles:
            for j in range(half):
                value = right[j]
                for u in range(2):
                    totals[u] = totals[u] + value * d_x[pl.ds((first + i + u) * half + j, 1), :]
        out[start + i] = totals[0]
        out[start + i + 1] = totals[1]
        return 0

    lax.fori_loop(0, count // 2, body, 0)


def left_kernel(tiles, based, place, *refs):
    pairs = tuple(zip(refs[:tiles], refs[tiles : 2 * tiles]))
    bases = refs[2 * tiles : 2 * tiles + 2] if based else (None, None)
    rows = refs[-1].shape[0]
    for which, out in enumerate(refs[-2:]):
        left_rows(pairs, bases[which], out, which * rows, rows, 0)


def last_tile_kernel(step, place, one, two, left_here, left_there, d_here, d_there, w_out, there, out_next, *refs):
    out_here, out_there, d_x, d_right, right, sent, partial, x = refs
    rows = there.shape[0]
    right[...] = one[...] + two[...]
    tile_body(step, place, right, left_here, left_there, d_here, d_there, w_out, out_here, out_there, d_x, d_right, partial, x)
    left_rows(((right, d_x),), there, sent, rows, rows, 0)
    sent[rows] = flat(out_next[...])
    sent[rows + 1] = flat(out_there[...])


def last_kept_kernel(place, right, d_x, here, kept):
    left_rows(((right, d_x),), here, kept, 0, here.shape[0], 0)


def share_kernel(cuts, place, kept, received, out_next, out_last, d_left, *packed):
    half = d_left.shape[0]
    block = half * half
    d_left[...] = kept[:half] + received[:half]
    for first, last, part in zip(cuts, cuts[1:], packed):
        at = slice(half + first, half + last)
        part[: last - first] = kept[at] + received[at]
    early, late = packed[0], packed[-1]
    for step, out in enumerate((out_next, out_last)):
        at = slice(step * block, (step + 1) * block)
        plane = 2 * half + step
        early[early.shape[0] - 2, at] = flat(out[half:])
        early[early.shape[0] - 1, at] = received[plane, block:]
        late[late.shape[0] - 2, at] = flat(out[:half])
        late[late.shape[0] - 1, at] = received[plane, :block]


def gather_out(place, rows, t, count, start, out, here, early_other, early_far, received, far):
    half = rows // 2
    block = half * half
    for far_half in (0, 1):
        source = (t + far_half * half) % rows
        at, wide = slice(source, source + count), slice(source * half, (source + count) * half)
        for far_core in (0, 1):
            core = place[1] + far_core * (1 - 2 * place[1])
            side = place[2] + far_half * (1 - 2 * place[2])
            for step in range(4):
                chip = jnp.bitwise_xor(place[0], step)
                first = pl.multiple_of(chip * 2 * rows + core * rows + side * half, half)
                if far_half:
                    if step < 2:
                        value = early_far[far_core, step, at]
                    else:
                        begin = (step - 2) * block + (t % half) * half
                        value = far[far.shape[0] - 2 + far_core, begin : begin + count * half].reshape(count, half, -1)
                elif far_core:
                    if step < 2:
                        value = early_other[step, at]
                    else:
                        value = received[rows + step - 2, wide].reshape(count, half, -1)
                else:
                    value = here[step][at]
                out[start : start + count, pl.ds(first, half), :] = value


def update_kernel(rows, place, *refs):
    here, early_other, early_far, received, far, far_next, gate, update, out = refs[:4], *refs[4:]
    half = rows // 2
    gather_out(place, rows, 0, half, 0, out, here, early_other, early_far, received, far)
    gather_out(place, rows, half, half, half, out, here, early_other, early_far, received, far_next)
    for t in range(0, rows, CHUNK):
        update[pl.ds(source_row(place, t, rows), CHUNK)] = gate[t : t + CHUNK] * out[t : t + CHUNK]


def base_kernel(rows, t, place, *refs):
    here, early_other, early_far, received, far, far_rows = refs[:4], *refs[4:9]
    gate, cotangent, w_gate, d_left, open_part, slope, mine, other, base, out = refs[9:]
    count, cols, chans = base.shape
    gather_out(place, rows, t, count, 0, out, here, early_other, early_far, received, far)
    w = gated_weights(place, mine, other, 0)
    at = slice(t, t + count)
    opened = gate[at]
    d_gate = cotangent[pl.ds(source_row(place, t, rows), count)] * (opened * out[...]) * (1.0 - opened)
    grad = flat(d_left[at] + far_rows[:count])
    both = jnp.concatenate([grad * flat(open_part[at]), grad * flat(slope[at])], axis=1)
    base[...] = (dot_t(flat(d_gate), w_gate[...]) + dot(both, w)).reshape(count, cols, -1)


def pair_kernel(first, place, normed, scale, base, d_right, d_right_near, d_right_across, open_part, slope, mine, other, d_mine):
    count, cols, chans = d_mine.shape
    w = gated_weights(place, mine, other, 2)
    at = slice(first, first + count)
    grad = flat(d_right[at] + d_right_near[...] + d_right_across[...])
    both = jnp.concatenate([grad * flat(open_part[at]), grad * flat(slope[at])], axis=1)
    d_normed = flat(base[...]) + dot(both, w)
    value = flat(normed[at])
    mean_grad = jnp.mean(d_normed, axis=-1, keepdims=True)
    mean_cross = jnp.mean(d_normed * value, axis=-1, keepdims=True)
    d_mine[...] = ((d_normed - mean_grad - value * mean_cross) * flat(scale[at])).reshape(count, cols, -1)


def join_kernel(firsts, sides, *refs):
    blocks, whole, sems = refs[: len(firsts)], refs[-2], refs[-1]
    side = lax.axis_index("ch")
    half = whole.shape[0] // 2
    copies = []
    for at, (block, first, mine) in enumerate(zip(blocks, firsts, sides)):
        start = (side if mine else 1 - side) * half + first
        copies.append(pltpu.make_async_copy(block, whole.at[pl.ds(start, block.shape[0])], sems.at[at]))
    for copy in copies:
        copy.start()
    for copy in copies:
        copy.wait()


def join(blocks, firsts, sides, shape, whole=None):
    anywhere = pl.BlockSpec(memory_space=pl.ANY)
    vmem = pl.BlockSpec(memory_space=pltpu.VMEM)
    given = [] if whole is None else [whole]
    return pl.pallas_call(
        functools.partial(join_kernel, firsts, sides),
        out_shape=jax.ShapeDtypeStruct(shape, F32),
        in_specs=[vmem] * len(blocks) + [anywhere] * len(given),
        out_specs=anywhere,
        input_output_aliases={len(blocks): 0} if given else {},
        scratch_shapes=[pltpu.SemaphoreType.DMA((len(blocks),))],
        compiler_params=pltpu.CompilerParams(vmem_limit_bytes=2 * 1024 * 1024),
    )(*blocks, *given)


def along(block, pairs):
    return lax.ppermute(block, "row", [(2 * a + core, 2 * b + core) for a, b in pairs for core in (0, 1)])


def other_core(block):
    return lax.ppermute(block, "row", [(i, i ^ 1) for i in range(lax.axis_size("row"))])


def other_half(block):
    return lax.ppermute(block, "ch", [(0, 1), (1, 0)])


NEXT = [(0, 1), (1, 0), (2, 3), (3, 2)]
MIDDLE = [(1, 2), (2, 1)]
OUTWARD = [(1, 0), (2, 3)]
INWARD = [(0, 1), (3, 2)]
ACROSS = [(0, 3), (3, 0), (1, 2), (2, 1)]


def on_tiles(pair, pair_mask, w_proj, w_gate, w_out, cotangent):
    rows, cols, width = pair.shape
    half = rows // 2
    chips = cols // (2 * rows)
    chans = 2 * w_out.shape[0]
    row, side = lax.axis_index("row"), lax.axis_index("ch")
    place = jnp.stack([row // 2, row % 2, side]).astype(jnp.int32)

    w_mine = jnp.swapaxes(w_proj, 1, 2)
    other = other_half(flat(w_mine)).reshape(w_mine.shape)
    kept = (half, cols, chans)
    other_out = other_half(w_out)
    normed, scale, keep, mine, *sent = call(
        first_kernel,
        [(half, cols, width)] * 2 + [(rows, cols), w_mine.shape] + [(half, cols, width)] * 2,
        (place, pair, pair_mask, w_mine),
        scratch=[((rows, cols), jnp.int32)],
        distant=3,
        sems=4,
    )
    theirs = [other_core(block) for block in sent]
    right, open_right, slope_right = call(
        functools.partial(right_kernel, rows), [kept] * 3, (place, normed, keep, mine, other)
    )
    right, other_out = lax.optimization_barrier((right, other_out))
    near = along(right, NEXT)
    middle = along(right, MIDDLE)
    _, cotangent_late = lax.optimization_barrier((right, cotangent))
    (third,) = call(
        third_kernel, [(chips + 1, rows, half, width)], (place, cotangent_late, keep), distant=1, sems=chips
    )
    theirs.append(other_core(third))
    quarter = (chips, rows, half, width)
    tile_outs = [(rows, half, width)] * 2 + [(2 * rows * half, chans), kept]
    tile_scratch = [(4, half * GROUP, chans), (2 * rows * half, chans)]
    out_here, out_there, d_x, d_right, rights = ([None] * 4 for _ in range(5))
    rights[0] = right
    left, left_there, open_left, slope_left, gate, d_here, d_there, w_all_out = call(
        functools.partial(prepare_kernel, rows),
        [(rows, cols, chans)] * 2 + [kept] * 2 + [(rows, cols, width), quarter, quarter, (chans, width)],
        (place, pair, keep, cotangent, *theirs, mine, other, w_gate, w_out, other_out),
        scratch=[(CHUNK, cols, width)],
    )

    def tile(step, *blocks):
        got = call(
            functools.partial(tile_kernel, step, len(blocks)),
            tile_outs + ([kept] if len(blocks) == 2 else []),
            (place, *blocks, left, left_there, d_here, d_there, w_all_out),
            scratch=tile_scratch,
        )
        out_here[step], out_there[step], d_x[step], d_right[step] = got[:4]
        rights[step] = got[4] if len(blocks) == 2 else blocks[0]

    near, d_here = lax.optimization_barrier((near, d_here))
    cross = along(near, MIDDLE)
    outer = along(middle, OUTWARD)
    tile(0, right)
    tile(1, near)
    early_other = other_core(jnp.stack(out_there[:2]))
    d_left_here, d_left_there = call(
        functools.partial(left_kernel, 1, False), [(rows, cols, chans)] * 2, (place, rights[0], d_x[0])
    )
    cross, early_other, d_left_here = lax.optimization_barrier((cross, early_other, d_left_here))
    far = along(cross, OUTWARD)
    early_far = other_half(jnp.stack([jnp.stack(out_here[:2]), early_other]))
    tile(2, cross, outer)
    inward = along(d_right[2], INWARD)
    swapped = along(d_right[2], MIDDLE)
    d_left_here, d_left_there = call(
        functools.partial(left_kernel, 2, True),
        [(rows, cols, chans)] * 2,
        (place, *rights[1:3], *d_x[1:3], d_left_here, d_left_there),
    )
    far, d_left_here = lax.optimization_barrier((far, d_left_here))
    out_here[3], out_there[3], d_x[3], d_right[3], rights[3], d_left_sent = call(
        functools.partial(last_tile_kernel, 3),
        tile_outs + [kept, (rows + 2, cols, chans)],
        (place, middle, far, left, left_there, d_here, d_there, w_all_out, d_left_there, out_there[2]),
        scratch=tile_scratch,
    )
    cuts = [half * eighths // 8 for eighths in CUTS]
    spans = list(zip(cuts, cuts[1:]))
    swapped, to_across = lax.optimization_barrier((swapped, d_right[3] + inward))
    to_across, to_near, early_far, d_left_sent = lax.optimization_barrier(
        (to_across, d_right[1] + swapped, early_far, d_left_sent)
    )
    from_across, from_near = [along(to_across[: cuts[1]], ACROSS)], [along(to_near[: cuts[1]], NEXT)]
    received = other_core(d_left_sent)
    _, d_left_here = lax.optimization_barrier((d_left_sent, d_left_here))
    (d_left_kept,) = call(last_kept_kernel, [(rows, cols, chans)], (place, rights[3], d_x[3], d_left_here))
    sizes = [last - first for first, last in spans]
    sizes[0] += 2
    sizes[-1] += 2
    d_left, *packed = call(
        functools.partial(share_kernel, cuts),
        [kept] + [(size, cols, chans) for size in sizes],
        (place, d_left_kept, received, out_here[2], out_here[3]),
    )
    far_parts = [other_half(block) for block in packed]
    for first, last in spans[1:]:
        from_near.append(along(to_near[first:last], NEXT))
        from_across[-1], last_across = lax.optimization_barrier((from_across[-1], to_across[first:last]))
        from_across.append(along(last_across, ACROSS))
    outs = (*out_here, early_other, early_far, received)
    mine_parts, other_parts = [], []
    for at, (first, last) in enumerate(spans):
        (base,) = call(
            functools.partial(base_kernel, rows, first),
            [(last - first, cols, width)],
            (place, *outs, far_parts[0], far_parts[at], gate, cotangent, w_gate, d_left, open_left, slope_left, mine, other),
            scratch=[(last - first, cols, width)],
        )
        if at:
            base, mine_parts[-1] = lax.optimization_barrier((base, mine_parts[-1]))
        (rows_done,) = call(
            functools.partial(pair_kernel, first),
            [(last - first, cols, width)],
            (place, normed, scale, base, d_right[0], from_near[at], from_across[at], open_right, slope_right, mine, other),
        )
        mine_parts.append(rows_done)
        other_parts.append(other_half(rows_done))
    _, gate_late = lax.optimization_barrier((mine_parts[-1], gate))
    (update,) = call(
        functools.partial(update_kernel, rows),
        [(rows, cols, width)],
        (place, *outs, far_parts[0], far_parts[-1], gate_late),
        scratch=[(rows, cols, width)],
    )
    d_pair = join(mine_parts, cuts[:-1], (True,) * len(spans), pair.shape)
    d_pair, update = lax.optimization_barrier((d_pair, update))
    for first, part in zip(cuts, other_parts):
        d_pair, part = lax.optimization_barrier((d_pair, part))
        d_pair = join([part], (first,), (False,), pair.shape, d_pair)
    return (update, d_pair)


def passed_along(block, axis, distance):
    devices = range(lax.axis_size(axis))
    route = [((i - distance) % len(devices), i) for i in devices]
    return lax.ppermute(block, axis, route)


def normalize(values):
    mean = jnp.mean(values, axis=-1, keepdims=True)
    centered = values - mean
    variance = jnp.mean(centered * centered, axis=-1, keepdims=True)
    scale = lax.rsqrt(variance + 1e-05)
    return (centered * scale, scale)


def on_ring(pair, pair_mask, w_proj, w_gate, w_out, cotangent):
    highest = lax.Precision.HIGHEST
    normed, pair_scale = normalize(pair)
    proj = jnp.einsum("rqz,pzc->pcrq", normed, w_proj, precision=highest)
    keep = pair_mask.astype(jnp.float32)
    sig_left = jax.nn.sigmoid(proj[1])
    sig_right = jax.nn.sigmoid(proj[3])
    left = keep * sig_left * proj[0]
    right = keep * sig_right * proj[2]
    chans, rows, cols = left.shape
    count = lax.axis_size("row")
    here = lax.axis_index("row")

    def visit(step, carry):
        block, store, partial_value = carry
        source = (here - step) % count
        store = lax.dynamic_update_slice_in_dim(store, block, source * rows, 1)
        product = jnp.einsum("cik,cjk->cij", left, block, precision=highest)
        partial_value = lax.dynamic_update_slice_in_dim(partial_value, product, source * rows, 2)
        block = passed_along(block, "row", 1)
        return (block, store, partial_value)

    store = jnp.zeros((chans, rows * count, cols), jnp.float32)
    partial_value = jnp.zeros((chans, rows, rows * count), jnp.float32)
    block, store, partial_value = lax.fori_loop(0, count - 1, visit, (right, store, partial_value))
    source = (here + 1) % count
    right_all = lax.dynamic_update_slice_in_dim(store, block, source * rows, 1)
    product = jnp.einsum("cik,cjk->cij", left, block, precision=highest)
    partial_value = lax.dynamic_update_slice_in_dim(partial_value, product, source * rows, 2)
    mixed = lax.psum_scatter(partial_value, "sub", scatter_dimension=2, tiled=True)
    first = jnp.sum(mixed, axis=0)
    second = jnp.sum(mixed * mixed, axis=0)
    projected = jnp.einsum("crq,cd->rqd", mixed, w_out, precision=highest)
    col_total = jnp.sum(w_out, axis=0)
    projected, first, second, col_total = lax.psum((projected, first, second, col_total), "ch")
    center = first / C
    spread = lax.rsqrt(second / C - center * center + 1e-05)
    outgoing = (projected - center[..., None] * col_total) * spread[..., None]
    gate = jax.nn.sigmoid(jnp.einsum("rqz,zd->rqd", normed, w_gate, precision=highest))
    update = gate * outgoing
    d_outgoing = cotangent * gate
    d_gate_pre = cotangent * outgoing * gate * (1.0 - gate)
    d_mixed_norm = jnp.einsum("rqd,cd->crq", d_outgoing, w_out, precision=highest)
    mean_one = jnp.sum(d_outgoing * col_total, axis=-1) / C
    mean_two = jnp.sum(d_outgoing * outgoing, axis=-1) / C
    mixed_norm = (mixed - center) * spread
    d_mixed = (d_mixed_norm - mean_one - mixed_norm * mean_two) * spread
    d_mixed_full = lax.all_gather(d_mixed, "sub", axis=2, tiled=True)
    d_left = jnp.einsum("cij,cjk->cik", d_mixed_full, right_all, precision=highest)
    d_right = jnp.transpose(
        lax.psum_scatter(
            jnp.einsum("cij,cik->jck", d_mixed_full, left, precision=highest),
            "row",
            scatter_dimension=0,
            tiled=True,
        ),
        (1, 0, 2),
    )
    d_proj = jnp.stack(
        [
            d_left * keep * sig_left,
            d_left * keep * proj[0] * sig_left * (1.0 - sig_left),
            d_right * keep * sig_right,
            d_right * keep * proj[2] * sig_right * (1.0 - sig_right),
        ]
    )
    d_normed_part = jnp.einsum("pcrq,pzc->rqz", d_proj, w_proj, precision=highest)
    d_normed = lax.psum(d_normed_part, "ch")
    d_normed = d_normed + jnp.einsum("rqd,zd->rqz", d_gate_pre, w_gate, precision=highest)
    mean_grad = jnp.mean(d_normed, axis=-1, keepdims=True)
    mean_cross = jnp.mean(d_normed * normed, axis=-1, keepdims=True)
    d_pair = (d_normed - mean_grad - normed * mean_cross) * pair_scale
    return (update, d_pair)


def solution(mesh):
    sizes = mesh.shape
    tiled = sizes["row"] == 8 and sizes["ch"] == 2 and sizes["sub"] == 1
    return jax.shard_map(
        on_tiles if tiled else on_ring,
        mesh=mesh,
        in_specs=(
            P(("grp", "row"), "sub", None),
            P(("grp", "row"), "sub"),
            P(None, None, "ch"),
            P(),
            P("ch", None),
            P(("grp", "row"), "sub", None),
        ),
        out_specs=(P(("grp", "row"), "sub", None), P(("grp", "row"), "sub", None)),
        check_vma=False,
    )
```

```python
import functools
import jax
import jax.numpy as jnp
from jax import lax
from jax.experimental import pallas as pl
from jax.experimental.pallas import tpu as pltpu
from jax.sharding import PartitionSpec as P

C = 128
EPS = 1e-05
F32 = jnp.float32
CHUNK = 4
CUTS = (0, 4, 8)
GROUP = 8


def halves(values):
    high = values.astype(jnp.bfloat16)
    return high, (values - high.astype(F32)).astype(jnp.bfloat16)


def contract(a, b, dims):
    (a_high, a_low), (b_high, b_low) = halves(a), halves(b)
    one = lambda x, y: lax.dot_general(x, y, (dims, ((), ())), preferred_element_type=F32)
    return one(a_high, b_high) + (one(a_high, b_low) + one(a_low, b_high))


def dot(a, b):
    return contract(a, b, ((1,), (0,)))


def dot_t(a, b):
    return contract(a, b, ((1,), (1,)))


def norm(values):
    mean = jnp.mean(values, axis=-1, keepdims=True)
    centered = values - mean
    variance = jnp.mean(centered * centered, axis=-1, keepdims=True)
    scale = lax.rsqrt(variance + EPS)
    return (centered * scale, scale)


def flat(values):
    return values.reshape(-1, values.shape[-1])


def call(kernel, outs, args, scratch=(), distant=0, sems=0):
    vmem = pl.BlockSpec(memory_space=pltpu.VMEM)
    spaces = [pl.BlockSpec(memory_space=pltpu.SMEM)] + [pl.BlockSpec(memory_space=pltpu.HBM)] * distant
    args = list(args)
    args[1 : 1 + distant] = [pltpu.with_memory_space_constraint(a, pltpu.HBM) for a in args[1 : 1 + distant]]
    return pl.pallas_call(
        kernel,
        out_shape=[jax.ShapeDtypeStruct(shape, F32) for shape in outs],
        in_specs=spaces + [vmem] * (len(args) - len(spaces)),
        out_specs=[vmem] * len(outs),
        scratch_shapes=[pltpu.VMEM(*shape) if isinstance(shape[0], tuple) else pltpu.VMEM(shape, F32) for shape in scratch]
        + ([pltpu.SemaphoreType.DMA((sems,))] if sems else []),
        compiler_params=pltpu.CompilerParams(vmem_limit_bytes=24 * 1024 * 1024),
        cost_estimate=pl.CostEstimate(flops=1000, bytes_accessed=1000, transcendentals=0),
    )(*args)


def source_row(place, t, rows):
    half = rows // 2
    if t < half:
        return place[2] * half + t
    return (1 - place[2]) * half + t - half


def first_col(place, chip, core, rows):
    half = rows // 2
    return pl.multiple_of(chip * 2 * rows + core * rows + place[2] * half, half)


def both_halves(place, mine, other):
    first = place[2] == 0
    a, b = jnp.where(first, mine, other), jnp.where(first, other, mine)
    return jnp.concatenate([a, b], axis=0)


def gated_weights(place, mine, other, which):
    return jnp.concatenate([both_halves(place, mine[p], other[p]) for p in (which, which + 1)], axis=0)


def gated(normed, keep_rows, w):
    count = keep_rows.shape[0]
    chans = w.shape[0] // 2
    spread = jnp.transpose(jnp.concatenate([keep_rows] * (8 // count), axis=0))
    keep = jnp.concatenate([spread[:, u : u + 1] for u in range(count)], axis=0)
    proj = dot_t(normed, w)
    sig = jax.nn.sigmoid(proj[:, chans:]) * keep
    return sig * proj[:, :chans], sig


def first_kernel(place, pair, mask, w_proj, normed, scale, keep, mine, first, second, flags, sems):
    half = first.shape[0]
    moves = ((pair.at[:half], first), (pair.at[half:], second), (mask, flags), (w_proj, mine))
    copies = [pltpu.make_async_copy(source, target, sems.at[at]) for at, (source, target) in enumerate(moves)]
    for copy in copies:
        copy.start()
    for copy in copies:
        copy.wait()
    keep[...] = flags[...].astype(F32)
    for t in range(0, half, CHUNK):
        at = slice(t, t + CHUNK)
        value, factor = norm(jnp.where(place[2] == 0, first[at], second[at]))
        normed[at] = value
        scale[at] = jnp.broadcast_to(factor, value.shape)


def third_kernel(place, cotangent, keep, packed, sems):
    rows = cotangent.shape[0]
    half, chips = rows // 2, packed.shape[0] - 1
    copies = []
    for chip in range(chips):
        source = cotangent.at[:, pl.ds(first_col(place, chip, 1 - place[1], rows), half), :]
        copies.append(pltpu.make_async_copy(source, packed.at[chip], sems.at[chip]))
    for copy in copies:
        copy.start()
    packed[chips, :, 0, :] = keep[...]
    for copy in copies:
        copy.wait()


def right_kernel(rows, place, normed, keep, mine, other, right, open_part, slope):
    half, cols, chans = right.shape
    w = gated_weights(place, mine, other, 2)
    for t in range(0, half, CHUNK):
        at = slice(t, t + CHUNK)
        value, sig = gated(flat(normed[at]), keep[pl.ds(source_row(place, t, rows), CHUNK), :], w)
        shape = (CHUNK, cols, chans)
        right[at] = value.reshape(shape)
        open_part[at] = sig.reshape(shape)
        slope[at] = (value * (1.0 - sig)).reshape(shape)


def prepare_kernel(rows, place, pair, keep, cotangent, first, second, third, mine, other, w_gate, mine_out, other_out, *refs):
    left_here, left_there, open_part, slope, gate, d_here, d_there, w_out, normed_rows = refs
    half, cols, chans = open_part.shape
    chips = cols // (2 * rows)
    shape = (CHUNK, cols, chans)
    w = gated_weights(place, mine, other, 0)
    w_out[...] = both_halves(place, mine_out[...], other_out[...])
    for t in range(0, rows, CHUNK):
        row = source_row(place, t, rows)
        at = slice(t, t + CHUNK)
        normed, _ = norm(flat(pair[pl.ds(row, CHUNK)]))
        value, sig = gated(normed, keep[pl.ds(row, CHUNK), :], w)
        left_here[at] = value.reshape(shape)
        if t < half:
            open_part[at] = sig.reshape(shape)
            slope[at] = (value * (1.0 - sig)).reshape(shape)
        gate[at] = jax.nn.sigmoid(dot(normed, w_gate[...])).reshape(CHUNK, cols, -1)
        for chip in range(chips):
            near = pl.ds(first_col(place, chip, place[1], rows), half)
            d_here[chip, at] = gate[at, near, :] * cotangent[pl.ds(row, CHUNK), near, :]
        their_row = row % half
        normed, _ = norm(flat(jnp.where(row < half, first[pl.ds(their_row, CHUNK)], second[pl.ds(their_row, CHUNK)])))
        value, _ = gated(normed, third[chips, pl.ds(row, CHUNK), 0, :], w)
        left_there[at] = value.reshape(shape)
        normed_rows[...] = normed.reshape(CHUNK, cols, -1)
        picked = [
            normed_rows[:, pl.ds(first_col(place, chip, place[1], rows), half), :] for chip in range(chips)
        ]
        opened = jax.nn.sigmoid(dot(flat(jnp.stack(picked)), w_gate[...])).reshape(chips, CHUNK, half, -1)
        for chip in range(chips):
            d_there[chip, at] = opened[chip] * third[chip, pl.ds(row, CHUNK)]


def tile_body(step, place, right, left_here, left_there, d_here, d_there, w_out, out_here, out_there, d_x, d_right, partial, x):
    rows = left_here.shape[0]
    half, cols, chans = right.shape
    groups = cols // GROUP

    def forward(pair_at, _):
        for which, left in enumerate((left_here, left_there)):
            i = pair_at * 2
            value = [left[i], left[i + 1]]
            for j in range(half):
                block = right[j]
                for u in range(2):
                    product = (value[u] * block).reshape(groups, GROUP, chans)
                    partial[2 * which + u, j * GROUP : (j + 1) * GROUP] = jnp.sum(product, axis=0)
            for u in range(2):
                total = partial[2 * which + u, pl.ds(0, half, stride=GROUP), :]
                for s in range(1, GROUP):
                    total = total + partial[2 * which + u, pl.ds(s, half, stride=GROUP), :]
                x[pl.ds(pl.multiple_of((which * rows + i + u) * half, half), half), :] = total
        return 0

    lax.fori_loop(0, rows // 2, forward, 0)
    chip = jnp.bitwise_xor(place[0], step)
    d_out = jnp.concatenate([flat(d_here[chip]), flat(d_there[chip])], axis=0)
    normed, scale = norm(x[...])
    out = dot(normed, w_out[...])
    out_here[...] = out[: rows * half].reshape(rows, half, -1)
    out_there[...] = out[rows * half :].reshape(rows, half, -1)
    d_normed = dot_t(d_out, w_out[...])
    mean_one = jnp.mean(d_normed, axis=-1, keepdims=True)
    mean_two = jnp.mean(d_normed * normed, axis=-1, keepdims=True)
    d_x[...] = (d_normed - mean_one - normed * mean_two) * scale
    wide = 2 * GROUP

    def backward(at, _):
        here = pl.ds(pl.multiple_of(at * wide, wide), wide)

        def add(block, totals):
            totals = list(totals)
            for u in range(GROUP):
                for which, left in enumerate((left_here, left_there)):
                    i = block * GROUP + u
                    value = left[i, here, :]
                    for j in range(half):
                        totals[j] = totals[j] + value * d_x[pl.ds((which * rows + i) * half + j, 1), :]
            return tuple(totals)

        totals = lax.fori_loop(0, rows // GROUP, add, (jnp.zeros((wide, chans), F32),) * half)
        for j in range(half):
            d_right[j, here, :] = totals[j]
        return 0

    lax.fori_loop(0, cols // wide, backward, 0)


def tile_kernel(step, parts, place, *refs):
    rights, rest = refs[:parts], refs[parts:]
    if parts == 2:
        sum_out = rest[9]
        sum_out[...] = rights[0][...] + rights[1][...]
        tile_body(step, place, sum_out, *rest[:9], *rest[10:])
    else:
        tile_body(step, place, rights[0], *rest)


def left_rows(tiles, base, out, first, count, start):
    half, cols, chans = tiles[0][0].shape

    def body(pair_at, _):
        i = pair_at * 2
        totals = [jnp.zeros((cols, chans), F32)] * 2 if base is None else [base[start + i], base[start + i + 1]]
        for right, d_x in tiles:
            for j in range(half):
                value = right[j]
                for u in range(2):
                    totals[u] = totals[u] + value * d_x[pl.ds((first + i + u) * half + j, 1), :]
        out[start + i] = totals[0]
        out[start + i + 1] = totals[1]
        return 0

    lax.fori_loop(0, count // 2, body, 0)


def left_kernel(tiles, based, place, *refs):
    pairs = tuple(zip(refs[:tiles], refs[tiles : 2 * tiles]))
    bases = refs[2 * tiles : 2 * tiles + 2] if based else (None, None)
    rows = refs[-1].shape[0]
    for which, out in enumerate(refs[-2:]):
        left_rows(pairs, bases[which], out, which * rows, rows, 0)


def last_tile_kernel(step, place, one, two, left_here, left_there, d_here, d_there, w_out, there, out_next, *refs):
    out_here, out_there, d_x, d_right, right, sent, partial, x = refs
    rows = there.shape[0]
    right[...] = one[...] + two[...]
    tile_body(step, place, right, left_here, left_there, d_here, d_there, w_out, out_here, out_there, d_x, d_right, partial, x)
    left_rows(((right, d_x),), there, sent, rows, rows, 0)
    sent[rows] = flat(out_next[...])
    sent[rows + 1] = flat(out_there[...])


def last_kept_kernel(place, right, d_x, here, kept):
    left_rows(((right, d_x),), here, kept, 0, here.shape[0], 0)


def share_kernel(cuts, place, kept, received, out_next, out_last, d_left, *packed):
    half = d_left.shape[0]
    block = half * half
    d_left[...] = kept[:half] + received[:half]
    for first, last, part in zip(cuts, cuts[1:], packed):
        at = slice(half + first, half + last)
        part[: last - first] = kept[at] + received[at]
    early, late = packed[0], packed[-1]
    for step, out in enumerate((out_next, out_last)):
        at = slice(step * block, (step + 1) * block)
        plane = 2 * half + step
        early[early.shape[0] - 2, at] = flat(out[half:])
        early[early.shape[0] - 1, at] = received[plane, block:]
        late[late.shape[0] - 2, at] = flat(out[:half])
        late[late.shape[0] - 1, at] = received[plane, :block]


def gather_out(place, rows, t, count, start, out, here, early_other, early_far, received, far):
    half = rows // 2
    block = half * half
    for far_half in (0, 1):
        source = (t + far_half * half) % rows
        at, wide = slice(source, source + count), slice(source * half, (source + count) * half)
        for far_core in (0, 1):
            core = place[1] + far_core * (1 - 2 * place[1])
            side = place[2] + far_half * (1 - 2 * place[2])
            for step in range(4):
                chip = jnp.bitwise_xor(place[0], step)
                first = pl.multiple_of(chip * 2 * rows + core * rows + side * half, half)
                if far_half:
                    if step < 2:
                        value = early_far[far_core, step, at]
                    else:
                        begin = (step - 2) * block + (t % half) * half
                        value = far[far.shape[0] - 2 + far_core, begin : begin + count * half].reshape(count, half, -1)
                elif far_core:
                    if step < 2:
                        value = early_other[step, at]
                    else:
                        value = received[rows + step - 2, wide].reshape(count, half, -1)
                else:
                    value = here[step][at]
                out[start : start + count, pl.ds(first, half), :] = value


def update_kernel(rows, place, *refs):
    here, early_other, early_far, received, far, far_next, gate, update, out = refs[:4], *refs[4:]
    half = rows // 2
    gather_out(place, rows, 0, half, 0, out, here, early_other, early_far, received, far)
    gather_out(place, rows, half, half, half, out, here, early_other, early_far, received, far_next)
    for t in range(0, rows, CHUNK):
        update[pl.ds(source_row(place, t, rows), CHUNK)] = gate[t : t + CHUNK] * out[t : t + CHUNK]


def base_kernel(rows, t, place, *refs):
    here, early_other, early_far, received, far, far_rows = refs[:4], *refs[4:9]
    gate, cotangent, w_gate, d_left, open_part, slope, mine, other, base, out = refs[9:]
    count, cols = base.shape[:2]
    gather_out(place, rows, t, count, 0, out, here, early_other, early_far, received, far)
    w = gated_weights(place, mine, other, 0)
    at = slice(t, t + count)
    opened = gate[at]
    d_gate = cotangent[pl.ds(source_row(place, t, rows), count)] * (opened * out[...]) * (1.0 - opened)
    grad = flat(d_left[at] + far_rows[:count])
    both = jnp.concatenate([grad * flat(open_part[at]), grad * flat(slope[at])], axis=1)
    base[...] = (dot_t(flat(d_gate), w_gate[...]) + dot(both, w)).reshape(count, cols, -1)


def pair_kernel(first, place, normed, scale, base, d_right, d_right_near, d_right_across, open_part, slope, mine, other, d_mine):
    count, cols = d_mine.shape[:2]
    w = gated_weights(place, mine, other, 2)
    at = slice(first, first + count)
    grad = flat(d_right[at] + d_right_near[...] + d_right_across[...])
    both = jnp.concatenate([grad * flat(open_part[at]), grad * flat(slope[at])], axis=1)
    d_normed = flat(base[...]) + dot(both, w)
    value = flat(normed[at])
    mean_grad = jnp.mean(d_normed, axis=-1, keepdims=True)
    mean_cross = jnp.mean(d_normed * value, axis=-1, keepdims=True)
    d_mine[...] = ((d_normed - mean_grad - value * mean_cross) * flat(scale[at])).reshape(count, cols, -1)


def join_kernel(firsts, sides, *refs):
    blocks, whole, sems = refs[: len(firsts)], refs[-2], refs[-1]
    side = lax.axis_index("ch")
    half = whole.shape[0] // 2
    copies = []
    for at, (block, first, mine) in enumerate(zip(blocks, firsts, sides)):
        start = (side if mine else 1 - side) * half + first
        copies.append(pltpu.make_async_copy(block, whole.at[pl.ds(start, block.shape[0])], sems.at[at]))
    for copy in copies:
        copy.start()
    for copy in copies:
        copy.wait()


def join(blocks, firsts, sides, shape, whole=None):
    anywhere = pl.BlockSpec(memory_space=pl.ANY)
    vmem = pl.BlockSpec(memory_space=pltpu.VMEM)
    given = [] if whole is None else [whole]
    return pl.pallas_call(
        functools.partial(join_kernel, firsts, sides),
        out_shape=jax.ShapeDtypeStruct(shape, F32),
        in_specs=[vmem] * len(blocks) + [anywhere] * len(given),
        out_specs=anywhere,
        input_output_aliases={len(blocks): 0} if given else {},
        scratch_shapes=[pltpu.SemaphoreType.DMA((len(blocks),))],
        compiler_params=pltpu.CompilerParams(vmem_limit_bytes=2 * 1024 * 1024),
    )(*blocks, *given)


def along(block, pairs):
    return lax.ppermute(block, "row", [(2 * a + core, 2 * b + core) for a, b in pairs for core in (0, 1)])


def other_core(block):
    return lax.ppermute(block, "row", [(i, i ^ 1) for i in range(lax.axis_size("row"))])


def other_half(block):
    return lax.ppermute(block, "ch", [(0, 1), (1, 0)])


NEXT = [(0, 1), (1, 0), (2, 3), (3, 2)]
MIDDLE = [(1, 2), (2, 1)]
OUTWARD = [(1, 0), (2, 3)]
INWARD = [(0, 1), (3, 2)]
ACROSS = [(0, 3), (3, 0), (1, 2), (2, 1)]


def on_tiles(pair, pair_mask, w_proj, w_gate, w_out, cotangent):
    rows, cols, width = pair.shape
    half = rows // 2
    chips = cols // (2 * rows)
    chans = 2 * w_out.shape[0]
    row, side = lax.axis_index("row"), lax.axis_index("ch")
    place = jnp.stack([row // 2, row % 2, side]).astype(jnp.int32)

    w_mine = jnp.swapaxes(w_proj, 1, 2)
    other = other_half(flat(w_mine)).reshape(w_mine.shape)
    kept = (half, cols, chans)
    other_out = other_half(w_out)
    normed, scale, keep, mine, *sent = call(
        first_kernel,
        [(half, cols, width)] * 2 + [(rows, cols), w_mine.shape] + [(half, cols, width)] * 2,
        (place, pair, pair_mask, w_mine),
        scratch=[((rows, cols), jnp.int32)],
        distant=3,
        sems=4,
    )
    theirs = [other_core(block) for block in sent]
    right, open_right, slope_right = call(
        functools.partial(right_kernel, rows), [kept] * 3, (place, normed, keep, mine, other)
    )
    right, other_out = lax.optimization_barrier((right, other_out))
    near = along(right, NEXT)
    middle = along(right, MIDDLE)
    _, cotangent_late = lax.optimization_barrier((right, cotangent))
    (third,) = call(
        third_kernel, [(chips + 1, rows, half, width)], (place, cotangent_late, keep), distant=1, sems=chips
    )
    theirs.append(other_core(third))
    quarter = (chips, rows, half, width)
    tile_outs = [(rows, half, width)] * 2 + [(2 * rows * half, chans), kept]
    tile_scratch = [(4, half * GROUP, chans), (2 * rows * half, chans)]
    out_here, out_there, d_x, d_right, rights = ([None] * 4 for _ in range(5))
    rights[0] = right
    left, left_there, open_left, slope_left, gate, d_here, d_there, w_all_out = call(
        functools.partial(prepare_kernel, rows),
        [(rows, cols, chans)] * 2 + [kept] * 2 + [(rows, cols, width), quarter, quarter, (chans, width)],
        (place, pair, keep, cotangent, *theirs, mine, other, w_gate, w_out, other_out),
        scratch=[(CHUNK, cols, width)],
    )

    def tile(step, *blocks):
        got = call(
            functools.partial(tile_kernel, step, len(blocks)),
            tile_outs + ([kept] if len(blocks) == 2 else []),
            (place, *blocks, left, left_there, d_here, d_there, w_all_out),
            scratch=tile_scratch,
        )
        out_here[step], out_there[step], d_x[step], d_right[step] = got[:4]
        rights[step] = got[4] if len(blocks) == 2 else blocks[0]

    near, d_here = lax.optimization_barrier((near, d_here))
    cross = along(near, MIDDLE)
    outer = along(middle, OUTWARD)
    tile(0, right)
    tile(1, near)
    early_other = other_core(jnp.stack(out_there[:2]))
    d_left_here, d_left_there = call(
        functools.partial(left_kernel, 1, False), [(rows, cols, chans)] * 2, (place, rights[0], d_x[0])
    )
    cross, early_other, d_left_here = lax.optimization_barrier((cross, early_other, d_left_here))
    far = along(cross, OUTWARD)
    early_far = other_half(jnp.stack([jnp.stack(out_here[:2]), early_other]))
    tile(2, cross, outer)
    inward = along(d_right[2], INWARD)
    swapped = along(d_right[2], MIDDLE)
    d_left_here, d_left_there = call(
        functools.partial(left_kernel, 2, True),
        [(rows, cols, chans)] * 2,
        (place, *rights[1:3], *d_x[1:3], d_left_here, d_left_there),
    )
    far, d_left_here = lax.optimization_barrier((far, d_left_here))
    out_here[3], out_there[3], d_x[3], d_right[3], rights[3], d_left_sent = call(
        functools.partial(last_tile_kernel, 3),
        tile_outs + [kept, (rows + 2, cols, chans)],
        (place, middle, far, left, left_there, d_here, d_there, w_all_out, d_left_there, out_there[2]),
        scratch=tile_scratch,
    )
    cuts = [half * eighths // 8 for eighths in CUTS]
    spans = list(zip(cuts, cuts[1:]))
    swapped, to_across = lax.optimization_barrier((swapped, d_right[3] + inward))
    to_across, to_near, early_far, d_left_sent = lax.optimization_barrier(
        (to_across, d_right[1] + swapped, early_far, d_left_sent)
    )
    from_across, from_near = [along(to_across[: cuts[1]], ACROSS)], [along(to_near[: cuts[1]], NEXT)]
    received = other_core(d_left_sent)
    _, d_left_here = lax.optimization_barrier((d_left_sent, d_left_here))
    (d_left_kept,) = call(last_kept_kernel, [(rows, cols, chans)], (place, rights[3], d_x[3], d_left_here))
    sizes = [last - first for first, last in spans]
    sizes[0] += 2
    sizes[-1] += 2
    d_left, *packed = call(
        functools.partial(share_kernel, cuts),
        [kept] + [(size, cols, chans) for size in sizes],
        (place, d_left_kept, received, out_here[2], out_here[3]),
    )
    far_parts = [other_half(block) for block in packed]
    for first, last in spans[1:]:
        from_near.append(along(to_near[first:last], NEXT))
        from_across[-1], last_across = lax.optimization_barrier((from_across[-1], to_across[first:last]))
        from_across.append(along(last_across, ACROSS))
    outs = (*out_here, early_other, early_far, received)
    mine_parts, other_parts = [], []
    for at, (first, last) in enumerate(spans):
        (base,) = call(
            functools.partial(base_kernel, rows, first),
            [(last - first, cols, width)],
            (place, *outs, far_parts[0], far_parts[at], gate, cotangent, w_gate, d_left, open_left, slope_left, mine, other),
            scratch=[(last - first, cols, width)],
        )
        if at:
            base, mine_parts[-1] = lax.optimization_barrier((base, mine_parts[-1]))
        (rows_done,) = call(
            functools.partial(pair_kernel, first),
            [(last - first, cols, width)],
            (place, normed, scale, base, d_right[0], from_near[at], from_across[at], open_right, slope_right, mine, other),
        )
        mine_parts.append(rows_done)
        other_parts.append(other_half(rows_done))
    _, gate_late = lax.optimization_barrier((mine_parts[-1], gate))
    (update,) = call(
        functools.partial(update_kernel, rows),
        [(rows, cols, width)],
        (place, *outs, far_parts[0], far_parts[-1], gate_late),
        scratch=[(rows, cols, width)],
    )
    d_pair = join(mine_parts, cuts[:-1], (True,) * len(spans), pair.shape)
    d_pair, update = lax.optimization_barrier((d_pair, update))
    for first, part in zip(cuts, other_parts):
        d_pair, part = lax.optimization_barrier((d_pair, part))
        d_pair = join([part], (first,), (False,), pair.shape, d_pair)
    return (update, d_pair)


def passed_along(block, axis, distance):
    devices = range(lax.axis_size(axis))
    route = [((i - distance) % len(devices), i) for i in devices]
    return lax.ppermute(block, axis, route)


def normalize(values):
    mean = jnp.mean(values, axis=-1, keepdims=True)
    centered = values - mean
    variance = jnp.mean(centered * centered, axis=-1, keepdims=True)
    scale = lax.rsqrt(variance + 1e-05)
    return (centered * scale, scale)


def on_ring(pair, pair_mask, w_proj, w_gate, w_out, cotangent):
    highest = lax.Precision.HIGHEST
    normed, pair_scale = normalize(pair)
    proj = jnp.einsum("rqz,pzc->pcrq", normed, w_proj, precision=highest)
    keep = pair_mask.astype(jnp.float32)
    sig_left = jax.nn.sigmoid(proj[1])
    sig_right = jax.nn.sigmoid(proj[3])
    left = keep * sig_left * proj[0]
    right = keep * sig_right * proj[2]
    chans, rows, cols = left.shape
    count = lax.axis_size("row")
    here = lax.axis_index("row")

    def visit(step, carry):
        block, store, partial_value = carry
        source = (here - step) % count
        store = lax.dynamic_update_slice_in_dim(store, block, source * rows, 1)
        product = jnp.einsum("cik,cjk->cij", left, block, precision=highest)
        partial_value = lax.dynamic_update_slice_in_dim(partial_value, product, source * rows, 2)
        block = passed_along(block, "row", 1)
        return (block, store, partial_value)

    store = jnp.zeros((chans, rows * count, cols), jnp.float32)
    partial_value = jnp.zeros((chans, rows, rows * count), jnp.float32)
    block, store, partial_value = lax.fori_loop(0, count - 1, visit, (right, store, partial_value))
    source = (here + 1) % count
    right_all = lax.dynamic_update_slice_in_dim(store, block, source * rows, 1)
    product = jnp.einsum("cik,cjk->cij", left, block, precision=highest)
    partial_value = lax.dynamic_update_slice_in_dim(partial_value, product, source * rows, 2)
    mixed = lax.psum_scatter(partial_value, "sub", scatter_dimension=2, tiled=True)
    first = jnp.sum(mixed, axis=0)
    second = jnp.sum(mixed * mixed, axis=0)
    projected = jnp.einsum("crq,cd->rqd", mixed, w_out, precision=highest)
    col_total = jnp.sum(w_out, axis=0)
    projected, first, second, col_total = lax.psum((projected, first, second, col_total), "ch")
    center = first / C
    spread = lax.rsqrt(second / C - center * center + 1e-05)
    outgoing = (projected - center[..., None] * col_total) * spread[..., None]
    gate = jax.nn.sigmoid(jnp.einsum("rqz,zd->rqd", normed, w_gate, precision=highest))
    update = gate * outgoing
    d_outgoing = cotangent * gate
    d_gate_pre = cotangent * outgoing * gate * (1.0 - gate)
    d_mixed_norm = jnp.einsum("rqd,cd->crq", d_outgoing, w_out, precision=highest)
    mean_one = jnp.sum(d_outgoing * col_total, axis=-1) / C
    mean_two = jnp.sum(d_outgoing * outgoing, axis=-1) / C
    mixed_norm = (mixed - center) * spread
    d_mixed = (d_mixed_norm - mean_one - mixed_norm * mean_two) * spread
    d_mixed_full = lax.all_gather(d_mixed, "sub", axis=2, tiled=True)
    d_left = jnp.einsum("cij,cjk->cik", d_mixed_full, right_all, precision=highest)
    d_right = jnp.transpose(
        lax.psum_scatter(
            jnp.einsum("cij,cik->jck", d_mixed_full, left, precision=highest),
            "row",
            scatter_dimension=0,
            tiled=True,
        ),
        (1, 0, 2),
    )
    d_proj = jnp.stack(
        [
            d_left * keep * sig_left,
            d_left * keep * proj[0] * sig_left * (1.0 - sig_left),
            d_right * keep * sig_right,
            d_right * keep * proj[2] * sig_right * (1.0 - sig_right),
        ]
    )
    d_normed_part = jnp.einsum("pcrq,pzc->rqz", d_proj, w_proj, precision=highest)
    d_normed = lax.psum(d_normed_part, "ch")
    d_normed = d_normed + jnp.einsum("rqd,zd->rqz", d_gate_pre, w_gate, precision=highest)
    mean_grad = jnp.mean(d_normed, axis=-1, keepdims=True)
    mean_cross = jnp.mean(d_normed * normed, axis=-1, keepdims=True)
    d_pair = (d_normed - mean_grad - normed * mean_cross) * pair_scale
    return (update, d_pair)


def solution(mesh):
    sizes = mesh.shape
    tiled = sizes["row"] == 8 and sizes["ch"] == 2 and sizes["sub"] == 1
    return jax.shard_map(
        on_tiles if tiled else on_ring,
        mesh=mesh,
        in_specs=(
            P(("grp", "row"), "sub", None),
            P(("grp", "row"), "sub"),
            P(None, None, "ch"),
            P(),
            P("ch", None),
            P(("grp", "row"), "sub", None),
        ),
        out_specs=(P(("grp", "row"), "sub", None), P(("grp", "row"), "sub", None)),
        check_vma=False,
    )
```

```python
import functools
import jax
import jax.numpy as jnp
from jax import lax
from jax.experimental import pallas as pl
from jax.experimental.pallas import tpu as pltpu
from jax.sharding import PartitionSpec as P

C = 128
EPS = 1e-05
F32 = jnp.float32
CHUNK = 4
CUTS = (0, 4, 8)
GROUP = 8


def halves(values):
    high = values.astype(jnp.bfloat16)
    return high, (values - high.astype(F32)).astype(jnp.bfloat16)


def contract(a, b, dims):
    (a_high, a_low), (b_high, b_low) = halves(a), halves(b)
    one = lambda x, y: lax.dot_general(x, y, (dims, ((), ())), preferred_element_type=F32)
    return one(a_high, b_high) + (one(a_high, b_low) + one(a_low, b_high))


def dot(a, b):
    return contract(a, b, ((1,), (0,)))


def dot_t(a, b):
    return contract(a, b, ((1,), (1,)))


def norm(values):
    mean = jnp.mean(values, axis=-1, keepdims=True)
    centered = values - mean
    variance = jnp.mean(centered * centered, axis=-1, keepdims=True)
    scale = lax.rsqrt(variance + EPS)
    return (centered * scale, scale)


def flat(values):
    return values.reshape(-1, values.shape[-1])


def call(kernel, outs, args, scratch=(), distant=0, sems=0):
    vmem = pl.BlockSpec(memory_space=pltpu.VMEM)
    spaces = [pl.BlockSpec(memory_space=pltpu.SMEM)] + [pl.BlockSpec(memory_space=pltpu.HBM)] * distant
    args = list(args)
    args[1 : 1 + distant] = [pltpu.with_memory_space_constraint(a, pltpu.HBM) for a in args[1 : 1 + distant]]
    return pl.pallas_call(
        kernel,
        out_shape=[jax.ShapeDtypeStruct(shape, F32) for shape in outs],
        in_specs=spaces + [vmem] * (len(args) - len(spaces)),
        out_specs=[vmem] * len(outs),
        scratch_shapes=[pltpu.VMEM(*shape) if isinstance(shape[0], tuple) else pltpu.VMEM(shape, F32) for shape in scratch]
        + ([pltpu.SemaphoreType.DMA((sems,))] if sems else []),
        compiler_params=pltpu.CompilerParams(vmem_limit_bytes=24 * 1024 * 1024),
        cost_estimate=pl.CostEstimate(flops=1000, bytes_accessed=1000, transcendentals=0),
    )(*args)


def source_row(place, t, rows):
    half = rows // 2
    if t < half:
        return place[2] * half + t
    return (1 - place[2]) * half + t - half


def first_col(place, chip, core, rows):
    half = rows // 2
    return pl.multiple_of(chip * 2 * rows + core * rows + place[2] * half, half)


def both_halves(place, mine, other):
    first = place[2] == 0
    a, b = jnp.where(first, mine, other), jnp.where(first, other, mine)
    return jnp.concatenate([a, b], axis=0)


def gated_weights(place, mine, other, which):
    return jnp.concatenate([both_halves(place, mine[p], other[p]) for p in (which, which + 1)], axis=0)


def gated(normed, keep_rows, w):
    count = keep_rows.shape[0]
    chans = w.shape[0] // 2
    spread = jnp.transpose(jnp.concatenate([keep_rows] * (8 // count), axis=0))
    keep = jnp.concatenate([spread[:, u : u + 1] for u in range(count)], axis=0)
    proj = dot_t(normed, w)
    sig = jax.nn.sigmoid(proj[:, chans:]) * keep
    return sig * proj[:, :chans], sig


def first_kernel(place, pair, mask, w_proj, normed, scale, keep, mine, first, second, flags, sems):
    half = first.shape[0]
    moves = ((pair.at[:half], first), (pair.at[half:], second), (mask, flags), (w_proj, mine))
    copies = [pltpu.make_async_copy(source, target, sems.at[at]) for at, (source, target) in enumerate(moves)]
    for copy in copies:
        copy.start()
    for copy in copies:
        copy.wait()
    keep[...] = flags[...].astype(F32)
    for t in range(0, half, CHUNK):
        at = slice(t, t + CHUNK)
        value, factor = norm(jnp.where(place[2] == 0, first[at], second[at]))
        normed[at] = value
        scale[at] = jnp.broadcast_to(factor, value.shape)


def third_kernel(place, cotangent, keep, packed, sems):
    rows = cotangent.shape[0]
    half, chips = rows // 2, packed.shape[0] - 1
    copies = []
    for chip in range(chips):
        source = cotangent.at[:, pl.ds(first_col(place, chip, 1 - place[1], rows), half), :]
        copies.append(pltpu.make_async_copy(source, packed.at[chip], sems.at[chip]))
    for copy in copies:
        copy.start()
    packed[chips, :, 0, :] = keep[...]
    for copy in copies:
        copy.wait()


def right_kernel(rows, place, normed, keep, mine, other, right, open_part, slope):
    half, cols, chans = right.shape
    w = gated_weights(place, mine, other, 2)
    for t in range(0, half, CHUNK):
        at = slice(t, t + CHUNK)
        value, sig = gated(flat(normed[at]), keep[pl.ds(source_row(place, t, rows), CHUNK), :], w)
        shape = (CHUNK, cols, chans)
        right[at] = value.reshape(shape)
        open_part[at] = sig.reshape(shape)
        slope[at] = (value * (1.0 - sig)).reshape(shape)


def prepare_kernel(rows, place, pair, keep, cotangent, first, second, third, mine, other, w_gate, mine_out, other_out, *refs):
    left_here, left_there, open_part, slope, gate, d_here, d_there, w_out, normed_rows = refs
    half, cols, chans = open_part.shape
    chips = cols // (2 * rows)
    shape = (CHUNK, cols, chans)
    w = gated_weights(place, mine, other, 0)
    w_out[...] = both_halves(place, mine_out[...], other_out[...])
    for t in range(0, rows, CHUNK):
        row = source_row(place, t, rows)
        at = slice(t, t + CHUNK)
        normed, _ = norm(flat(pair[pl.ds(row, CHUNK)]))
        value, sig = gated(normed, keep[pl.ds(row, CHUNK), :], w)
        left_here[at] = value.reshape(shape)
        if t < half:
            open_part[at] = sig.reshape(shape)
            slope[at] = (value * (1.0 - sig)).reshape(shape)
        gate[at] = jax.nn.sigmoid(dot(normed, w_gate[...])).reshape(CHUNK, cols, -1)
        for chip in range(chips):
            near = pl.ds(first_col(place, chip, place[1], rows), half)
            d_here[chip, at] = gate[at, near, :] * cotangent[pl.ds(row, CHUNK), near, :]
        their_row = row % half
        normed, _ = norm(flat(jnp.where(row < half, first[pl.ds(their_row, CHUNK)], second[pl.ds(their_row, CHUNK)])))
        value, _ = gated(normed, third[chips, pl.ds(row, CHUNK), 0, :], w)
        left_there[at] = value.reshape(shape)
        normed_rows[...] = normed.reshape(CHUNK, cols, -1)
        picked = [
            normed_rows[:, pl.ds(first_col(place, chip, place[1], rows), half), :] for chip in range(chips)
        ]
        opened = jax.nn.sigmoid(dot(flat(jnp.stack(picked)), w_gate[...])).reshape(chips, CHUNK, half, -1)
        for chip in range(chips):
            d_there[chip, at] = opened[chip] * third[chip, pl.ds(row, CHUNK)]


def tile_body(step, place, right, left_here, left_there, d_here, d_there, w_out, out_here, out_there, d_x, d_right, partial, x):
    rows = left_here.shape[0]
    half, cols, chans = right.shape
    groups = cols // GROUP

    def forward(pair_at, _):
        for which, left in enumerate((left_here, left_there)):
            i = pair_at * 2
            value = [left[i], left[i + 1]]
            for j in range(half):
                block = right[j]
                for u in range(2):
                    product = (value[u] * block).reshape(groups, GROUP, chans)
                    partial[2 * which + u, j * GROUP : (j + 1) * GROUP] = jnp.sum(product, axis=0)
            for u in range(2):
                total = partial[2 * which + u, pl.ds(0, half, stride=GROUP), :]
                for s in range(1, GROUP):
                    total = total + partial[2 * which + u, pl.ds(s, half, stride=GROUP), :]
                x[pl.ds(pl.multiple_of((which * rows + i + u) * half, half), half), :] = total
        return 0

    lax.fori_loop(0, rows // 2, forward, 0)
    chip = jnp.bitwise_xor(place[0], step)
    d_out = jnp.concatenate([flat(d_here[chip]), flat(d_there[chip])], axis=0)
    normed, scale = norm(x[...])
    out = dot(normed, w_out[...])
    out_here[...] = out[: rows * half].reshape(rows, half, -1)
    out_there[...] = out[rows * half :].reshape(rows, half, -1)
    d_normed = dot_t(d_out, w_out[...])
    mean_one = jnp.mean(d_normed, axis=-1, keepdims=True)
    mean_two = jnp.mean(d_normed * normed, axis=-1, keepdims=True)
    d_x[...] = (d_normed - mean_one - normed * mean_two) * scale
    wide = 2 * GROUP

    def backward(at, _):
        here = pl.ds(pl.multiple_of(at * wide, wide), wide)

        def add(block, totals):
            totals = list(totals)
            for u in range(GROUP):
                for which, left in enumerate((left_here, left_there)):
                    i = block * GROUP + u
                    value = left[i, here, :]
                    for j in range(half):
                        totals[j] = totals[j] + value * d_x[pl.ds((which * rows + i) * half + j, 1), :]
            return tuple(totals)

        totals = lax.fori_loop(0, rows // GROUP, add, (jnp.zeros((wide, chans), F32),) * half)
        for j in range(half):
            d_right[j, here, :] = totals[j]
        return 0

    lax.fori_loop(0, cols // wide, backward, 0)


def tile_kernel(step, parts, place, *refs):
    rights, rest = refs[:parts], refs[parts:]
    if parts == 2:
        sum_out = rest[9]
        sum_out[...] = rights[0][...] + rights[1][...]
        tile_body(step, place, sum_out, *rest[:9], *rest[10:])
    else:
        tile_body(step, place, rights[0], *rest)


def left_rows(tiles, base, out, first, count, start):
    half, cols, chans = tiles[0][0].shape

    def body(pair_at, _):
        i = pair_at * 2
        totals = [jnp.zeros((cols, chans), F32)] * 2 if base is None else [base[start + i], base[start + i + 1]]
        for right, d_x in tiles:
            for j in range(half):
                value = right[j]
                for u in range(2):
                    totals[u] = totals[u] + value * d_x[pl.ds((first + i + u) * half + j, 1), :]
        out[start + i] = totals[0]
        out[start + i + 1] = totals[1]
        return 0

    lax.fori_loop(0, count // 2, body, 0)


def left_kernel(tiles, based, place, *refs):
    pairs = tuple(zip(refs[:tiles], refs[tiles : 2 * tiles]))
    bases = refs[2 * tiles : 2 * tiles + 2] if based else (None, None)
    rows = refs[-1].shape[0]
    for which, out in enumerate(refs[-2:]):
        left_rows(pairs, bases[which], out, which * rows, rows, 0)


def last_tile_kernel(step, place, one, two, left_here, left_there, d_here, d_there, w_out, there, out_next, *refs):
    out_here, out_there, d_x, d_right, right, sent, partial, x = refs
    rows = there.shape[0]
    right[...] = one[...] + two[...]
    tile_body(step, place, right, left_here, left_there, d_here, d_there, w_out, out_here, out_there, d_x, d_right, partial, x)
    left_rows(((right, d_x),), there, sent, rows, rows, 0)
    sent[rows] = flat(out_next[...])
    sent[rows + 1] = flat(out_there[...])


def last_kept_kernel(place, right, d_x, here, kept):
    left_rows(((right, d_x),), here, kept, 0, here.shape[0], 0)


def share_kernel(cuts, place, kept, received, out_next, out_last, d_left, *packed):
    half = d_left.shape[0]
    block = half * half
    d_left[...] = kept[:half] + received[:half]
    for first, last, part in zip(cuts, cuts[1:], packed):
        at = slice(half + first, half + last)
        part[: last - first] = kept[at] + received[at]
    early, late, spare = packed[0], packed[-2], packed[-1]
    for step, out in enumerate((out_next, out_last)):
        at = slice(step * block, (step + 1) * block)
        plane = 2 * half + step
        early[early.shape[0] - 2, at] = flat(out[half:])
        early[early.shape[0] - 1, at] = received[plane, block:]
        late[late.shape[0] - 1, at] = flat(out[:half])
        spare[0, at] = received[plane, :block]


def gather_out(place, rows, t, count, start, out, here, early_other, early_far, received, far):
    half = rows // 2
    block = half * half
    for far_half in (0, 1):
        source = (t + far_half * half) % rows
        at, wide = slice(source, source + count), slice(source * half, (source + count) * half)
        for far_core in (0, 1):
            core = place[1] + far_core * (1 - 2 * place[1])
            side = place[2] + far_half * (1 - 2 * place[2])
            for step in range(4):
                chip = jnp.bitwise_xor(place[0], step)
                first = pl.multiple_of(chip * 2 * rows + core * rows + side * half, half)
                if far_half:
                    if step < 2:
                        value = early_far[far_core, step, at]
                    else:
                        begin = (step - 2) * block + (t % half) * half
                        ref, plane = far[far_core]
                        value = ref[plane, begin : begin + count * half].reshape(count, half, -1)
                elif far_core:
                    if step < 2:
                        value = early_other[step, at]
                    else:
                        value = received[rows + step - 2, wide].reshape(count, half, -1)
                else:
                    value = here[step][at]
                out[start : start + count, pl.ds(first, half), :] = value


def update_kernel(rows, place, *refs):
    here, early_other, early_far, received, far, far_next, far_rows, gate, update, out = refs[:4], *refs[4:]
    half = rows // 2
    last = far.shape[0] - 1
    first_planes = ((far, last - 1), (far, last))
    second_planes = ((far_next, far_next.shape[0] - 1), (far_rows, far_rows.shape[0] - 1))
    gather_out(place, rows, 0, half, 0, out, here, early_other, early_far, received, first_planes)
    gather_out(place, rows, half, half, half, out, here, early_other, early_far, received, second_planes)
    for t in range(0, rows, CHUNK):
        update[pl.ds(source_row(place, t, rows), CHUNK)] = gate[t : t + CHUNK] * out[t : t + CHUNK]


def base_kernel(rows, t, place, *refs):
    here, early_other, early_far, received, far, far_rows = refs[:4], *refs[4:9]
    gate, cotangent, w_gate, d_left, open_part, slope, mine, other, base, out = refs[9:]
    count, cols = base.shape[:2]
    planes = ((far, far.shape[0] - 2), (far, far.shape[0] - 1))
    gather_out(place, rows, t, count, 0, out, here, early_other, early_far, received, planes)
    w = gated_weights(place, mine, other, 0)
    at = slice(t, t + count)
    opened = gate[at]
    d_gate = cotangent[pl.ds(source_row(place, t, rows), count)] * (opened * out[...]) * (1.0 - opened)
    grad = flat(d_left[at] + far_rows[:count])
    both = jnp.concatenate([grad * flat(open_part[at]), grad * flat(slope[at])], axis=1)
    base[...] = (dot_t(flat(d_gate), w_gate[...]) + dot(both, w)).reshape(count, cols, -1)


def pair_kernel(first, count, place, normed, scale, base, d_right, d_right_near, d_right_across, open_part, slope, mine, other, *refs):
    d_mine = refs[-1]
    cols = d_mine.shape[1]
    if len(refs) == 2:
        d_mine[count] = refs[0][0]
    w = gated_weights(place, mine, other, 2)
    at = slice(first, first + count)
    grad = flat(d_right[at] + d_right_near[...] + d_right_across[...])
    both = jnp.concatenate([grad * flat(open_part[at]), grad * flat(slope[at])], axis=1)
    d_normed = flat(base[...]) + dot(both, w)
    value = flat(normed[at])
    mean_grad = jnp.mean(d_normed, axis=-1, keepdims=True)
    mean_cross = jnp.mean(d_normed * value, axis=-1, keepdims=True)
    d_mine[:count] = ((d_normed - mean_grad - value * mean_cross) * flat(scale[at])).reshape(count, cols, -1)


def join_kernel(firsts, counts, sides, *refs):
    blocks, whole, sems = refs[: len(firsts)], refs[-2], refs[-1]
    side = lax.axis_index("ch")
    half = whole.shape[0] // 2
    copies = []
    for at, (block, first, count, mine) in enumerate(zip(blocks, firsts, counts, sides)):
        start = (side if mine else 1 - side) * half + first
        copies.append(pltpu.make_async_copy(block.at[:count], whole.at[pl.ds(start, count)], sems.at[at]))
    for copy in copies:
        copy.start()
    for copy in copies:
        copy.wait()


def join(blocks, firsts, counts, sides, shape, whole=None):
    anywhere = pl.BlockSpec(memory_space=pl.ANY)
    vmem = pl.BlockSpec(memory_space=pltpu.VMEM)
    given = [] if whole is None else [whole]
    return pl.pallas_call(
        functools.partial(join_kernel, firsts, counts, sides),
        out_shape=jax.ShapeDtypeStruct(shape, F32),
        in_specs=[vmem] * len(blocks) + [anywhere] * len(given),
        out_specs=anywhere,
        input_output_aliases={len(blocks): 0} if given else {},
        scratch_shapes=[pltpu.SemaphoreType.DMA((len(blocks),))],
        compiler_params=pltpu.CompilerParams(vmem_limit_bytes=2 * 1024 * 1024),
    )(*blocks, *given)


def along(block, pairs):
    return lax.ppermute(block, "row", [(2 * a + core, 2 * b + core) for a, b in pairs for core in (0, 1)])


def other_core(block):
    return lax.ppermute(block, "row", [(i, i ^ 1) for i in range(lax.axis_size("row"))])


def other_half(block):
    return lax.ppermute(block, "ch", [(0, 1), (1, 0)])


NEXT = [(0, 1), (1, 0), (2, 3), (3, 2)]
MIDDLE = [(1, 2), (2, 1)]
OUTWARD = [(1, 0), (2, 3)]
INWARD = [(0, 1), (3, 2)]
ACROSS = [(0, 3), (3, 0), (1, 2), (2, 1)]


def on_tiles(pair, pair_mask, w_proj, w_gate, w_out, cotangent):
    rows, cols, width = pair.shape
    half = rows // 2
    chips = cols // (2 * rows)
    chans = 2 * w_out.shape[0]
    row, side = lax.axis_index("row"), lax.axis_index("ch")
    place = jnp.stack([row // 2, row % 2, side]).astype(jnp.int32)

    w_mine = jnp.swapaxes(w_proj, 1, 2)
    other = other_half(flat(w_mine)).reshape(w_mine.shape)
    kept = (half, cols, chans)
    other_out = other_half(w_out)
    normed, scale, keep, mine, *sent = call(
        first_kernel,
        [(half, cols, width)] * 2 + [(rows, cols), w_mine.shape] + [(half, cols, width)] * 2,
        (place, pair, pair_mask, w_mine),
        scratch=[((rows, cols), jnp.int32)],
        distant=3,
        sems=4,
    )
    theirs = [other_core(block) for block in sent]
    right, open_right, slope_right = call(
        functools.partial(right_kernel, rows), [kept] * 3, (place, normed, keep, mine, other)
    )
    right, other_out = lax.optimization_barrier((right, other_out))
    near = along(right, NEXT)
    middle = along(right, MIDDLE)
    _, cotangent_late = lax.optimization_barrier((right, cotangent))
    (third,) = call(
        third_kernel, [(chips + 1, rows, half, width)], (place, cotangent_late, keep), distant=1, sems=chips
    )
    theirs.append(other_core(third))
    quarter = (chips, rows, half, width)
    tile_outs = [(rows, half, width)] * 2 + [(2 * rows * half, chans), kept]
    tile_scratch = [(4, half * GROUP, chans), (2 * rows * half, chans)]
    out_here, out_there, d_x, d_right, rights = ([None] * 4 for _ in range(5))
    rights[0] = right
    left, left_there, open_left, slope_left, gate, d_here, d_there, w_all_out = call(
        functools.partial(prepare_kernel, rows),
        [(rows, cols, chans)] * 2 + [kept] * 2 + [(rows, cols, width), quarter, quarter, (chans, width)],
        (place, pair, keep, cotangent, *theirs, mine, other, w_gate, w_out, other_out),
        scratch=[(CHUNK, cols, width)],
    )

    def tile(step, *blocks):
        got = call(
            functools.partial(tile_kernel, step, len(blocks)),
            tile_outs + ([kept] if len(blocks) == 2 else []),
            (place, *blocks, left, left_there, d_here, d_there, w_all_out),
            scratch=tile_scratch,
        )
        out_here[step], out_there[step], d_x[step], d_right[step] = got[:4]
        rights[step] = got[4] if len(blocks) == 2 else blocks[0]

    near, d_here = lax.optimization_barrier((near, d_here))
    cross = along(near, MIDDLE)
    outer = along(middle, OUTWARD)
    tile(0, right)
    tile(1, near)
    early_other = other_core(jnp.stack(out_there[:2]))
    d_left_here, d_left_there = call(
        functools.partial(left_kernel, 1, False), [(rows, cols, chans)] * 2, (place, rights[0], d_x[0])
    )
    cross, early_other, d_left_here = lax.optimization_barrier((cross, early_other, d_left_here))
    far = along(cross, OUTWARD)
    early_far = other_half(jnp.stack([jnp.stack(out_here[:2]), early_other]))
    tile(2, cross, outer)
    inward = along(d_right[2], INWARD)
    swapped = along(d_right[2], MIDDLE)
    d_left_here, d_left_there = call(
        functools.partial(left_kernel, 2, True),
        [(rows, cols, chans)] * 2,
        (place, *rights[1:3], *d_x[1:3], d_left_here, d_left_there),
    )
    far, d_left_here = lax.optimization_barrier((far, d_left_here))
    out_here[3], out_there[3], d_x[3], d_right[3], rights[3], d_left_sent = call(
        functools.partial(last_tile_kernel, 3),
        tile_outs + [kept, (rows + 2, cols, chans)],
        (place, middle, far, left, left_there, d_here, d_there, w_all_out, d_left_there, out_there[2]),
        scratch=tile_scratch,
    )
    cuts = [half * eighths // 8 for eighths in CUTS]
    spans = list(zip(cuts, cuts[1:]))
    swapped, to_across = lax.optimization_barrier((swapped, d_right[3] + inward))
    to_across, to_near, early_far, d_left_sent = lax.optimization_barrier(
        (to_across, d_right[1] + swapped, early_far, d_left_sent)
    )
    from_across, from_near = [along(to_across[: cuts[1]], ACROSS)], [along(to_near[: cuts[1]], NEXT)]
    received = other_core(d_left_sent)
    _, d_left_here = lax.optimization_barrier((d_left_sent, d_left_here))
    (d_left_kept,) = call(last_kept_kernel, [(rows, cols, chans)], (place, rights[3], d_x[3], d_left_here))
    sizes = [last - first for first, last in spans]
    sizes[0] += 2
    sizes[-1] += 1
    sizes.append(1)
    d_left, *packed = call(
        functools.partial(share_kernel, cuts),
        [kept] + [(size, cols, chans) for size in sizes],
        (place, d_left_kept, received, out_here[2], out_here[3]),
    )
    spare = packed.pop()
    far_parts = [other_half(block) for block in packed]
    for first, last in spans[1:]:
        from_near.append(along(to_near[first:last], NEXT))
        from_across[-1], last_across = lax.optimization_barrier((from_across[-1], to_across[first:last]))
        from_across.append(along(last_across, ACROSS))
    outs = (*out_here, early_other, early_far, received)
    mine_parts, other_parts = [], []
    for at, (first, last) in enumerate(spans):
        (base,) = call(
            functools.partial(base_kernel, rows, first),
            [(last - first, cols, width)],
            (place, *outs, far_parts[0], far_parts[at], gate, cotangent, w_gate, d_left, open_left, slope_left, mine, other),
            scratch=[(last - first, cols, width)],
        )
        if at:
            base, mine_parts[-1] = lax.optimization_barrier((base, mine_parts[-1]))
        (rows_done,) = call(
            functools.partial(pair_kernel, first, last - first),
            [(last - first + (at == 0), cols, width)],
            (place, normed, scale, base, d_right[0], from_near[at], from_across[at], open_right, slope_right, mine, other)
            + ((spare,) if at == 0 else ()),
        )
        mine_parts.append(rows_done)
        other_parts.append(other_half(rows_done))
    _, gate_late = lax.optimization_barrier((mine_parts[-1], gate))
    (update,) = call(
        functools.partial(update_kernel, rows),
        [(rows, cols, width)],
        (place, *outs, far_parts[0], far_parts[-1], other_parts[0], gate_late),
        scratch=[(rows, cols, width)],
    )
    counts = [last - first for first, last in spans]
    d_pair = join(mine_parts, cuts[:-1], counts, (True,) * len(spans), pair.shape)
    d_pair, update = lax.optimization_barrier((d_pair, update))
    for first, count, part in zip(cuts, counts, other_parts):
        d_pair, part = lax.optimization_barrier((d_pair, part))
        d_pair = join([part], (first,), (count,), (False,), pair.shape, d_pair)
    return (update, d_pair)


def passed_along(block, axis, distance):
    devices = range(lax.axis_size(axis))
    route = [((i - distance) % len(devices), i) for i in devices]
    return lax.ppermute(block, axis, route)


def normalize(values):
    mean = jnp.mean(values, axis=-1, keepdims=True)
    centered = values - mean
    variance = jnp.mean(centered * centered, axis=-1, keepdims=True)
    scale = lax.rsqrt(variance + 1e-05)
    return (centered * scale, scale)


def on_ring(pair, pair_mask, w_proj, w_gate, w_out, cotangent):
    highest = lax.Precision.HIGHEST
    normed, pair_scale = normalize(pair)
    proj = jnp.einsum("rqz,pzc->pcrq", normed, w_proj, precision=highest)
    keep = pair_mask.astype(jnp.float32)
    sig_left = jax.nn.sigmoid(proj[1])
    sig_right = jax.nn.sigmoid(proj[3])
    left = keep * sig_left * proj[0]
    right = keep * sig_right * proj[2]
    chans, rows, cols = left.shape
    count = lax.axis_size("row")
    here = lax.axis_index("row")

    def visit(step, carry):
        block, store, partial_value = carry
        source = (here - step) % count
        store = lax.dynamic_update_slice_in_dim(store, block, source * rows, 1)
        product = jnp.einsum("cik,cjk->cij", left, block, precision=highest)
        partial_value = lax.dynamic_update_slice_in_dim(partial_value, product, source * rows, 2)
        block = passed_along(block, "row", 1)
        return (block, store, partial_value)

    store = jnp.zeros((chans, rows * count, cols), jnp.float32)
    partial_value = jnp.zeros((chans, rows, rows * count), jnp.float32)
    block, store, partial_value = lax.fori_loop(0, count - 1, visit, (right, store, partial_value))
    source = (here + 1) % count
    right_all = lax.dynamic_update_slice_in_dim(store, block, source * rows, 1)
    product = jnp.einsum("cik,cjk->cij", left, block, precision=highest)
    partial_value = lax.dynamic_update_slice_in_dim(partial_value, product, source * rows, 2)
    mixed = lax.psum_scatter(partial_value, "sub", scatter_dimension=2, tiled=True)
    first = jnp.sum(mixed, axis=0)
    second = jnp.sum(mixed * mixed, axis=0)
    projected = jnp.einsum("crq,cd->rqd", mixed, w_out, precision=highest)
    col_total = jnp.sum(w_out, axis=0)
    projected, first, second, col_total = lax.psum((projected, first, second, col_total), "ch")
    center = first / C
    spread = lax.rsqrt(second / C - center * center + 1e-05)
    outgoing = (projected - center[..., None] * col_total) * spread[..., None]
    gate = jax.nn.sigmoid(jnp.einsum("rqz,zd->rqd", normed, w_gate, precision=highest))
    update = gate * outgoing
    d_outgoing = cotangent * gate
    d_gate_pre = cotangent * outgoing * gate * (1.0 - gate)
    d_mixed_norm = jnp.einsum("rqd,cd->crq", d_outgoing, w_out, precision=highest)
    mean_one = jnp.sum(d_outgoing * col_total, axis=-1) / C
    mean_two = jnp.sum(d_outgoing * outgoing, axis=-1) / C
    mixed_norm = (mixed - center) * spread
    d_mixed = (d_mixed_norm - mean_one - mixed_norm * mean_two) * spread
    d_mixed_full = lax.all_gather(d_mixed, "sub", axis=2, tiled=True)
    d_left = jnp.einsum("cij,cjk->cik", d_mixed_full, right_all, precision=highest)
    d_right = jnp.transpose(
        lax.psum_scatter(
            jnp.einsum("cij,cik->jck", d_mixed_full, left, precision=highest),
            "row",
            scatter_dimension=0,
            tiled=True,
        ),
        (1, 0, 2),
    )
    d_proj = jnp.stack(
        [
            d_left * keep * sig_left,
            d_left * keep * proj[0] * sig_left * (1.0 - sig_left),
            d_right * keep * sig_right,
            d_right * keep * proj[2] * sig_right * (1.0 - sig_right),
        ]
    )
    d_normed_part = jnp.einsum("pcrq,pzc->rqz", d_proj, w_proj, precision=highest)
    d_normed = lax.psum(d_normed_part, "ch")
    d_normed = d_normed + jnp.einsum("rqd,zd->rqz", d_gate_pre, w_gate, precision=highest)
    mean_grad = jnp.mean(d_normed, axis=-1, keepdims=True)
    mean_cross = jnp.mean(d_normed * normed, axis=-1, keepdims=True)
    d_pair = (d_normed - mean_grad - normed * mean_cross) * pair_scale
    return (update, d_pair)


def solution(mesh):
    sizes = mesh.shape
    tiled = sizes["row"] == 8 and sizes["ch"] == 2 and sizes["sub"] == 1
    return jax.shard_map(
        on_tiles if tiled else on_ring,
        mesh=mesh,
        in_specs=(
            P(("grp", "row"), "sub", None),
            P(("grp", "row"), "sub"),
            P(None, None, "ch"),
            P(),
            P("ch", None),
            P(("grp", "row"), "sub", None),
        ),
        out_specs=(P(("grp", "row"), "sub", None), P(("grp", "row"), "sub", None)),
        check_vma=False,
    )
```

```python
import functools
import jax
import jax.numpy as jnp
from jax import lax
from jax.experimental import pallas as pl
from jax.experimental.pallas import tpu as pltpu
from jax.sharding import PartitionSpec as P

C = 128
EPS = 1e-05
F32 = jnp.float32
CHUNK = 4
CUTS = (0, 4, 8)
GROUP = 8


def halves(values):
    high = values.astype(jnp.bfloat16)
    return high, (values - high.astype(F32)).astype(jnp.bfloat16)


def contract(a, b, dims):
    (a_high, a_low), (b_high, b_low) = halves(a), halves(b)
    one = lambda x, y: lax.dot_general(x, y, (dims, ((), ())), preferred_element_type=F32)
    return one(a_high, b_high) + (one(a_high, b_low) + one(a_low, b_high))


def dot(a, b):
    return contract(a, b, ((1,), (0,)))


def dot_t(a, b):
    return contract(a, b, ((1,), (1,)))


def norm(values):
    mean = jnp.mean(values, axis=-1, keepdims=True)
    centered = values - mean
    variance = jnp.mean(centered * centered, axis=-1, keepdims=True)
    scale = lax.rsqrt(variance + EPS)
    return (centered * scale, scale)


def flat(values):
    return values.reshape(-1, values.shape[-1])


def call(kernel, outs, args, scratch=(), distant=0, sems=0):
    vmem = pl.BlockSpec(memory_space=pltpu.VMEM)
    spaces = [pl.BlockSpec(memory_space=pltpu.SMEM)] + [pl.BlockSpec(memory_space=pltpu.HBM)] * distant
    args = list(args)
    args[1 : 1 + distant] = [pltpu.with_memory_space_constraint(a, pltpu.HBM) for a in args[1 : 1 + distant]]
    return pl.pallas_call(
        kernel,
        out_shape=[jax.ShapeDtypeStruct(shape, F32) for shape in outs],
        in_specs=spaces + [vmem] * (len(args) - len(spaces)),
        out_specs=[vmem] * len(outs),
        scratch_shapes=[pltpu.VMEM(*shape) if isinstance(shape[0], tuple) else pltpu.VMEM(shape, F32) for shape in scratch]
        + ([pltpu.SemaphoreType.DMA((sems,))] if sems else []),
        compiler_params=pltpu.CompilerParams(vmem_limit_bytes=24 * 1024 * 1024),
        cost_estimate=pl.CostEstimate(flops=1000, bytes_accessed=1000, transcendentals=0),
    )(*args)


def source_row(place, t, rows):
    half = rows // 2
    if t < half:
        return place[2] * half + t
    return (1 - place[2]) * half + t - half


def first_col(place, chip, core, rows):
    half = rows // 2
    return pl.multiple_of(chip * 2 * rows + core * rows + place[2] * half, half)


def both_halves(place, mine, other):
    first = place[2] == 0
    a, b = jnp.where(first, mine, other), jnp.where(first, other, mine)
    return jnp.concatenate([a, b], axis=0)


def gated_weights(place, mine, other, which):
    return jnp.concatenate([both_halves(place, mine[p], other[p]) for p in (which, which + 1)], axis=0)


def gated(normed, keep_rows, w):
    count = keep_rows.shape[0]
    chans = w.shape[0] // 2
    spread = jnp.transpose(jnp.concatenate([keep_rows] * (8 // count), axis=0))
    keep = jnp.concatenate([spread[:, u : u + 1] for u in range(count)], axis=0)
    proj = dot_t(normed, w)
    sig = jax.nn.sigmoid(proj[:, chans:]) * keep
    return sig * proj[:, :chans], sig


def first_kernel(place, pair, mask, w_proj, normed, scale, keep, mine, first, second, flags, sems):
    half = first.shape[0]
    moves = ((pair.at[:half], first), (pair.at[half:], second), (mask, flags), (w_proj, mine))
    copies = [pltpu.make_async_copy(source, target, sems.at[at]) for at, (source, target) in enumerate(moves)]
    for copy in copies:
        copy.start()
    for copy in copies:
        copy.wait()
    keep[...] = flags[...].astype(F32)
    for t in range(0, half, CHUNK):
        at = slice(t, t + CHUNK)
        value, factor = norm(jnp.where(place[2] == 0, first[at], second[at]))
        normed[at] = value
        scale[at] = jnp.broadcast_to(factor, value.shape)


def third_kernel(place, cotangent, keep, packed, sems):
    rows = cotangent.shape[0]
    half, chips = rows // 2, packed.shape[0] - 1
    copies = []
    for chip in range(chips):
        source = cotangent.at[:, pl.ds(first_col(place, chip, 1 - place[1], rows), half), :]
        copies.append(pltpu.make_async_copy(source, packed.at[chip], sems.at[chip]))
    for copy in copies:
        copy.start()
    packed[chips, :, 0, :] = keep[...]
    for copy in copies:
        copy.wait()


def right_kernel(rows, place, normed, keep, mine, other, right, open_part, slope):
    half, cols, chans = right.shape
    w = gated_weights(place, mine, other, 2)
    for t in range(0, half, CHUNK):
        at = slice(t, t + CHUNK)
        value, sig = gated(flat(normed[at]), keep[pl.ds(source_row(place, t, rows), CHUNK), :], w)
        shape = (CHUNK, cols, chans)
        right[at] = value.reshape(shape)
        open_part[at] = sig.reshape(shape)
        slope[at] = (value * (1.0 - sig)).reshape(shape)


def prepare_kernel(rows, place, pair, keep, cotangent, first, second, third, mine, other, w_gate, mine_out, other_out, *refs):
    left_here, left_there, open_part, slope, gate, d_here, d_there, w_out, normed_rows = refs
    half, cols, chans = open_part.shape
    chips = cols // (2 * rows)
    shape = (CHUNK, cols, chans)
    w = gated_weights(place, mine, other, 0)
    w_out[...] = both_halves(place, mine_out[...], other_out[...])
    for t in range(0, rows, CHUNK):
        row = source_row(place, t, rows)
        at = slice(t, t + CHUNK)
        normed, _ = norm(flat(pair[pl.ds(row, CHUNK)]))
        value, sig = gated(normed, keep[pl.ds(row, CHUNK), :], w)
        left_here[at] = value.reshape(shape)
        if t < half:
            open_part[at] = sig.reshape(shape)
            slope[at] = (value * (1.0 - sig)).reshape(shape)
        gate[at] = jax.nn.sigmoid(dot(normed, w_gate[...])).reshape(CHUNK, cols, -1)
        for chip in range(chips):
            near = pl.ds(first_col(place, chip, place[1], rows), half)
            d_here[chip, at] = gate[at, near, :] * cotangent[pl.ds(row, CHUNK), near, :]
        their_row = row % half
        normed, _ = norm(flat(jnp.where(row < half, first[pl.ds(their_row, CHUNK)], second[pl.ds(their_row, CHUNK)])))
        value, _ = gated(normed, third[chips, pl.ds(row, CHUNK), 0, :], w)
        left_there[at] = value.reshape(shape)
        normed_rows[...] = normed.reshape(CHUNK, cols, -1)
        picked = [
            normed_rows[:, pl.ds(first_col(place, chip, place[1], rows), half), :] for chip in range(chips)
        ]
        opened = jax.nn.sigmoid(dot(flat(jnp.stack(picked)), w_gate[...])).reshape(chips, CHUNK, half, -1)
        for chip in range(chips):
            d_there[chip, at] = opened[chip] * third[chip, pl.ds(row, CHUNK)]


def tile_body(step, place, right, left_here, left_there, d_here, d_there, w_out, out_here, out_there, d_x, d_right, partial, x):
    rows = left_here.shape[0]
    half, cols, chans = right.shape
    groups = cols // GROUP

    def forward(pair_at, _):
        for which, left in enumerate((left_here, left_there)):
            i = pair_at * 2
            value = [left[i], left[i + 1]]
            for j in range(half):
                block = right[j]
                for u in range(2):
                    product = (value[u] * block).reshape(groups, GROUP, chans)
                    partial[2 * which + u, j * GROUP : (j + 1) * GROUP] = jnp.sum(product, axis=0)
            for u in range(2):
                total = partial[2 * which + u, pl.ds(0, half, stride=GROUP), :]
                for s in range(1, GROUP):
                    total = total + partial[2 * which + u, pl.ds(s, half, stride=GROUP), :]
                x[pl.ds(pl.multiple_of((which * rows + i + u) * half, half), half), :] = total
        return 0

    lax.fori_loop(0, rows // 2, forward, 0)
    chip = jnp.bitwise_xor(place[0], step)
    d_out = jnp.concatenate([flat(d_here[chip]), flat(d_there[chip])], axis=0)
    normed, scale = norm(x[...])
    out = dot(normed, w_out[...])
    out_here[...] = out[: rows * half].reshape(rows, half, -1)
    out_there[...] = out[rows * half :].reshape(rows, half, -1)
    d_normed = dot_t(d_out, w_out[...])
    mean_one = jnp.mean(d_normed, axis=-1, keepdims=True)
    mean_two = jnp.mean(d_normed * normed, axis=-1, keepdims=True)
    d_x[...] = (d_normed - mean_one - normed * mean_two) * scale
    wide = 2 * GROUP

    def backward(at, _):
        here = pl.ds(pl.multiple_of(at * wide, wide), wide)

        def add(block, totals):
            totals = list(totals)
            for u in range(GROUP):
                for which, left in enumerate((left_here, left_there)):
                    i = block * GROUP + u
                    value = left[i, here, :]
                    for j in range(half):
                        totals[j] = totals[j] + value * d_x[pl.ds((which * rows + i) * half + j, 1), :]
            return tuple(totals)

        totals = lax.fori_loop(0, rows // GROUP, add, (jnp.zeros((wide, chans), F32),) * half)
        for j in range(half):
            d_right[j, here, :] = totals[j]
        return 0

    lax.fori_loop(0, cols // wide, backward, 0)


def tile_kernel(step, parts, place, *refs):
    rights, rest = refs[:parts], refs[parts:]
    if parts == 2:
        sum_out = rest[9]
        sum_out[...] = rights[0][...] + rights[1][...]
        tile_body(step, place, sum_out, *rest[:9], *rest[10:])
    else:
        tile_body(step, place, rights[0], *rest)


def left_rows(tiles, base, out, first, count, start):
    half, cols, chans = tiles[0][0].shape

    def body(pair_at, _):
        i = pair_at * 2
        totals = [jnp.zeros((cols, chans), F32)] * 2 if base is None else [base[start + i], base[start + i + 1]]
        for right, d_x in tiles:
            for j in range(half):
                value = right[j]
                for u in range(2):
                    totals[u] = totals[u] + value * d_x[pl.ds((first + i + u) * half + j, 1), :]
        out[start + i] = totals[0]
        out[start + i + 1] = totals[1]
        return 0

    lax.fori_loop(0, count // 2, body, 0)


def left_kernel(tiles, based, place, *refs):
    pairs = tuple(zip(refs[:tiles], refs[tiles : 2 * tiles]))
    bases = refs[2 * tiles : 2 * tiles + 2] if based else (None, None)
    rows = refs[-1].shape[0]
    for which, out in enumerate(refs[-2:]):
        left_rows(pairs, bases[which], out, which * rows, rows, 0)


def last_tile_kernel(step, place, one, two, left_here, left_there, d_here, d_there, w_out, there, out_next, *refs):
    out_here, out_there, d_x, d_right, right, sent, partial, x = refs
    rows = there.shape[0]
    right[...] = one[...] + two[...]
    tile_body(step, place, right, left_here, left_there, d_here, d_there, w_out, out_here, out_there, d_x, d_right, partial, x)
    left_rows(((right, d_x),), there, sent, rows, rows, 0)
    sent[rows] = flat(out_next[...])
    sent[rows + 1] = flat(out_there[...])


def last_kept_kernel(place, right, d_x, here, kept):
    left_rows(((right, d_x),), here, kept, 0, here.shape[0], 0)


def share_kernel(cuts, place, kept, received, out_next, out_last, d_left, *packed):
    half = d_left.shape[0]
    block = half * half
    d_left[...] = kept[:half] + received[:half]
    for first, last, part in zip(cuts, cuts[1:], packed):
        at = slice(half + first, half + last)
        part[: last - first] = kept[at] + received[at]
    early, late = packed[0], packed[-1]
    for step, out in enumerate((out_next, out_last)):
        at = slice(step * block, (step + 1) * block)
        plane = 2 * half + step
        early[early.shape[0] - 2, at] = flat(out[half:])
        early[early.shape[0] - 1, at] = received[plane, block:]
        late[late.shape[0] - 2, at] = flat(out[:half])
        late[late.shape[0] - 1, at] = received[plane, :block]


def gather_out(place, rows, t, count, start, out, here, early_other, early_far, received, far):
    half = rows // 2
    block = half * half
    for far_half in (0, 1):
        source = (t + far_half * half) % rows
        at, wide = slice(source, source + count), slice(source * half, (source + count) * half)
        for far_core in (0, 1):
            core = place[1] + far_core * (1 - 2 * place[1])
            side = place[2] + far_half * (1 - 2 * place[2])
            for step in range(4):
                chip = jnp.bitwise_xor(place[0], step)
                first = pl.multiple_of(chip * 2 * rows + core * rows + side * half, half)
                if far_half:
                    if step < 2:
                        value = early_far[far_core, step, at]
                    else:
                        begin = (step - 2) * block + (t % half) * half
                        value = far[far.shape[0] - 2 + far_core, begin : begin + count * half].reshape(count, half, -1)
                elif far_core:
                    if step < 2:
                        value = early_other[step, at]
                    else:
                        value = received[rows + step - 2, wide].reshape(count, half, -1)
                else:
                    value = here[step][at]
                out[start : start + count, pl.ds(first, half), :] = value


def update_kernel(rows, place, *refs):
    here, early_other, early_far, received, far, far_next, gate, update, out = refs[:4], *refs[4:]
    half = rows // 2
    gather_out(place, rows, 0, half, 0, out, here, early_other, early_far, received, far)
    gather_out(place, rows, half, half, half, out, here, early_other, early_far, received, far_next)
    for t in range(0, rows, CHUNK):
        update[pl.ds(source_row(place, t, rows), CHUNK)] = gate[t : t + CHUNK] * out[t : t + CHUNK]


def base_kernel(rows, t, place, *refs):
    here, early_other, early_far, received, far, far_rows = refs[:4], *refs[4:9]
    gate, cotangent, w_gate, d_left, open_part, slope, mine, other, base, out = refs[9:]
    count, cols = base.shape[:2]
    gather_out(place, rows, t, count, 0, out, here, early_other, early_far, received, far)
    w = gated_weights(place, mine, other, 0)
    at = slice(t, t + count)
    opened = gate[at]
    d_gate = cotangent[pl.ds(source_row(place, t, rows), count)] * (opened * out[...]) * (1.0 - opened)
    grad = flat(d_left[at] + far_rows[:count])
    both = jnp.concatenate([grad * flat(open_part[at]), grad * flat(slope[at])], axis=1)
    base[...] = (dot_t(flat(d_gate), w_gate[...]) + dot(both, w)).reshape(count, cols, -1)


def pair_kernel(first, place, normed, scale, base, d_right, d_right_near, d_right_across, open_part, slope, mine, other, d_mine):
    count, cols = d_mine.shape[:2]
    w = gated_weights(place, mine, other, 2)
    at = slice(first, first + count)
    grad = flat(d_right[at] + d_right_near[...] + d_right_across[...])
    both = jnp.concatenate([grad * flat(open_part[at]), grad * flat(slope[at])], axis=1)
    d_normed = flat(base[...]) + dot(both, w)
    value = flat(normed[at])
    mean_grad = jnp.mean(d_normed, axis=-1, keepdims=True)
    mean_cross = jnp.mean(d_normed * value, axis=-1, keepdims=True)
    d_mine[...] = ((d_normed - mean_grad - value * mean_cross) * flat(scale[at])).reshape(count, cols, -1)


def join_kernel(firsts, sides, *refs):
    blocks, whole, sems = refs[: len(firsts)], refs[-2], refs[-1]
    side = lax.axis_index("ch")
    half = whole.shape[0] // 2
    copies = []
    for at, (block, first, mine) in enumerate(zip(blocks, firsts, sides)):
        start = (side if mine else 1 - side) * half + first
        copies.append(pltpu.make_async_copy(block, whole.at[pl.ds(start, block.shape[0])], sems.at[at]))
    for copy in copies:
        copy.start()
    for copy in copies:
        copy.wait()


def join(blocks, firsts, sides, shape, whole=None):
    anywhere = pl.BlockSpec(memory_space=pl.ANY)
    vmem = pl.BlockSpec(memory_space=pltpu.VMEM)
    given = [] if whole is None else [whole]
    return pl.pallas_call(
        functools.partial(join_kernel, firsts, sides),
        out_shape=jax.ShapeDtypeStruct(shape, F32),
        in_specs=[vmem] * len(blocks) + [anywhere] * len(given),
        out_specs=anywhere,
        input_output_aliases={len(blocks): 0} if given else {},
        scratch_shapes=[pltpu.SemaphoreType.DMA((len(blocks),))],
        compiler_params=pltpu.CompilerParams(vmem_limit_bytes=2 * 1024 * 1024),
    )(*blocks, *given)


def along(block, pairs):
    return lax.ppermute(block, "row", [(2 * a + core, 2 * b + core) for a, b in pairs for core in (0, 1)])


def other_core(block):
    return lax.ppermute(block, "row", [(i, i ^ 1) for i in range(lax.axis_size("row"))])


def other_half(block):
    return lax.ppermute(block, "ch", [(0, 1), (1, 0)])


NEXT = [(0, 1), (1, 0), (2, 3), (3, 2)]
MIDDLE = [(1, 2), (2, 1)]
OUTWARD = [(1, 0), (2, 3)]
INWARD = [(0, 1), (3, 2)]
ACROSS = [(0, 3), (3, 0), (1, 2), (2, 1)]


def on_tiles(pair, pair_mask, w_proj, w_gate, w_out, cotangent):
    rows, cols, width = pair.shape
    half = rows // 2
    chips = cols // (2 * rows)
    chans = 2 * w_out.shape[0]
    row, side = lax.axis_index("row"), lax.axis_index("ch")
    place = jnp.stack([row // 2, row % 2, side]).astype(jnp.int32)

    w_mine = jnp.swapaxes(w_proj, 1, 2)
    other = other_half(flat(w_mine)).reshape(w_mine.shape)
    kept = (half, cols, chans)
    other_out = other_half(w_out)
    normed, scale, keep, mine, *sent = call(
        first_kernel,
        [(half, cols, width)] * 2 + [(rows, cols), w_mine.shape] + [(half, cols, width)] * 2,
        (place, pair, pair_mask, w_mine),
        scratch=[((rows, cols), jnp.int32)],
        distant=3,
        sems=4,
    )
    theirs = [other_core(block) for block in sent]
    right, open_right, slope_right = call(
        functools.partial(right_kernel, rows), [kept] * 3, (place, normed, keep, mine, other)
    )
    right, other_out = lax.optimization_barrier((right, other_out))
    near = along(right, NEXT)
    middle = along(right, MIDDLE)
    _, cotangent_late = lax.optimization_barrier((right, cotangent))
    (third,) = call(
        third_kernel, [(chips + 1, rows, half, width)], (place, cotangent_late, keep), distant=1, sems=chips
    )
    theirs.append(other_core(third))
    quarter = (chips, rows, half, width)
    tile_outs = [(rows, half, width)] * 2 + [(2 * rows * half, chans), kept]
    tile_scratch = [(4, half * GROUP, chans), (2 * rows * half, chans)]
    out_here, out_there, d_x, d_right, rights = ([None] * 4 for _ in range(5))
    rights[0] = right
    left, left_there, open_left, slope_left, gate, d_here, d_there, w_all_out = call(
        functools.partial(prepare_kernel, rows),
        [(rows, cols, chans)] * 2 + [kept] * 2 + [(rows, cols, width), quarter, quarter, (chans, width)],
        (place, pair, keep, cotangent, *theirs, mine, other, w_gate, w_out, other_out),
        scratch=[(CHUNK, cols, width)],
    )

    def tile(step, *blocks):
        got = call(
            functools.partial(tile_kernel, step, len(blocks)),
            tile_outs + ([kept] if len(blocks) == 2 else []),
            (place, *blocks, left, left_there, d_here, d_there, w_all_out),
            scratch=tile_scratch,
        )
        out_here[step], out_there[step], d_x[step], d_right[step] = got[:4]
        rights[step] = got[4] if len(blocks) == 2 else blocks[0]

    near, d_here = lax.optimization_barrier((near, d_here))
    cross = along(near, MIDDLE)
    outer = along(middle, OUTWARD)
    tile(0, right)
    tile(1, near)
    early_other = other_core(jnp.stack(out_there[:2]))
    d_left_here, d_left_there = call(
        functools.partial(left_kernel, 1, False), [(rows, cols, chans)] * 2, (place, rights[0], d_x[0])
    )
    cross, early_other, d_left_here = lax.optimization_barrier((cross, early_other, d_left_here))
    far = along(cross, OUTWARD)
    early_far = other_half(jnp.stack([jnp.stack(out_here[:2]), early_other]))
    tile(2, cross, outer)
    inward = along(d_right[2], INWARD)
    swapped = along(d_right[2], MIDDLE)
    d_left_here, d_left_there = call(
        functools.partial(left_kernel, 2, True),
        [(rows, cols, chans)] * 2,
        (place, *rights[1:3], *d_x[1:3], d_left_here, d_left_there),
    )
    far, d_left_here = lax.optimization_barrier((far, d_left_here))
    out_here[3], out_there[3], d_x[3], d_right[3], rights[3], d_left_sent = call(
        functools.partial(last_tile_kernel, 3),
        tile_outs + [kept, (rows + 2, cols, chans)],
        (place, middle, far, left, left_there, d_here, d_there, w_all_out, d_left_there, out_there[2]),
        scratch=tile_scratch,
    )
    cuts = [half * eighths // 8 for eighths in CUTS]
    spans = list(zip(cuts, cuts[1:]))
    swapped, to_across = lax.optimization_barrier((swapped, d_right[3] + inward))
    to_across, swapped, early_far, d_left_sent = lax.optimization_barrier((to_across, swapped, early_far, d_left_sent))
    to_near = d_right[1] + swapped
    from_across, from_near = [along(to_across[: cuts[1]], ACROSS)], [along(to_near[: cuts[1]], NEXT)]
    received = other_core(d_left_sent)
    _, d_left_here = lax.optimization_barrier((d_left_sent, d_left_here))
    (d_left_kept,) = call(last_kept_kernel, [(rows, cols, chans)], (place, rights[3], d_x[3], d_left_here))
    sizes = [last - first for first, last in spans]
    sizes[0] += 2
    sizes[-1] += 2
    d_left, *packed = call(
        functools.partial(share_kernel, cuts),
        [kept] + [(size, cols, chans) for size in sizes],
        (place, d_left_kept, received, out_here[2], out_here[3]),
    )
    far_parts = [other_half(block) for block in packed]
    for first, last in spans[1:]:
        from_near.append(along(to_near[first:last], NEXT))
        from_across[-1], last_across = lax.optimization_barrier((from_across[-1], to_across[first:last]))
        from_across.append(along(last_across, ACROSS))
    outs = (*out_here, early_other, early_far, received)
    mine_parts, other_parts = [], []
    for at, (first, last) in enumerate(spans):
        (base,) = call(
            functools.partial(base_kernel, rows, first),
            [(last - first, cols, width)],
            (place, *outs, far_parts[0], far_parts[at], gate, cotangent, w_gate, d_left, open_left, slope_left, mine, other),
            scratch=[(last - first, cols, width)],
        )
        if at:
            base, mine_parts[-1] = lax.optimization_barrier((base, mine_parts[-1]))
        (rows_done,) = call(
            functools.partial(pair_kernel, first),
            [(last - first, cols, width)],
            (place, normed, scale, base, d_right[0], from_near[at], from_across[at], open_right, slope_right, mine, other),
        )
        mine_parts.append(rows_done)
        other_parts.append(other_half(rows_done))
    _, gate_late = lax.optimization_barrier((mine_parts[-1], gate))
    (update,) = call(
        functools.partial(update_kernel, rows),
        [(rows, cols, width)],
        (place, *outs, far_parts[0], far_parts[-1], gate_late),
        scratch=[(rows, cols, width)],
    )
    d_pair = join(mine_parts, cuts[:-1], (True,) * len(spans), pair.shape)
    d_pair, update = lax.optimization_barrier((d_pair, update))
    for first, part in zip(cuts, other_parts):
        d_pair, part = lax.optimization_barrier((d_pair, part))
        d_pair = join([part], (first,), (False,), pair.shape, d_pair)
    return (update, d_pair)


def passed_along(block, axis, distance):
    devices = range(lax.axis_size(axis))
    route = [((i - distance) % len(devices), i) for i in devices]
    return lax.ppermute(block, axis, route)


def normalize(values):
    mean = jnp.mean(values, axis=-1, keepdims=True)
    centered = values - mean
    variance = jnp.mean(centered * centered, axis=-1, keepdims=True)
    scale = lax.rsqrt(variance + 1e-05)
    return (centered * scale, scale)


def on_ring(pair, pair_mask, w_proj, w_gate, w_out, cotangent):
    highest = lax.Precision.HIGHEST
    normed, pair_scale = normalize(pair)
    proj = jnp.einsum("rqz,pzc->pcrq", normed, w_proj, precision=highest)
    keep = pair_mask.astype(jnp.float32)
    sig_left = jax.nn.sigmoid(proj[1])
    sig_right = jax.nn.sigmoid(proj[3])
    left = keep * sig_left * proj[0]
    right = keep * sig_right * proj[2]
    chans, rows, cols = left.shape
    count = lax.axis_size("row")
    here = lax.axis_index("row")

    def visit(step, carry):
        block, store, partial_value = carry
        source = (here - step) % count
        store = lax.dynamic_update_slice_in_dim(store, block, source * rows, 1)
        product = jnp.einsum("cik,cjk->cij", left, block, precision=highest)
        partial_value = lax.dynamic_update_slice_in_dim(partial_value, product, source * rows, 2)
        block = passed_along(block, "row", 1)
        return (block, store, partial_value)

    store = jnp.zeros((chans, rows * count, cols), jnp.float32)
    partial_value = jnp.zeros((chans, rows, rows * count), jnp.float32)
    block, store, partial_value = lax.fori_loop(0, count - 1, visit, (right, store, partial_value))
    source = (here + 1) % count
    right_all = lax.dynamic_update_slice_in_dim(store, block, source * rows, 1)
    product = jnp.einsum("cik,cjk->cij", left, block, precision=highest)
    partial_value = lax.dynamic_update_slice_in_dim(partial_value, product, source * rows, 2)
    mixed = lax.psum_scatter(partial_value, "sub", scatter_dimension=2, tiled=True)
    first = jnp.sum(mixed, axis=0)
    second = jnp.sum(mixed * mixed, axis=0)
    projected = jnp.einsum("crq,cd->rqd", mixed, w_out, precision=highest)
    col_total = jnp.sum(w_out, axis=0)
    projected, first, second, col_total = lax.psum((projected, first, second, col_total), "ch")
    center = first / C
    spread = lax.rsqrt(second / C - center * center + 1e-05)
    outgoing = (projected - center[..., None] * col_total) * spread[..., None]
    gate = jax.nn.sigmoid(jnp.einsum("rqz,zd->rqd", normed, w_gate, precision=highest))
    update = gate * outgoing
    d_outgoing = cotangent * gate
    d_gate_pre = cotangent * outgoing * gate * (1.0 - gate)
    d_mixed_norm = jnp.einsum("rqd,cd->crq", d_outgoing, w_out, precision=highest)
    mean_one = jnp.sum(d_outgoing * col_total, axis=-1) / C
    mean_two = jnp.sum(d_outgoing * outgoing, axis=-1) / C
    mixed_norm = (mixed - center) * spread
    d_mixed = (d_mixed_norm - mean_one - mixed_norm * mean_two) * spread
    d_mixed_full = lax.all_gather(d_mixed, "sub", axis=2, tiled=True)
    d_left = jnp.einsum("cij,cjk->cik", d_mixed_full, right_all, precision=highest)
    d_right = jnp.transpose(
        lax.psum_scatter(
            jnp.einsum("cij,cik->jck", d_mixed_full, left, precision=highest),
            "row",
            scatter_dimension=0,
            tiled=True,
        ),
        (1, 0, 2),
    )
    d_proj = jnp.stack(
        [
            d_left * keep * sig_left,
            d_left * keep * proj[0] * sig_left * (1.0 - sig_left),
            d_right * keep * sig_right,
            d_right * keep * proj[2] * sig_right * (1.0 - sig_right),
        ]
    )
    d_normed_part = jnp.einsum("pcrq,pzc->rqz", d_proj, w_proj, precision=highest)
    d_normed = lax.psum(d_normed_part, "ch")
    d_normed = d_normed + jnp.einsum("rqd,zd->rqz", d_gate_pre, w_gate, precision=highest)
    mean_grad = jnp.mean(d_normed, axis=-1, keepdims=True)
    mean_cross = jnp.mean(d_normed * normed, axis=-1, keepdims=True)
    d_pair = (d_normed - mean_grad - normed * mean_cross) * pair_scale
    return (update, d_pair)


def solution(mesh):
    sizes = mesh.shape
    tiled = sizes["row"] == 8 and sizes["ch"] == 2 and sizes["sub"] == 1
    return jax.shard_map(
        on_tiles if tiled else on_ring,
        mesh=mesh,
        in_specs=(
            P(("grp", "row"), "sub", None),
            P(("grp", "row"), "sub"),
            P(None, None, "ch"),
            P(),
            P("ch", None),
            P(("grp", "row"), "sub", None),
        ),
        out_specs=(P(("grp", "row"), "sub", None), P(("grp", "row"), "sub", None)),
        check_vma=False,
    )
```
